32 devices in a mesh: cfg: 2 (over core), tok: 4 (over z), mlp: 4 (over y, x).
Axes of the slice: x: 2, y: 2, z: 4, core: 2. Of those that a mesh axis runs over, the one named last changes fastest.
Arguments:
- hidden: bfloat16 [2, 1536, 4, 3072], P('cfg', ('tok', 'mlp')), may hold values from -6 to 6
- latents: float32 [1536, 4, 64], P(('tok', 'mlp'), None, 'cfg'), may hold values from -6 to 6
- vec: float32 [2, 4, 3072], P('cfg'), may hold values from -9 to 9
- slot_token: int32 [4, 1536], replicated, may hold values from 0 to 1535, each once within a row
- text_len: int32 [2, 4], P('cfg'), may hold values from 64 to 512, as said below
- step_index: int32 [1], replicated, may hold values from 0 to 27
- guidance: float32 [1], replicated, may hold values from 2 to 5
- w_mod: bfloat16 [3072, 15360], P(None, ('tok', 'mlp')), may hold values from -0.109375 to 0.109375
- w_qkv: bfloat16 [1, 3072, 3, 2048], P(None, 'cfg', None, 'mlp'), may hold values from -0.109375 to 0.109375
- w_mlp_in: bfloat16 [1, 3072, 12288], P(None, 'cfg', 'mlp'), may hold values from -0.109375 to 0.109375
- qk_gain: float32 [1, 2, 128], replicated, may hold values from 1.5 to 2.5
- w_attn_out: bfloat16 [1, 2048, 3072], P(None, 'mlp', 'cfg'), may hold values from -0.125 to 0.125
- w_mlp_out: bfloat16 [1, 12288, 3072], P(None, 'mlp', 'cfg'), may hold values from -0.0546875 to 0.0546875
- w_final: bfloat16 [3072, 64], replicated, may hold values from -0.109375 to 0.109375
Outputs:
- velocity: float32 [1536, 4, 64], P(('tok', 'mlp'), None, 'cfg')
- latents_next: float32 [1536, 4, 64], P(('tok', 'mlp'), None, 'cfg')
- stream_out: bfloat16 [2, 1536, 4, 3072], P('cfg', ('tok', 'mlp'))
The draws below stay inside these ranges and needn't reach their ends.
Inputs may be any that keep to these rules, and one draw needn't show every extreme that they name: `text_len`: real text tokens of each request; its other text slots are padding; exactly one request has all 512. `slot_token`: row p lists the token held by each slot of request p: text tokens are 0 to 511, image tokens follow row by row on the 32 x 32 grid.
All inputs are finite; a program needn't handle non-finite values.
Results may differ from the reference program's by a relative error of at most 0.018.
Values may be sent and summed in bfloat16 or wider, within the bound.
No kernel may reach another device: no remote copies, remote signals or barrier semaphores. Data moves between devices by JAX's collectives and lax.ppermute only.
A program may use at most 192 MiB of HBM per device.

```python
import math
import jax
import jax.numpy as jnp
from jax import lax

D = 3072
FF = 12288
HEAD_DIM = 128
CH = 64
HEADS = 16
LAYERS = 1
SIDE = 32
TXT = 512
STEPS = 28
PROMPTS = 4
S = 1536
MODS = 5
N_MLP = 4


def draw_text_len(key, part):
    lengths = jax.random.randint(key, (2 * PROMPTS,), TXT // 8, TXT)
    chosen = jax.random.randint(jax.random.fold_in(key, 7), (), 0, 2 * PROMPTS)
    lengths = jnp.where(jnp.arange(2 * PROMPTS) == chosen, TXT, lengths)
    return lengths.reshape(2, PROMPTS).astype(jnp.int32)


def steps_of(rng, dims, cuts, low, top_value):
    level, own = 1.0, jax.random.fold_in(rng, 6)
    for dim, blocks in cuts:
        steps = jnp.exp(jax.random.uniform(jax.random.fold_in(own, dim), (blocks,), jnp.float32, low / len(cuts), top_value / len(cuts)))
        level = level * jnp.repeat(steps, dims[dim] // blocks).reshape([-1 if axis == dim else 1 for axis in range(len(dims))])
    return level


def noise(rng, shape, scale, limit, cuts=(), dtype=jnp.bfloat16):
    loudness = steps_of(rng, shape, cuts, -0.22, 0.18) if cuts else 1.0
    entries = jax.random.normal(rng, shape, jnp.float32) * scale * loudness
    return jnp.minimum(jnp.maximum(entries, -limit), limit).astype(dtype)


def setup_inputs(seed: int = 0) -> dict:
    streams_of = jax.random.split(jax.random.key(seed), 15)
    hidden = noise(streams_of[0], (2, S, PROMPTS, D), 1.0, 6.0, ((0, 2), (1, 16)))
    latents = noise(streams_of[1], (S, PROMPTS, CH), 1.0, 6.0, ((0, 16), (2, 2)), jnp.float32)
    vec = noise(streams_of[2], (2, PROMPTS, D), 1.5, 9.0, ((0, 2),), jnp.float32)
    slot_token = jax.vmap(lambda own: jax.random.permutation(own, S))(jax.random.split(streams_of[3], PROMPTS)).reshape((PROMPTS, S)).astype(jnp.int32)
    text_len = draw_text_len(jax.random.fold_in(streams_of[14], 71), 0)
    step_index = jax.random.randint(streams_of[5], (1,), 0, STEPS).astype(jnp.int32)
    guidance = jnp.clip(jax.random.uniform(streams_of[6], (1,), jnp.float32, 2.0, 5.0), 2.0, 5.0)
    w_mod = noise(streams_of[7], (D, MODS * D), D ** -0.5, 0.109375, ((1, 16),))
    w_qkv = noise(streams_of[8], (LAYERS, D, 3, HEADS * HEAD_DIM), D ** -0.5, 0.109375, ((1, 2), (3, 4)))
    w_mlp_in = noise(streams_of[9], (LAYERS, D, FF), D ** -0.5, 0.109375, ((1, 2), (2, 4)))
    qk_gain = jnp.clip(jax.random.uniform(streams_of[10], (LAYERS, 2, HEAD_DIM), jnp.float32, 1.5, 2.5), 1.5, 2.5)
    w_attn_out = noise(streams_of[11], (LAYERS, HEADS * HEAD_DIM, D), (HEADS * HEAD_DIM) ** -0.5, 0.125, ((1, 4), (2, 2)))
    w_mlp_out = noise(streams_of[12], (LAYERS, FF, D), FF ** -0.5, 0.0546875, ((1, 4), (2, 2)))
    w_final = noise(streams_of[13], (D, CH), D ** -0.5, 0.109375)
    return dict(hidden=hidden, latents=latents, vec=vec, slot_token=slot_token, text_len=text_len, step_index=step_index, guidance=guidance, w_mod=w_mod, w_qkv=w_qkv, w_mlp_in=w_mlp_in, qk_gain=qk_gain, w_attn_out=w_attn_out, w_mlp_out=w_mlp_out, w_final=w_final)


EPSILON = 1e-06
ROPE_BASE = 10000.0
TIME_SHIFT = 3.0

def layer_norm(values):
    average = lax.optimization_barrier(jnp.mean(values, axis=-1, keepdims=True))
    centred = values - average
    spread = lax.optimization_barrier(jnp.mean(centred * centred, axis=-1, keepdims=True))
    return centred * lax.rsqrt(spread + EPSILON)

def rms_norm(values, gains):
    return values * lax.rsqrt(lax.optimization_barrier(jnp.mean(values * values, axis=-1, keepdims=True)) + EPSILON) * gains

def rope_table(tokens, head_size, text_count, side_count):
    pair_count = head_size // 2
    first_pairs = head_size // 16
    axis_pairs = (head_size - head_size // 8) // 4
    pair_index = jnp.arange(pair_count).astype(jnp.float32)
    in_rows = (pair_index >= first_pairs) & (pair_index < first_pairs + axis_pairs)
    in_cols = pair_index >= first_pairs + axis_pairs
    log_base = math.log(ROPE_BASE)
    freq_rows = jnp.where(in_rows, jnp.exp(-log_base * (pair_index - first_pairs) / axis_pairs), 0.0)
    freq_cols = jnp.where(in_cols, jnp.exp(-log_base * (pair_index - first_pairs - axis_pairs) / axis_pairs), 0.0)
    is_image = tokens >= text_count
    image_pos = jnp.where(is_image, tokens - text_count, 0).astype(jnp.int32)
    row_pos = (image_pos // side_count).astype(jnp.float32)
    col_pos = (image_pos % side_count).astype(jnp.float32)
    angles = row_pos[..., None] * freq_rows + col_pos[..., None] * freq_cols
    return (jnp.cos(angles), jnp.sin(angles))

def apply_rope(values, cosine, sine_table):
    even_part = values[..., 0::2]
    odd_part = values[..., 1::2]
    return jnp.concatenate([even_part * cosine - odd_part * sine_table, even_part * sine_table + odd_part * cosine], axis=-1)

def sigma_at(position, steps_total):
    remain = 1.0 - position / steps_total
    return TIME_SHIFT * remain / (1.0 + (TIME_SHIFT - 1.0) * remain)

def reference(hidden, latents, vec, slot_token, text_len, step_index, guidance, w_mod, w_qkv, w_mlp_in, qk_gain, w_attn_out, w_mlp_out, w_final):
    head_total = HEADS * HEAD_DIM
    head_cols = head_total // N_MLP
    unit_cols = FF // N_MLP
    slot_tokens = slot_token.T
    cosine, sine_table = rope_table(slot_tokens, HEAD_DIM, TXT, SIDE)
    is_image = slot_tokens >= TXT
    halves = []
    streams = []
    for half_idx in range(2):
        stream = hidden[half_idx]
        modulation = jnp.dot(jax.nn.silu(vec[half_idx]).astype(jnp.bfloat16), w_mod, preferred_element_type=jnp.float32)
        key_valid = (slot_token >= TXT) | (slot_token < text_len[half_idx][:, None])
        for layer_idx in range(LAYERS):
            offset_cols = 3 * layer_idx * D
            shift_mod = modulation[:, offset_cols:offset_cols + D]
            scale_mod = modulation[:, offset_cols + D:offset_cols + 2 * D]
            gate_mod = modulation[:, offset_cols + 2 * D:offset_cols + 3 * D]
            normed = (layer_norm(stream.astype(jnp.float32)) * (1.0 + scale_mod[None]) + shift_mod[None]).astype(jnp.bfloat16)
            flattened = normed.reshape(S * PROMPTS, D)
            projected = jnp.dot(flattened, w_qkv[layer_idx].reshape(D, 3 * head_total), preferred_element_type=jnp.float32)
            projected = projected.reshape(S, PROMPTS, 3, HEADS, HEAD_DIM)
            unit_pre = jnp.dot(flattened, w_mlp_in[layer_idx], preferred_element_type=jnp.float32)
            queries = apply_rope(rms_norm(projected[:, :, 0], qk_gain[layer_idx, 0]), cosine[:, :, None], sine_table[:, :, None]).astype(jnp.bfloat16)
            keys_rot = apply_rope(rms_norm(projected[:, :, 1], qk_gain[layer_idx, 1]), cosine[:, :, None], sine_table[:, :, None]).astype(jnp.bfloat16)
            values = projected[:, :, 2].astype(jnp.bfloat16)
            queries = lax.optimization_barrier(queries).astype(jnp.float32)
            keys_rot = lax.optimization_barrier(keys_rot).astype(jnp.float32)
            values = lax.optimization_barrier(values).astype(jnp.float32)
            activation = jax.nn.gelu(unit_pre, approximate=True).astype(jnp.bfloat16)
            outputs = []
            for prompt_idx in range(PROMPTS):
                scores = jnp.einsum('she,the->hst', queries[:, prompt_idx], keys_rot[:, prompt_idx]) / math.sqrt(HEAD_DIM)
                softened = jnp.exp(scores) * key_valid[prompt_idx][None, None, :].astype(jnp.float32)
                rounded = lax.optimization_barrier(softened.astype(jnp.bfloat16)).astype(jnp.float32)
                numerator = jnp.einsum('hst,the->she', rounded, values[:, prompt_idx])
                denominator = lax.optimization_barrier(jnp.sum(softened, axis=-1))
                outputs.append((numerator / denominator.T[:, :, None]).astype(jnp.bfloat16))
            attended = jnp.stack(outputs, axis=1).reshape(S * PROMPTS, head_total)
            branch_out = jnp.zeros((S * PROMPTS, D), jnp.float32)
            for shard_idx in range(N_MLP):
                head_lo = shard_idx * head_cols
                unit_lo = shard_idx * unit_cols
                shard_term = jnp.dot(attended[:, head_lo:head_lo + head_cols], w_attn_out[layer_idx, head_lo:head_lo + head_cols], preferred_element_type=jnp.float32)
                shard_term = shard_term + jnp.dot(activation[:, unit_lo:unit_lo + unit_cols], w_mlp_out[layer_idx, unit_lo:unit_lo + unit_cols], preferred_element_type=jnp.float32)
                branch_out = branch_out + lax.optimization_barrier(shard_term.astype(jnp.bfloat16)).astype(jnp.float32)
            stream = (stream.astype(jnp.float32) + gate_mod[None] * branch_out.reshape(S, PROMPTS, D)).astype(jnp.bfloat16)
        streams.append(stream)
        final_lo = 3 * LAYERS * D
        final_shift = modulation[:, final_lo:final_lo + D]
        final_scale = modulation[:, final_lo + D:final_lo + 2 * D]
        final_normed = (layer_norm(stream.astype(jnp.float32)) * (1.0 + final_scale[None]) + final_shift[None]).astype(jnp.bfloat16)
        half_velocity = jnp.dot(final_normed.reshape(S * PROMPTS, D), w_final, preferred_element_type=jnp.float32).reshape(S, PROMPTS, CH)
        halves.append(jnp.where(is_image[:, :, None], half_velocity, 0.0))
    velocity = halves[1] + guidance[0] * (halves[0] - halves[1])
    current = step_index[0].astype(jnp.float32)
    step_size = sigma_at(current + 1.0, STEPS) - sigma_at(current, STEPS)
    return (velocity, latents + step_size * velocity, jnp.stack(streams, axis=0))
```

```python
import math

import jax
import jax.numpy as jnp
from jax import lax
from jax.experimental import pallas as pl
from jax.experimental.pallas import tpu as pltpu
from jax.sharding import PartitionSpec as P

LAYERS = 1
SIDE = 32
TXT = 512
STEPS = 28
PROMPTS = 4


EPSILON = 1e-06
ROPE_BASE = 10000.0
TIME_SHIFT = 3.0


def xor_swap(value, axis, apart):
    return lax.ppermute(value, axis, [(i, i ^ apart) for i in range(lax.axis_size(axis))])


def layer_norm(values):
    average = jnp.mean(values, axis=-1, keepdims=True)
    centred = values - average
    spread = jnp.mean(centred * centred, axis=-1, keepdims=True)
    return centred * lax.rsqrt(spread + EPSILON)


def rms_norm(values, gains):
    return values * lax.rsqrt(jnp.mean(values * values, axis=-1, keepdims=True) + EPSILON) * gains


def rope_table(tokens, head_size, text_count, side_count):
    pair_count = head_size // 2
    first_pairs = head_size // 16
    axis_pairs = (head_size - head_size // 8) // 4
    pair_index = jnp.arange(pair_count).astype(jnp.float32)
    in_rows = (pair_index >= first_pairs) & (pair_index < first_pairs + axis_pairs)
    in_cols = pair_index >= first_pairs + axis_pairs
    log_base = math.log(ROPE_BASE)
    freq_rows = jnp.where(
        in_rows, jnp.exp(-log_base * (pair_index - first_pairs) / axis_pairs), 0.0
    )
    freq_cols = jnp.where(
        in_cols, jnp.exp(-log_base * (pair_index - first_pairs - axis_pairs) / axis_pairs), 0.0
    )
    is_image = tokens >= text_count
    image_pos = jnp.where(is_image, tokens - text_count, 0)
    row_pos = (image_pos // side_count).astype(jnp.float32)
    col_pos = (image_pos % side_count).astype(jnp.float32)
    angles = row_pos[..., None] * freq_rows + col_pos[..., None] * freq_cols
    return (jnp.cos(angles), jnp.sin(angles))


def apply_rope(values, cosine, sine_table):
    even_part = values[..., 0::2]
    odd_part = values[..., 1::2]
    return jnp.concatenate(
        [even_part * cosine - odd_part * sine_table, even_part * sine_table + odd_part * cosine],
        axis=-1,
    )


def sigma_at(position, steps_total):
    remain = 1.0 - position / steps_total
    return TIME_SHIFT * remain / (1.0 + (TIME_SHIFT - 1.0) * remain)


def on_device(
    hidden,
    latents,
    vec,
    slot_token,
    text_len,
    step_index,
    guidance,
    w_mod,
    w_qkv,
    w_mlp_in,
    qk_gain,
    w_attn_out,
    w_mlp_out,
    w_final,
):
    rows_dev = hidden.shape[1]
    prompts = hidden.shape[2]
    model_width = hidden.shape[3]
    head_size = qk_gain.shape[-1]
    mlp_count = lax.axis_size("mlp")
    tile_rows = rows_dev * mlp_count
    tok_index = lax.axis_index("tok")
    mlp_index = lax.axis_index("mlp")
    half_index = lax.axis_index("cfg")
    stream = hidden[0]
    silu_vec = jax.nn.silu(vec[0]).astype(jnp.bfloat16)
    mod_part = jnp.dot(silu_vec, w_mod, preferred_element_type=jnp.float32)
    modulation = lax.all_gather(mod_part, ("tok", "mlp"), axis=1, tiled=True)
    key_valid = ((slot_token >= TXT) | (slot_token < text_len[0][:, None])).astype(jnp.float32)
    tile_tokens = lax.dynamic_slice_in_dim(slot_token, tok_index * tile_rows, tile_rows, 1).T
    cosine, sine_table = rope_table(tile_tokens, head_size, TXT, SIDE)
    shift_mod = modulation[:, 0:model_width]
    scale_mod = modulation[:, model_width : 2 * model_width]
    gate_mod = modulation[:, 2 * model_width : 3 * model_width]
    normed = (
        layer_norm(stream.astype(jnp.float32)) * (1.0 + scale_mod[None]) + shift_mod[None]
    ).astype(jnp.bfloat16)
    tile_input = lax.all_gather(normed, "mlp", axis=0, tiled=True)
    qkv_weight = w_qkv[0]
    unit_weight = w_mlp_in[0]
    qkv_cols = qkv_weight.shape[1] * qkv_weight.shape[2]
    pieces = (
        lax.all_gather(qkv_weight, "cfg", axis=0, tiled=True),
        lax.all_gather(unit_weight, "cfg", axis=0, tiled=True),
    )
    number = pieces[0].shape[0]
    qkv_piece = pieces[0].reshape(number, qkv_cols)
    qkv_pre = jnp.einsum("tpd,dk->tpk", tile_input, qkv_piece, preferred_element_type=jnp.float32)
    unit_pre = jnp.einsum("tpd,dk->tpk", tile_input, pieces[1], preferred_element_type=jnp.float32)
    heads_dev = qkv_weight.shape[2] // head_size
    projected = qkv_pre.reshape(tile_rows, prompts, 3, heads_dev, head_size)
    queries = apply_rope(
        rms_norm(projected[:, :, 0], qk_gain[0, 0]), cosine[:, :, None], sine_table[:, :, None]
    ).astype(jnp.bfloat16)
    keys_rot = apply_rope(
        rms_norm(projected[:, :, 1], qk_gain[0, 1]), cosine[:, :, None], sine_table[:, :, None]
    ).astype(jnp.bfloat16)
    values = projected[:, :, 2].astype(jnp.bfloat16)
    activation = jax.nn.gelu(unit_pre, approximate=True).astype(jnp.bfloat16)
    keys_piece = lax.all_gather(keys_rot, "tok", axis=0, tiled=True)
    values_piece = lax.all_gather(values, "tok", axis=0, tiled=True)
    scores = jnp.einsum(
        "sphe,tphe->phst", queries, keys_piece, preferred_element_type=jnp.float32
    ) / math.sqrt(head_size)
    softened = jnp.exp(scores) * key_valid[:, None, None, :]
    numerator = jnp.einsum(
        "phst,tphe->sphe",
        softened.astype(jnp.bfloat16),
        values_piece,
        preferred_element_type=jnp.float32,
    )
    numerator, denominator = (numerator, jnp.sum(softened, axis=-1))
    attended = (numerator / jnp.transpose(denominator, (2, 0, 1))[..., None]).astype(jnp.bfloat16)
    attended = attended.reshape(tile_rows, prompts, heads_dev * head_size)
    out_attn = lax.all_gather(w_attn_out[0], "cfg", axis=1, tiled=True)
    out_units = lax.all_gather(w_mlp_out[0], "cfg", axis=1, tiled=True)
    branch_out = lax.psum_scatter(
        (
            jnp.einsum("tpk,kd->tpd", attended, out_attn, preferred_element_type=jnp.float32)
            + jnp.einsum("tpk,kd->tpd", activation, out_units, preferred_element_type=jnp.float32)
        ).astype(jnp.bfloat16),
        "mlp",
        scatter_dimension=0,
        tiled=True,
    ).astype(jnp.float32)
    stream = (stream.astype(jnp.float32) + gate_mod[None] * branch_out).astype(jnp.bfloat16)
    final_lo = 3 * LAYERS * model_width
    final_shift = modulation[:, final_lo : final_lo + model_width]
    final_scale = modulation[:, final_lo + model_width : final_lo + 2 * model_width]
    final_normed = (
        layer_norm(stream.astype(jnp.float32)) * (1.0 + final_scale[None]) + final_shift[None]
    ).astype(jnp.bfloat16)
    own_first = (tok_index * mlp_count + mlp_index) * rows_dev
    own_tokens = lax.dynamic_slice_in_dim(slot_token, own_first, rows_dev, 1).T
    half_velocity = jnp.einsum(
        "rpd,dc->rpc", final_normed, w_final, preferred_element_type=jnp.float32
    )
    half_velocity = jnp.where((own_tokens >= TXT)[:, :, None], half_velocity, 0.0)
    return guided(half_velocity, half_index, latents, step_index, guidance) + (stream[None],)


VMEM_BYTES = 56 * 1024 * 1024
TILE = 512
SLOTS = 3
ANY = pl.BlockSpec(memory_space=pl.ANY)
VMEM = pl.BlockSpec(memory_space=pltpu.VMEM)
SMEM = pl.BlockSpec(memory_space=pltpu.SMEM)


def kernel_params():
    return pltpu.CompilerParams(vmem_limit_bytes=VMEM_BYTES)


def flip_by_bit(values, axis, bit):
    return jnp.where(bit, jnp.flip(values, axis), values)


def from_xor_order(values, axis, index, bits):
    shape = values.shape
    split = shape[:axis] + (2,) * bits + shape[axis + 1 :]
    values = values.reshape(split)
    for place in range(bits):
        bit = (index >> (bits - 1 - place)) & 1
        values = flip_by_bit(values, axis + place, bit == 1)
    return values.reshape(shape)


to_xor_order = from_xor_order


def pick_kernel(place_ref, *refs):
    count = len(refs) // 2
    for j in range(count):
        refs[count + j][...] = refs[j][0]


def pick(place, states):
    count, rows, width = states.shape
    take = lambda j: lambda i, s: (s[0] ^ j, i, 0)
    return pl.pallas_call(
        pick_kernel,
        out_shape=(jax.ShapeDtypeStruct((rows, width), states.dtype),) * count,
        grid_spec=pltpu.PrefetchScalarGridSpec(
            num_scalar_prefetch=1,
            grid=(2,),
            in_specs=[pl.BlockSpec((1, rows // 2, width), take(j)) for j in range(count)],
            out_specs=[pl.BlockSpec((rows // 2, width), lambda i, s: (i, 0))] * count,
        ),
        compiler_params=kernel_params(),
        cost_estimate=pl.CostEstimate(flops=0, bytes_accessed=4 * states.size, transcendentals=0),
        name="pick",
    )(place, *([states] * count))


def sort_pairs_kernel(w_ref, sorter, out):
    part = pl.program_id(0)
    wide = sorter.shape[0]

    @pl.when(part < 2)
    def _():
        for lo in range(0, out.shape[1], wide):
            out[:, lo : lo + wide] = jnp.dot(
                w_ref[0, :, lo : lo + wide], sorter[...], preferred_element_type=jnp.float32
            ).astype(jnp.bfloat16)

    @pl.when(part == 2)
    def _():
        out[...] = w_ref[0]


def sort_pairs(weight, sorter):
    parts, depth, cols = weight.shape
    rows = depth // 2
    return pl.pallas_call(
        sort_pairs_kernel,
        out_shape=jax.ShapeDtypeStruct((depth, parts * cols), weight.dtype),
        grid=(parts, 2),
        in_specs=[
            pl.BlockSpec((1, rows, cols), lambda p, i: (p, i, 0)),
            pl.BlockSpec(sorter.shape, lambda p, i: (0, 0)),
        ],
        out_specs=pl.BlockSpec((rows, cols), lambda p, i: (i, p)),
        compiler_params=kernel_params(),
        cost_estimate=pl.CostEstimate(
            flops=4 * depth * cols * sorter.shape[0], bytes_accessed=4 * weight.size, transcendentals=0
        ),
        name="sort_pairs",
    )(weight, sorter)


def project_kernel(
    half_ref,
    shift,
    scale,
    cos_ref,
    sin_ref,
    gain,
    x0,
    x1,
    x2,
    x3,
    wq_own,
    wq_other,
    wu_own,
    wu_other,
    q_out,
    k_out,
    v_out,
    act_out,
    landed,
    normed,
    held,
    ready,
    x_sem,
    w_sem,
    out_sem,
):
    half = half_ref[0]
    depth = wq_own.shape[0]
    head = gain.shape[1]
    pieces = (x0, x1, x2, x3)
    rows = x0.shape[0]
    units = wu_own.shape[1] // TILE

    def weights(own, other, column, slot):
        return [
            pltpu.make_async_copy(
                ref.at[:, pl.ds(column, TILE)], held.at[slot, side], w_sem.at[slot, side]
            )
            for side, ref in enumerate((own, other))
        ]

    def result(out, column, slot):
        return pltpu.make_async_copy(
            ready.at[slot], out.at[:, pl.ds(column, TILE)], out_sem.at[slot]
        )

    loads = [pltpu.make_async_copy(ref, landed.at[i], x_sem.at[i]) for i, ref in enumerate(pieces)]
    loads[0].start()
    for copy in weights(wq_own, wq_other, 0, 0):
        copy.start()
    for load in loads[1:]:
        load.start()
    for part in (1, 2):
        for copy in weights(wq_own, wq_other, part * TILE, part):
            copy.start()

    for index, load in enumerate(loads):
        load.wait()
        block = layer_norm(landed[index].astype(jnp.float32))
        block = (block * scale[...] + shift[...]).astype(jnp.bfloat16)
        normed[0, index * rows : (index + 1) * rows, :] = block[:, :depth]
        normed[1, index * rows : (index + 1) * rows, :] = block[:, depth:]

    def product(slot):
        return jnp.dot(
            normed[half], held[slot, 0], preferred_element_type=jnp.float32
        ) + jnp.dot(normed[1 - half], held[slot, 1], preferred_element_type=jnp.float32)

    for part, out in enumerate((q_out, k_out, v_out)):
        for copy in weights(wq_own, wq_other, part * TILE, part):
            copy.wait()
        values = product(part)
        if part == 2:
            result(out, 0, 0).wait()
            ready[0] = values.astype(jnp.bfloat16)
        else:
            for lo in range(0, TILE, head):
                turned = rms_norm(values[:, lo : lo + head], gain[part : part + 1, :])
                turned = turned * cos_ref[...] + pltpu.roll(turned, head // 2, 1) * sin_ref[...]
                ready[part, :, lo : lo + head] = turned.astype(jnp.bfloat16)
        result(out, 0, part % 2).start()
        for copy in weights(wu_own, wu_other, part * TILE, part):
            copy.start()

    @pl.loop(0, units)
    def _(index):
        slot = lax.rem(index, SLOTS)
        to = lax.rem(index + 1, 2)
        column = pl.multiple_of(index * TILE, TILE)
        for copy in weights(wu_own, wu_other, column, slot):
            copy.wait()
        values = jax.nn.gelu(product(slot), approximate=True).astype(jnp.bfloat16)
        result(act_out, column, to).wait()
        ready[to] = values
        result(act_out, column, to).start()

        @pl.when(index + SLOTS < units)
        def _():
            later = pl.multiple_of((index + SLOTS) * TILE, TILE)
            for copy in weights(wu_own, wu_other, later, slot):
                copy.start()

    for slot in range(2):
        result(act_out, 0, slot).wait()


def project(half, pieces, shift, scale, cos_rows, sin_rows, gain, wq_own, wq_other, wu_own, wu_other):
    rows = sum(piece.shape[0] for piece in pieces)
    width = pieces[0].shape[1]
    depth = wq_own.shape[0]
    units = wu_own.shape[1]
    head_out = jax.ShapeDtypeStruct((rows, TILE), jnp.bfloat16)
    return pl.pallas_call(
        project_kernel,
        out_shape=(head_out, head_out, head_out, jax.ShapeDtypeStruct((rows, units), jnp.bfloat16)),
        in_specs=[SMEM] + [VMEM] * 5 + [ANY] * 8,
        out_specs=[ANY] * 4,
        scratch_shapes=[
            pltpu.VMEM((len(pieces), rows // len(pieces), width), jnp.bfloat16),
            pltpu.VMEM((2, rows, depth), jnp.bfloat16),
            pltpu.VMEM((SLOTS, 2, depth, TILE), jnp.bfloat16),
            pltpu.VMEM((2, rows, TILE), jnp.bfloat16),
            pltpu.SemaphoreType.DMA((len(pieces),)),
            pltpu.SemaphoreType.DMA((SLOTS, 2)),
            pltpu.SemaphoreType.DMA((2,)),
        ],
        compiler_params=kernel_params(),
        cost_estimate=pl.CostEstimate(
            flops=2 * rows * width * (3 * TILE + units),
            bytes_accessed=2 * width * (3 * TILE + units) + 2 * rows * (width + 3 * TILE + units),
            transcendentals=rows * units,
        ),
        name="project",
    )(half, shift, scale, cos_rows, sin_rows, gain, *pieces, wq_own, wq_other, wu_own, wu_other)


def combine_kernel(
    half_ref,
    bias,
    q,
    k0,
    k1,
    k2,
    k3,
    v0,
    v1,
    v2,
    v3,
    act,
    wa_own,
    wa_other,
    wm_own,
    wm_other,
    p0,
    p1,
    p2,
    p3,
    attended,
    units,
    held_a,
    held_m,
    ready,
    act_sem,
    w_sem,
    out_sem,
):
    half = half_ref[0]
    keys, values, outs = (k0, k1, k2, k3), (v0, v1, v2, v3), (p0, p1, p2, p3)
    rows = q.shape[0]
    size = k0.shape[0]
    piece = p0.shape[0]
    head = 128
    steps = wa_own.shape[1] // TILE

    def weights(wa, wm, column, slot):
        return [
            pltpu.make_async_copy(wa.at[:, pl.ds(column, TILE)], held_a.at[slot], w_sem.at[slot, 0]),
            pltpu.make_async_copy(wm.at[:, pl.ds(column, TILE)], held_m.at[slot], w_sem.at[slot, 1]),
        ]

    def results(column, slot):
        return [
            pltpu.make_async_copy(
                ready.at[slot, pl.ds(i * piece, piece)],
                out.at[:, pl.ds(column, TILE)],
                out_sem.at[slot, i],
            )
            for i, out in enumerate(outs)
        ]

    load = pltpu.make_async_copy(act, units, act_sem)
    load.start()
    for slot in range(SLOTS):
        for copy in weights(wa_own, wm_own, slot * TILE, slot):
            copy.start()

    @pl.loop(0, q.shape[1] // head)
    def _(index):
        lanes = pl.ds(pl.multiple_of(index * head, head), head)
        total = jnp.zeros((rows, 1), jnp.float32)
        numerator = jnp.zeros((rows, head), jnp.float32)
        for part in range(len(keys)):
            scores = lax.dot_general(
                q[:, lanes],
                keys[part][:, lanes],
                (((1,), (1,)), ((), ())),
                preferred_element_type=jnp.float32,
            )
            soft = jnp.exp(
                scores * (1.0 / math.sqrt(head)) + bias[:, part * size : (part + 1) * size]
            )
            total += jnp.sum(soft, axis=-1, keepdims=True)
            numerator += jnp.dot(
                soft.astype(jnp.bfloat16), values[part][:, lanes], preferred_element_type=jnp.float32
            )
        attended[:, lanes] = (numerator / total).astype(jnp.bfloat16)

    load.wait()

    def write(index, slot, column, first, wa, wm):
        for copy in weights(wa, wm, 0, slot):
            copy.wait()
        partial = jnp.dot(attended[...], held_a[slot], preferred_element_type=jnp.float32)
        partial += jnp.dot(units[...], held_m[slot], preferred_element_type=jnp.float32)
        to = lax.rem(index, 2)

        @pl.when(index >= 2)
        def _():
            for copy in results(0, to):
                copy.wait()

        ready[to] = partial.astype(jnp.bfloat16)
        for copy in results(column, to):
            copy.start()

    @pl.loop(0, 2 * steps)
    def _(index):
        slot = lax.rem(index, SLOTS)
        place = lax.rem(index + steps * half, 2 * steps)
        write(index, slot, pl.multiple_of(place * TILE, TILE), 0, wa_own, wm_own)

        @pl.when(index + SLOTS < 2 * steps)
        def _():
            later = pl.multiple_of((index + SLOTS - steps) * TILE, TILE)
            for copy in weights(wa_other, wm_other, later, slot):
                copy.start()

    for slot in range(2):
        for copy in results(0, slot):
            copy.wait()


def combine(half, bias, q, keys, values, act, wa_own, wa_other, wm_own, wm_other):
    rows, heads = q.shape
    units = act.shape[1]
    slots = bias.shape[1]
    half_cols = wa_own.shape[1]
    assert half_cols == SLOTS * TILE
    pieces = len(keys)
    part = jax.ShapeDtypeStruct((rows // pieces, 2 * half_cols), jnp.bfloat16)
    return pl.pallas_call(
        combine_kernel,
        out_shape=(part,) * pieces,
        in_specs=[SMEM] + [VMEM] * (2 + 2 * pieces) + [ANY] * 5,
        out_specs=[ANY] * pieces,
        scratch_shapes=[
            pltpu.VMEM((rows, heads), jnp.bfloat16),
            pltpu.VMEM((rows, units), jnp.bfloat16),
            pltpu.VMEM((SLOTS, heads, TILE), jnp.bfloat16),
            pltpu.VMEM((SLOTS, units, TILE), jnp.bfloat16),
            pltpu.VMEM((2, rows, TILE), jnp.bfloat16),
            pltpu.SemaphoreType.DMA,
            pltpu.SemaphoreType.DMA((SLOTS, 2)),
            pltpu.SemaphoreType.DMA((2, pieces)),
        ],
        compiler_params=kernel_params(),
        cost_estimate=pl.CostEstimate(
            flops=4 * rows * (heads + units) * half_cols + 4 * rows * slots * heads,
            bytes_accessed=4 * (heads + units) * half_cols + 2 * rows * (heads + units + 2 * half_cols),
            transcendentals=rows * slots * heads // 128,
        ),
        name="combine",
    )(half, bias, q, *keys, *values, act, wa_own, wa_other, wm_own, wm_other)


def finish_kernel(stream, shift, scale, w_final, velocity):
    normed = (layer_norm(stream[...].astype(jnp.float32)) * scale[...] + shift[...]).astype(jnp.bfloat16)
    velocity[...] = lax.dot_general(
        normed, w_final[...], (((1,), (1,)), ((), ())), preferred_element_type=jnp.float32
    )


def finish(stream, shift, scale, w_final):
    return pl.pallas_call(
        finish_kernel,
        out_shape=jax.ShapeDtypeStruct((stream.shape[0], w_final.shape[0]), jnp.float32),
        compiler_params=kernel_params(),
        cost_estimate=pl.CostEstimate(
            flops=2 * stream.size * w_final.shape[0], bytes_accessed=2 * stream.size, transcendentals=0
        ),
        name="finish",
    )(stream, shift, scale, w_final)


def after(values, *done):
    return lax.optimization_barrier((values, *done))[0]


def by_prompt(
    hidden,
    latents,
    vec,
    slot_token,
    text_len,
    step_index,
    guidance,
    w_mod,
    w_qkv,
    w_mlp_in,
    qk_gain,
    w_attn_out,
    w_mlp_out,
    w_final,
):
    rows_dev, prompts, model_width = hidden.shape[1:]
    head_size = qk_gain.shape[-1]
    tok_index = lax.axis_index("tok")
    mlp_index = lax.axis_index("mlp")
    half_index = lax.axis_index("cfg")
    half = half_index[None].astype(jnp.int32)

    sends = pick(tok_index[None].astype(jnp.int32), jnp.transpose(hidden[0], (1, 0, 2)))

    silu_vec = jax.nn.silu(vec[0]).astype(jnp.bfloat16)
    mod_part = jnp.dot(after(silu_vec, sends[0]), w_mod, preferred_element_type=jnp.float32)
    pair_order = jnp.concatenate([jnp.arange(0, head_size, 2), jnp.arange(1, head_size, 2)])
    sorter = (jnp.arange(head_size)[:, None] == pair_order[None, :]).astype(jnp.bfloat16)
    sorter = jnp.kron(jnp.eye(2, dtype=jnp.bfloat16), sorter)
    wq_own = sort_pairs(jnp.transpose(w_qkv[0], (1, 0, 2)), after(sorter, mod_part))
    wu_own, wa_own, wm_own = w_mlp_in[0], w_attn_out[0], w_mlp_out[0]
    wu_other = xor_swap(wu_own, "cfg", 1)
    wq_other = xor_swap(after(wq_own, wu_other), "cfg", 1)
    gain = qk_gain[0][:, pair_order]

    states_0, states_1 = sends[0], xor_swap(sends[1], "tok", 1)
    by_x, by_y = xor_swap(states_0, "mlp", 1), xor_swap(states_0, "mlp", 2)
    mods = to_xor_order(mod_part, 0, tok_index, 2)
    mods = jnp.stack([mods[0::2], xor_swap(mods[1::2], "tok", 1)], 1)
    mods = jnp.concatenate([mods[0], xor_swap(after(mods[1], wq_own), "tok", 2)], 0)
    mods = jnp.stack([mods, xor_swap(after(mods, by_x, by_y, states_1), "mlp", 1)], 1)
    cut = rows_dev // 2
    far_top, far_low = xor_swap(by_x[:cut], "mlp", 2), xor_swap(by_y[cut:], "mlp", 1)
    mods = jnp.concatenate([mods, xor_swap(mods, "mlp", 2)], 1)
    mods = from_xor_order(from_xor_order(mods, 1, mlp_index, 2), 0, tok_index, 2)
    shift_mod, scale_mod, gate_mod, final_shift, final_scale = jnp.split(
        mods.reshape(1, 5 * model_width), 5, 1
    )
    scale_mod = 1.0 + scale_mod
    final_scale = 1.0 + final_scale
    wm_other = xor_swap(after(wm_own, shift_mod), "cfg", 1)
    wa_other = xor_swap(after(wa_own, wm_other), "cfg", 1)

    tokens = lax.dynamic_index_in_dim(slot_token, tok_index, 0, keepdims=False)
    tokens = tokens.reshape(prompts, 4, rows_dev)
    tokens = from_xor_order(from_xor_order(tokens, 1, mlp_index, 2), 0, tok_index, 2)
    cosine, sine_table = rope_table(tokens.reshape(-1), head_size, TXT, SIDE)
    cosine = jnp.concatenate([cosine, cosine], 1).reshape(prompts, 4 * rows_dev, head_size)
    sine_table = jnp.concatenate([-sine_table, sine_table], 1).reshape(cosine.shape)
    own_len = lax.dynamic_index_in_dim(text_len[0], tok_index, 0, keepdims=False)
    bias = jnp.where((tokens >= TXT) | (tokens < own_len), 0.0, -1e30).reshape(1, -1)

    own, queries, keys, values, acts = [], [], [], [], []
    done = (far_top, far_low, shift_mod)
    for j in range(prompts):
        if j == 0:
            states, far = states_0, jnp.concatenate([far_top, far_low], 0)
        else:
            states = states_1 if j == 1 else xor_swap(after(sends[j], own[-1]), "tok", j)
            send = after(states, *done)
            by_x, by_y, far = [xor_swap(send, "mlp", k) for k in (1, 2, 3)]
        own.append(states)
        q, k, v, act = project(
            half,
            (states, by_x, by_y, far),
            shift_mod,
            scale_mod,
            cosine[j],
            sine_table[j],
            gain,
            wq_own,
            wq_other,
            wu_own,
            wu_other,
        )
        queries.append(q)
        keys.append(k)
        values.append(v)
        acts.append(act)
        if j:
            done = (queries[j - 1], by_x, by_y, far, wm_other if j == 1 else wa_other)

    streams, moved, speeds = [None] * prompts, [None] * prompts, [None] * prompts
    parts = [None] * prompts

    def sum_up(j, *done):
        p0, by_x, by_y, far = parts[j]
        terms = [part.astype(jnp.float32) for part in (after(p0, *done), by_x, by_y, far)]
        branch = (terms[0] + terms[1]) + (terms[2] + terms[3])
        streams[j] = (own[j].astype(jnp.float32) + gate_mod * branch).astype(jnp.bfloat16)
        moved[j] = xor_swap(streams[j], "tok", j) if j else streams[j]
        speeds[j] = finish(streams[j], final_shift, final_scale, w_final.T)
        if j:
            speeds[j] = xor_swap(speeds[j], "tok", j)

    done = ()
    for j in reversed(range(prompts)):
        p0, p1, p2, p3 = combine(
            half,
            bias,
            after(queries[j], *done),
            keys,
            values,
            acts[j],
            wa_own,
            wa_other,
            wm_own,
            wm_other,
        )
        parts[j] = (p0, xor_swap(p1, "mlp", 1), xor_swap(p2, "mlp", 2), xor_swap(p3, "mlp", 3))
        if j + 2 < prompts:
            sum_up(j + 2, p0, *([moved[j + 3]] if j + 3 < prompts else []))
            done = (streams[j + 2],)
    sum_up(1, streams[2])
    sum_up(0, streams[1], moved[2])

    streams = moved
    stream = from_xor_order(jnp.stack(streams, 1), 1, tok_index, 2)
    half_velocity = from_xor_order(jnp.stack(speeds, 1), 1, tok_index, 2)
    own_first = (tok_index * 4 + mlp_index) * rows_dev
    own_tokens = lax.dynamic_slice_in_dim(slot_token, own_first, rows_dev, 1).T
    half_velocity = jnp.where((own_tokens >= TXT)[:, :, None], half_velocity, 0.0)
    return guided(half_velocity, half_index, latents, step_index, guidance) + (stream[None],)


def guided(half_velocity, half_index, latents, step_index, guidance):
    channel_half = latents.shape[2]
    own_part = lax.dynamic_slice_in_dim(half_velocity, half_index * channel_half, channel_half, 2)
    sent_part = lax.dynamic_slice_in_dim(
        half_velocity, (1 - half_index) * channel_half, channel_half, 2
    )
    partner = xor_swap(sent_part, "cfg", 1)
    first_half = half_index == 0
    cond_part = jnp.where(first_half, own_part, partner)
    uncond_part = jnp.where(first_half, partner, own_part)
    velocity = uncond_part + guidance[0] * (cond_part - uncond_part)
    current = step_index[0].astype(jnp.float32)
    step_size = sigma_at(current + 1.0, STEPS) - sigma_at(current, STEPS)
    return (velocity, latents + step_size * velocity)


def fits_by_prompt(mesh):
    return mesh.shape["cfg"] == 2 and mesh.shape["tok"] == PROMPTS and mesh.shape["mlp"] == 4


def solution(mesh):
    return jax.shard_map(
        by_prompt if fits_by_prompt(mesh) else on_device,
        mesh=mesh,
        in_specs=(
            P("cfg", ("tok", "mlp"), None, None),
            P(("tok", "mlp"), None, "cfg"),
            P("cfg", None, None),
            P(),
            P("cfg", None),
            P(),
            P(),
            P(None, ("tok", "mlp")),
            P(None, "cfg", None, "mlp"),
            P(None, "cfg", "mlp"),
            P(),
            P(None, "mlp", "cfg"),
            P(None, "mlp", "cfg"),
            P(),
        ),
        out_specs=(
            P(("tok", "mlp"), None, "cfg"),
            P(("tok", "mlp"), None, "cfg"),
            P("cfg", ("tok", "mlp"), None, None),
        ),
        check_vma=False,
    )
```

```python
import math

import jax
import jax.numpy as jnp
from jax import lax
from jax.experimental import pallas as pl
from jax.experimental.pallas import tpu as pltpu
from jax.sharding import PartitionSpec as P

LAYERS = 1
SIDE = 32
TXT = 512
STEPS = 28
PROMPTS = 4


EPSILON = 1e-06
ROPE_BASE = 10000.0
TIME_SHIFT = 3.0


def xor_swap(value, axis, apart):
    return lax.ppermute(value, axis, [(i, i ^ apart) for i in range(lax.axis_size(axis))])


def layer_norm(values):
    average = jnp.mean(values, axis=-1, keepdims=True)
    centred = values - average
    spread = jnp.mean(centred * centred, axis=-1, keepdims=True)
    return centred * lax.rsqrt(spread + EPSILON)


def rms_norm(values, gains):
    return values * lax.rsqrt(jnp.mean(values * values, axis=-1, keepdims=True) + EPSILON) * gains


def rope_table(tokens, head_size, text_count, side_count):
    pair_count = head_size // 2
    first_pairs = head_size // 16
    axis_pairs = (head_size - head_size // 8) // 4
    pair_index = jnp.arange(pair_count).astype(jnp.float32)
    in_rows = (pair_index >= first_pairs) & (pair_index < first_pairs + axis_pairs)
    in_cols = pair_index >= first_pairs + axis_pairs
    log_base = math.log(ROPE_BASE)
    freq_rows = jnp.where(
        in_rows, jnp.exp(-log_base * (pair_index - first_pairs) / axis_pairs), 0.0
    )
    freq_cols = jnp.where(
        in_cols, jnp.exp(-log_base * (pair_index - first_pairs - axis_pairs) / axis_pairs), 0.0
    )
    is_image = tokens >= text_count
    image_pos = jnp.where(is_image, tokens - text_count, 0)
    row_pos = (image_pos // side_count).astype(jnp.float32)
    col_pos = (image_pos % side_count).astype(jnp.float32)
    angles = row_pos[..., None] * freq_rows + col_pos[..., None] * freq_cols
    return (jnp.cos(angles), jnp.sin(angles))


def apply_rope(values, cosine, sine_table):
    even_part = values[..., 0::2]
    odd_part = values[..., 1::2]
    return jnp.concatenate(
        [even_part * cosine - odd_part * sine_table, even_part * sine_table + odd_part * cosine],
        axis=-1,
    )


def sigma_at(position, steps_total):
    remain = 1.0 - position / steps_total
    return TIME_SHIFT * remain / (1.0 + (TIME_SHIFT - 1.0) * remain)


def on_device(
    hidden,
    latents,
    vec,
    slot_token,
    text_len,
    step_index,
    guidance,
    w_mod,
    w_qkv,
    w_mlp_in,
    qk_gain,
    w_attn_out,
    w_mlp_out,
    w_final,
):
    rows_dev = hidden.shape[1]
    prompts = hidden.shape[2]
    model_width = hidden.shape[3]
    head_size = qk_gain.shape[-1]
    mlp_count = lax.axis_size("mlp")
    tile_rows = rows_dev * mlp_count
    tok_index = lax.axis_index("tok")
    mlp_index = lax.axis_index("mlp")
    half_index = lax.axis_index("cfg")
    stream = hidden[0]
    silu_vec = jax.nn.silu(vec[0]).astype(jnp.bfloat16)
    mod_part = jnp.dot(silu_vec, w_mod, preferred_element_type=jnp.float32)
    modulation = lax.all_gather(mod_part, ("tok", "mlp"), axis=1, tiled=True)
    key_valid = ((slot_token >= TXT) | (slot_token < text_len[0][:, None])).astype(jnp.float32)
    tile_tokens = lax.dynamic_slice_in_dim(slot_token, tok_index * tile_rows, tile_rows, 1).T
    cosine, sine_table = rope_table(tile_tokens, head_size, TXT, SIDE)
    shift_mod = modulation[:, 0:model_width]
    scale_mod = modulation[:, model_width : 2 * model_width]
    gate_mod = modulation[:, 2 * model_width : 3 * model_width]
    normed = (
        layer_norm(stream.astype(jnp.float32)) * (1.0 + scale_mod[None]) + shift_mod[None]
    ).astype(jnp.bfloat16)
    tile_input = lax.all_gather(normed, "mlp", axis=0, tiled=True)
    qkv_weight = w_qkv[0]
    unit_weight = w_mlp_in[0]
    qkv_cols = qkv_weight.shape[1] * qkv_weight.shape[2]
    pieces = (
        lax.all_gather(qkv_weight, "cfg", axis=0, tiled=True),
        lax.all_gather(unit_weight, "cfg", axis=0, tiled=True),
    )
    number = pieces[0].shape[0]
    qkv_piece = pieces[0].reshape(number, qkv_cols)
    qkv_pre = jnp.einsum("tpd,dk->tpk", tile_input, qkv_piece, preferred_element_type=jnp.float32)
    unit_pre = jnp.einsum("tpd,dk->tpk", tile_input, pieces[1], preferred_element_type=jnp.float32)
    heads_dev = qkv_weight.shape[2] // head_size
    projected = qkv_pre.reshape(tile_rows, prompts, 3, heads_dev, head_size)
    queries = apply_rope(
        rms_norm(projected[:, :, 0], qk_gain[0, 0]), cosine[:, :, None], sine_table[:, :, None]
    ).astype(jnp.bfloat16)
    keys_rot = apply_rope(
        rms_norm(projected[:, :, 1], qk_gain[0, 1]), cosine[:, :, None], sine_table[:, :, None]
    ).astype(jnp.bfloat16)
    values = projected[:, :, 2].astype(jnp.bfloat16)
    activation = jax.nn.gelu(unit_pre, approximate=True).astype(jnp.bfloat16)
    keys_piece = lax.all_gather(keys_rot, "tok", axis=0, tiled=True)
    values_piece = lax.all_gather(values, "tok", axis=0, tiled=True)
    scores = jnp.einsum(
        "sphe,tphe->phst", queries, keys_piece, preferred_element_type=jnp.float32
    ) / math.sqrt(head_size)
    softened = jnp.exp(scores) * key_valid[:, None, None, :]
    numerator = jnp.einsum(
        "phst,tphe->sphe",
        softened.astype(jnp.bfloat16),
        values_piece,
        preferred_element_type=jnp.float32,
    )
    numerator, denominator = (numerator, jnp.sum(softened, axis=-1))
    attended = (numerator / jnp.transpose(denominator, (2, 0, 1))[..., None]).astype(jnp.bfloat16)
    attended = attended.reshape(tile_rows, prompts, heads_dev * head_size)
    out_attn = lax.all_gather(w_attn_out[0], "cfg", axis=1, tiled=True)
    out_units = lax.all_gather(w_mlp_out[0], "cfg", axis=1, tiled=True)
    branch_out = lax.psum_scatter(
        (
            jnp.einsum("tpk,kd->tpd", attended, out_attn, preferred_element_type=jnp.float32)
            + jnp.einsum("tpk,kd->tpd", activation, out_units, preferred_element_type=jnp.float32)
        ).astype(jnp.bfloat16),
        "mlp",
        scatter_dimension=0,
        tiled=True,
    ).astype(jnp.float32)
    stream = (stream.astype(jnp.float32) + gate_mod[None] * branch_out).astype(jnp.bfloat16)
    final_lo = 3 * LAYERS * model_width
    final_shift = modulation[:, final_lo : final_lo + model_width]
    final_scale = modulation[:, final_lo + model_width : final_lo + 2 * model_width]
    final_normed = (
        layer_norm(stream.astype(jnp.float32)) * (1.0 + final_scale[None]) + final_shift[None]
    ).astype(jnp.bfloat16)
    own_first = (tok_index * mlp_count + mlp_index) * rows_dev
    own_tokens = lax.dynamic_slice_in_dim(slot_token, own_first, rows_dev, 1).T
    half_velocity = jnp.einsum(
        "rpd,dc->rpc", final_normed, w_final, preferred_element_type=jnp.float32
    )
    half_velocity = jnp.where((own_tokens >= TXT)[:, :, None], half_velocity, 0.0)
    return guided(half_velocity, half_index, latents, step_index, guidance) + (stream[None],)


VMEM_BYTES = 56 * 1024 * 1024
TILE = 512
SLOTS = 3
ANY = pl.BlockSpec(memory_space=pl.ANY)
VMEM = pl.BlockSpec(memory_space=pltpu.VMEM)
SMEM = pl.BlockSpec(memory_space=pltpu.SMEM)


def kernel_params():
    return pltpu.CompilerParams(vmem_limit_bytes=VMEM_BYTES)


def flip_by_bit(values, axis, bit):
    return jnp.where(bit, jnp.flip(values, axis), values)


def from_xor_order(values, axis, index, bits):
    shape = values.shape
    split = shape[:axis] + (2,) * bits + shape[axis + 1 :]
    values = values.reshape(split)
    for place in range(bits):
        bit = (index >> (bits - 1 - place)) & 1
        values = flip_by_bit(values, axis + place, bit == 1)
    return values.reshape(shape)


def xor_rows(count, index):
    places = jnp.arange(count)
    return (places[:, None] ^ index) == places[None, :]


def pick_kernel(place_ref, *refs):
    count = len(refs) // 2
    for j in range(count):
        refs[count + j][...] = refs[j][0]


def pick(place, states):
    count, rows, width = states.shape
    take = lambda j: lambda i, s: (s[0] ^ j, i, 0)
    return pl.pallas_call(
        pick_kernel,
        out_shape=(jax.ShapeDtypeStruct((rows, width), states.dtype),) * count,
        grid_spec=pltpu.PrefetchScalarGridSpec(
            num_scalar_prefetch=1,
            grid=(2,),
            in_specs=[pl.BlockSpec((1, rows // 2, width), take(j)) for j in range(count)],
            out_specs=[pl.BlockSpec((rows // 2, width), lambda i, s: (i, 0))] * count,
        ),
        compiler_params=kernel_params(),
        cost_estimate=pl.CostEstimate(flops=0, bytes_accessed=4 * states.size, transcendentals=0),
        name="pick",
    )(place, *([states] * count))


def sort_pairs_kernel(w_ref, sorter, out):
    part = pl.program_id(0)
    wide = sorter.shape[0]

    @pl.when(part < 2)
    def _():
        for lo in range(0, out.shape[1], wide):
            out[:, lo : lo + wide] = jnp.dot(
                w_ref[0, :, lo : lo + wide], sorter[...], preferred_element_type=jnp.float32
            ).astype(jnp.bfloat16)

    @pl.when(part == 2)
    def _():
        out[...] = w_ref[0]


def sort_pairs(weight, sorter):
    parts, depth, cols = weight.shape
    rows = depth // 2
    return pl.pallas_call(
        sort_pairs_kernel,
        out_shape=jax.ShapeDtypeStruct((depth, parts * cols), weight.dtype),
        grid=(parts, 2),
        in_specs=[
            pl.BlockSpec((1, rows, cols), lambda p, i: (p, i, 0)),
            pl.BlockSpec(sorter.shape, lambda p, i: (0, 0)),
        ],
        out_specs=pl.BlockSpec((rows, cols), lambda p, i: (i, p)),
        compiler_params=kernel_params(),
        cost_estimate=pl.CostEstimate(
            flops=4 * depth * cols * sorter.shape[0], bytes_accessed=4 * weight.size, transcendentals=0
        ),
        name="sort_pairs",
    )(weight, sorter)


def project_kernel(
    half_ref,
    shift,
    scale,
    cos_ref,
    sin_ref,
    gain,
    x0,
    x1,
    x2,
    x3,
    wq_own,
    wq_other,
    wu_own,
    wu_other,
    q_out,
    k_out,
    v_out,
    act_out,
    landed,
    normed,
    held,
    ready,
    x_sem,
    w_sem,
    out_sem,
):
    half = half_ref[0]
    depth = wq_own.shape[0]
    head = gain.shape[1]
    pieces = (x0, x1, x2, x3)
    rows = x0.shape[0]
    units = wu_own.shape[1] // TILE

    def weights(own, other, column, slot):
        return [
            pltpu.make_async_copy(
                ref.at[:, pl.ds(column, TILE)], held.at[slot, side], w_sem.at[slot, side]
            )
            for side, ref in enumerate((own, other))
        ]

    def result(out, column, slot):
        return pltpu.make_async_copy(
            ready.at[slot], out.at[:, pl.ds(column, TILE)], out_sem.at[slot]
        )

    loads = [pltpu.make_async_copy(ref, landed.at[i], x_sem.at[i]) for i, ref in enumerate(pieces)]
    loads[0].start()
    for copy in weights(wq_own, wq_other, 0, 0):
        copy.start()
    for load in loads[1:]:
        load.start()
    for part in (1, 2):
        for copy in weights(wq_own, wq_other, part * TILE, part):
            copy.start()

    for index, load in enumerate(loads):
        load.wait()
        block = layer_norm(landed[index].astype(jnp.float32))
        block = (block * scale[...] + shift[...]).astype(jnp.bfloat16)
        normed[0, index * rows : (index + 1) * rows, :] = block[:, :depth]
        normed[1, index * rows : (index + 1) * rows, :] = block[:, depth:]

    cosine = jnp.concatenate([cos_ref[...], cos_ref[...]], 1)
    sine = jnp.concatenate([-sin_ref[...], sin_ref[...]], 1)

    def product(slot):
        return jnp.dot(
            normed[half], held[slot, 0], preferred_element_type=jnp.float32
        ) + jnp.dot(normed[1 - half], held[slot, 1], preferred_element_type=jnp.float32)

    for part, out in enumerate((q_out, k_out, v_out)):
        for copy in weights(wq_own, wq_other, part * TILE, part):
            copy.wait()
        values = product(part)
        if part == 2:
            result(out, 0, 0).wait()
            ready[0] = values.astype(jnp.bfloat16)
        else:
            for lo in range(0, TILE, head):
                turned = rms_norm(values[:, lo : lo + head], gain[part : part + 1, :])
                turned = turned * cosine + pltpu.roll(turned, head // 2, 1) * sine
                ready[part, :, lo : lo + head] = turned.astype(jnp.bfloat16)
        result(out, 0, part % 2).start()
        for copy in weights(wu_own, wu_other, part * TILE, part):
            copy.start()

    @pl.loop(0, units)
    def _(index):
        slot = lax.rem(index, SLOTS)
        to = lax.rem(index + 1, 2)
        column = pl.multiple_of(index * TILE, TILE)
        for copy in weights(wu_own, wu_other, column, slot):
            copy.wait()
        values = jax.nn.gelu(product(slot), approximate=True).astype(jnp.bfloat16)
        result(act_out, column, to).wait()
        ready[to] = values
        result(act_out, column, to).start()

        @pl.when(index + SLOTS < units)
        def _():
            later = pl.multiple_of((index + SLOTS) * TILE, TILE)
            for copy in weights(wu_own, wu_other, later, slot):
                copy.start()

    for slot in range(2):
        result(act_out, 0, slot).wait()


def project(half, pieces, shift, scale, cos_rows, sin_rows, gain, wq_own, wq_other, wu_own, wu_other):
    rows = sum(piece.shape[0] for piece in pieces)
    width = pieces[0].shape[1]
    depth = wq_own.shape[0]
    units = wu_own.shape[1]
    head_out = jax.ShapeDtypeStruct((rows, TILE), jnp.bfloat16)
    return pl.pallas_call(
        project_kernel,
        out_shape=(head_out, head_out, head_out, jax.ShapeDtypeStruct((rows, units), jnp.bfloat16)),
        in_specs=[SMEM] + [VMEM] * 5 + [ANY] * 8,
        out_specs=[ANY] * 4,
        scratch_shapes=[
            pltpu.VMEM((len(pieces), rows // len(pieces), width), jnp.bfloat16),
            pltpu.VMEM((2, rows, depth), jnp.bfloat16),
            pltpu.VMEM((SLOTS, 2, depth, TILE), jnp.bfloat16),
            pltpu.VMEM((2, rows, TILE), jnp.bfloat16),
            pltpu.SemaphoreType.DMA((len(pieces),)),
            pltpu.SemaphoreType.DMA((SLOTS, 2)),
            pltpu.SemaphoreType.DMA((2,)),
        ],
        compiler_params=kernel_params(),
        cost_estimate=pl.CostEstimate(
            flops=2 * rows * width * (3 * TILE + units),
            bytes_accessed=2 * width * (3 * TILE + units) + 2 * rows * (width + 3 * TILE + units),
            transcendentals=rows * units,
        ),
        name="project",
    )(half, shift, scale, cos_rows, sin_rows, gain, *pieces, wq_own, wq_other, wu_own, wu_other)


def combine_kernel(
    half_ref,
    bias,
    q,
    k0,
    k1,
    k2,
    k3,
    v0,
    v1,
    v2,
    v3,
    act,
    wa_own,
    wa_other,
    wm_own,
    wm_other,
    p0,
    p1,
    p2,
    p3,
    attended,
    units,
    held_a,
    held_m,
    ready,
    act_sem,
    w_sem,
    out_sem,
):
    half = half_ref[0]
    keys, values, outs = (k0, k1, k2, k3), (v0, v1, v2, v3), (p0, p1, p2, p3)
    rows = q.shape[0]
    size = k0.shape[0]
    piece = p0.shape[0]
    head = 128
    steps = wa_own.shape[1] // TILE

    def weights(wa, wm, column, slot):
        return [
            pltpu.make_async_copy(wa.at[:, pl.ds(column, TILE)], held_a.at[slot], w_sem.at[slot, 0]),
            pltpu.make_async_copy(wm.at[:, pl.ds(column, TILE)], held_m.at[slot], w_sem.at[slot, 1]),
        ]

    def results(column, slot):
        return [
            pltpu.make_async_copy(
                ready.at[slot, pl.ds(i * piece, piece)],
                out.at[:, pl.ds(column, TILE)],
                out_sem.at[slot, i],
            )
            for i, out in enumerate(outs)
        ]

    load = pltpu.make_async_copy(act, units, act_sem)
    load.start()
    for slot in range(SLOTS):
        for copy in weights(wa_own, wm_own, slot * TILE, slot):
            copy.start()

    @pl.loop(0, q.shape[1] // head)
    def _(index):
        lanes = pl.ds(pl.multiple_of(index * head, head), head)
        total = jnp.zeros((rows, 1), jnp.float32)
        numerator = jnp.zeros((rows, head), jnp.float32)
        for part in range(len(keys)):
            scores = lax.dot_general(
                q[:, lanes],
                keys[part][:, lanes],
                (((1,), (1,)), ((), ())),
                preferred_element_type=jnp.float32,
            )
            soft = jnp.exp(
                scores * (1.0 / math.sqrt(head)) + bias[:, part * size : (part + 1) * size]
            )
            total += jnp.sum(soft, axis=-1, keepdims=True)
            numerator += jnp.dot(
                soft.astype(jnp.bfloat16), values[part][:, lanes], preferred_element_type=jnp.float32
            )
        attended[:, lanes] = (numerator / total).astype(jnp.bfloat16)

    load.wait()

    def write(index, slot, column, first, wa, wm):
        for copy in weights(wa, wm, 0, slot):
            copy.wait()
        partial = jnp.dot(attended[...], held_a[slot], preferred_element_type=jnp.float32)
        partial += jnp.dot(units[...], held_m[slot], preferred_element_type=jnp.float32)
        to = lax.rem(index, 2)

        @pl.when(index >= 2)
        def _():
            for copy in results(0, to):
                copy.wait()

        ready[to] = partial.astype(jnp.bfloat16)
        for copy in results(column, to):
            copy.start()

    @pl.loop(0, 2 * steps)
    def _(index):
        slot = lax.rem(index, SLOTS)
        place = lax.rem(index + steps * half, 2 * steps)
        write(index, slot, pl.multiple_of(place * TILE, TILE), 0, wa_own, wm_own)

        @pl.when(index + SLOTS < 2 * steps)
        def _():
            later = pl.multiple_of((index + SLOTS - steps) * TILE, TILE)
            for copy in weights(wa_other, wm_other, later, slot):
                copy.start()

    for slot in range(2):
        for copy in results(0, slot):
            copy.wait()


def combine(half, bias, q, keys, values, act, wa_own, wa_other, wm_own, wm_other):
    rows, heads = q.shape
    units = act.shape[1]
    slots = bias.shape[1]
    half_cols = wa_own.shape[1]
    assert half_cols == SLOTS * TILE
    pieces = len(keys)
    part = jax.ShapeDtypeStruct((rows // pieces, 2 * half_cols), jnp.bfloat16)
    return pl.pallas_call(
        combine_kernel,
        out_shape=(part,) * pieces,
        in_specs=[SMEM] + [VMEM] * (2 + 2 * pieces) + [ANY] * 5,
        out_specs=[ANY] * pieces,
        scratch_shapes=[
            pltpu.VMEM((rows, heads), jnp.bfloat16),
            pltpu.VMEM((rows, units), jnp.bfloat16),
            pltpu.VMEM((SLOTS, heads, TILE), jnp.bfloat16),
            pltpu.VMEM((SLOTS, units, TILE), jnp.bfloat16),
            pltpu.VMEM((2, rows, TILE), jnp.bfloat16),
            pltpu.SemaphoreType.DMA,
            pltpu.SemaphoreType.DMA((SLOTS, 2)),
            pltpu.SemaphoreType.DMA((2, pieces)),
        ],
        compiler_params=kernel_params(),
        cost_estimate=pl.CostEstimate(
            flops=4 * rows * (heads + units) * half_cols + 4 * rows * slots * heads,
            bytes_accessed=4 * (heads + units) * half_cols + 2 * rows * (heads + units + 2 * half_cols),
            transcendentals=rows * slots * heads // 128,
        ),
        name="combine",
    )(half, bias, q, *keys, *values, act, wa_own, wa_other, wm_own, wm_other)


def finish_kernel(stream, shift, scale, w_final, velocity):
    normed = (layer_norm(stream[...].astype(jnp.float32)) * scale[...] + shift[...]).astype(jnp.bfloat16)
    velocity[...] = lax.dot_general(
        normed, w_final[...], (((1,), (1,)), ((), ())), preferred_element_type=jnp.float32
    )


def finish(stream, shift, scale, w_final):
    return pl.pallas_call(
        finish_kernel,
        out_shape=jax.ShapeDtypeStruct((stream.shape[0], w_final.shape[0]), jnp.float32),
        compiler_params=kernel_params(),
        cost_estimate=pl.CostEstimate(
            flops=2 * stream.size * w_final.shape[0], bytes_accessed=2 * stream.size, transcendentals=0
        ),
        name="finish",
    )(stream, shift, scale, w_final)


def add(left, right):
    return (left.astype(jnp.float32) + right.astype(jnp.float32)).astype(jnp.bfloat16)


def after(values, *done):
    return lax.optimization_barrier((values, *done))[0]


def by_prompt(
    hidden,
    latents,
    vec,
    slot_token,
    text_len,
    step_index,
    guidance,
    w_mod,
    w_qkv,
    w_mlp_in,
    qk_gain,
    w_attn_out,
    w_mlp_out,
    w_final,
):
    rows_dev, prompts, model_width = hidden.shape[1:]
    head_size = qk_gain.shape[-1]
    tok_index = lax.axis_index("tok")
    mlp_index = lax.axis_index("mlp")
    half_index = lax.axis_index("cfg")
    half = half_index[None].astype(jnp.int32)

    sends = pick(tok_index[None].astype(jnp.int32), jnp.transpose(hidden[0], (1, 0, 2)))

    silu_vec = jax.nn.silu(vec[0]).astype(jnp.bfloat16)
    silu_vec = jnp.dot(
        xor_rows(prompts, tok_index).astype(jnp.bfloat16), after(silu_vec, sends[0])
    ).astype(jnp.bfloat16)
    mod_part = jnp.dot(silu_vec, w_mod, preferred_element_type=jnp.float32)

    tokens = lax.dynamic_index_in_dim(slot_token, tok_index, 0, keepdims=False).reshape(-1, rows_dev)
    own_len = lax.dynamic_index_in_dim(text_len[0], tok_index, 0, keepdims=False)
    order = xor_rows(4 * prompts, 4 * tok_index + mlp_index)
    tokens = jnp.dot(
        order.astype(jnp.float32), tokens.astype(jnp.float32), precision=lax.Precision.HIGHEST
    )
    tokens = jnp.round(tokens).astype(jnp.int32)
    bias = jnp.where((tokens >= TXT) | (tokens < own_len), 0.0, -1e30).reshape(1, -1)
    cosine, sine_table = rope_table(tokens.reshape(-1), head_size, TXT, SIDE)
    cosine = cosine.reshape(prompts, 4 * rows_dev, -1)
    sine_table = sine_table.reshape(cosine.shape)

    pair_order = jnp.concatenate([jnp.arange(0, head_size, 2), jnp.arange(1, head_size, 2)])
    sorter = (jnp.arange(head_size)[:, None] == pair_order[None, :]).astype(jnp.bfloat16)
    sorter = jnp.kron(jnp.eye(2, dtype=jnp.bfloat16), sorter)
    wq_own = sort_pairs(jnp.transpose(w_qkv[0], (1, 0, 2)), after(sorter, mod_part))
    wu_own, wa_own, wm_own = w_mlp_in[0], w_attn_out[0], w_mlp_out[0]
    wu_other = xor_swap(wu_own, "cfg", 1)
    wq_other = xor_swap(after(wq_own, wu_other), "cfg", 1)
    gain = qk_gain[0][:, pair_order]

    states_0, states_1 = sends[0], xor_swap(sends[1], "tok", 1)
    by_x, by_y = xor_swap(states_0, "mlp", 1), xor_swap(states_0, "mlp", 2)
    mods = jnp.stack([mod_part[0::2], xor_swap(mod_part[1::2], "tok", 1)], 1)
    mods = jnp.concatenate([mods[0], xor_swap(after(mods[1], wq_own), "tok", 2)], 0)
    mods = jnp.stack([mods, xor_swap(after(mods, by_x, by_y, states_1), "mlp", 1)], 1)
    cut = rows_dev // 2
    far_top, far_low = xor_swap(by_x[:cut], "mlp", 2), xor_swap(by_y[cut:], "mlp", 1)
    mods = jnp.concatenate([mods, xor_swap(after(mods, far_top, far_low), "mlp", 2)], 1)
    mods = jnp.dot(
        order.astype(jnp.float32), mods.reshape(order.shape[0], -1), precision=lax.Precision.HIGHEST
    )
    shift_mod, scale_mod, gate_mod, final_shift, final_scale = jnp.split(
        mods.reshape(1, 5 * model_width), 5, 1
    )
    scale_mod = 1.0 + scale_mod
    final_scale = 1.0 + final_scale
    wm_other = xor_swap(after(wm_own, shift_mod), "cfg", 1)
    wa_other = xor_swap(after(wa_own, wm_other), "cfg", 1)

    own, queries, keys, values, acts = [], [], [], [], []
    done = (far_top, far_low, shift_mod)
    for j in range(prompts):
        if j == 0:
            states, far = states_0, jnp.concatenate([far_top, far_low], 0)
        else:
            states = states_1 if j == 1 else xor_swap(after(sends[j], own[-1], *queries[: j - 2]), "tok", j)
            send = after(states, *done)
            by_x, by_y, far = [xor_swap(send, "mlp", k) for k in (1, 2, 3)]
        own.append(states)
        q, k, v, act = project(
            half,
            (states, by_x, by_y, far),
            shift_mod,
            scale_mod,
            cosine[j],
            sine_table[j],
            gain,
            wq_own,
            wq_other,
            wu_own,
            wu_other,
        )
        queries.append(q)
        keys.append(k)
        values.append(v)
        acts.append(act)
        if j:
            done = (queries[j - 1], by_x, by_y, far, wm_other if j == 1 else wa_other)

    streams, moved, speeds = [None] * prompts, [None] * prompts, [None] * prompts
    parts = [None] * prompts

    def straight(j):
        p0, p1, p2, p3 = parts[j]
        parts[j] = (p0, [xor_swap(p, "mlp", k) for k, p in ((1, p1), (2, p2), (3, p3))])

    def first_step(j):
        p0, p1, p2, p3 = parts[j]
        if j == 0:
            top, low = xor_swap(p3[:cut], "mlp", 1), xor_swap(p3[cut:], "mlp", 2)
        elif j % 2:
            top, low = xor_swap(p3, "mlp", 1), None
        else:
            top, low = None, xor_swap(p3, "mlp", 2)
        parts[j] = (p0, p1, p2, top, low)

    def second_step(j, *done):
        p0, p1, p2, top, low = parts[j]
        if j == 0:
            p1 = jnp.concatenate([p1[:cut], add(p1[cut:], low)], 0)
            p2 = jnp.concatenate([add(p2[:cut], top), p2[cut:]], 0)
        elif j % 2:
            p2 = add(p2, after(top, *done))
        else:
            p1 = add(p1, after(low, *done))
        parts[j] = (p0, [xor_swap(p1, "mlp", 1), xor_swap(p2, "mlp", 2)])
        return p2 if j % 2 else p1

    def sum_up(j, *done):
        p0, terms = parts[j]
        branch = after(p0, *done).astype(jnp.float32)
        for term in terms:
            branch = branch + term.astype(jnp.float32)
        streams[j] = (own[j].astype(jnp.float32) + gate_mod * branch).astype(jnp.bfloat16)
        moved[j] = xor_swap(streams[j], "tok", j) if j else streams[j]
        speeds[j] = finish(streams[j], final_shift, final_scale, w_final.T)
        if j:
            speeds[j] = xor_swap(speeds[j], "tok", j)
        return streams[j]

    done = ()
    for j in reversed(range(prompts)):
        parts[j] = combine(
            half,
            bias,
            after(queries[j], *done),
            keys,
            values,
            acts[j],
            wa_own,
            wa_other,
            wm_own,
            wm_other,
        )
        mark, done = parts[j][0], ()
        if j + 1 == prompts:
            straight(j)
            continue
        first_step(j)
        if j + 2 < prompts:
            done += (sum_up(j + 2, mark, *([moved[j + 3]] if j + 3 < prompts else [])),)
            done += (second_step(j + 1, mark),)
    done = (sum_up(1, streams[2]), second_step(0))
    sum_up(0, *done, moved[2])

    streams = moved
    stream = from_xor_order(jnp.stack(streams, 1), 1, tok_index, 2)
    half_velocity = from_xor_order(jnp.stack(speeds, 1), 1, tok_index, 2)
    own_first = (tok_index * 4 + mlp_index) * rows_dev
    own_tokens = lax.dynamic_slice_in_dim(slot_token, own_first, rows_dev, 1).T
    half_velocity = jnp.where((own_tokens >= TXT)[:, :, None], half_velocity, 0.0)
    return guided(half_velocity, half_index, latents, step_index, guidance) + (stream[None],)


def guided(half_velocity, half_index, latents, step_index, guidance):
    channel_half = latents.shape[2]
    own_part = lax.dynamic_slice_in_dim(half_velocity, half_index * channel_half, channel_half, 2)
    sent_part = lax.dynamic_slice_in_dim(
        half_velocity, (1 - half_index) * channel_half, channel_half, 2
    )
    partner = xor_swap(sent_part, "cfg", 1)
    first_half = half_index == 0
    cond_part = jnp.where(first_half, own_part, partner)
    uncond_part = jnp.where(first_half, partner, own_part)
    velocity = uncond_part + guidance[0] * (cond_part - uncond_part)
    current = step_index[0].astype(jnp.float32)
    step_size = sigma_at(current + 1.0, STEPS) - sigma_at(current, STEPS)
    return (velocity, latents + step_size * velocity)


def fits_by_prompt(mesh):
    return mesh.shape["cfg"] == 2 and mesh.shape["tok"] == PROMPTS and mesh.shape["mlp"] == 4


def solution(mesh):
    return jax.shard_map(
        by_prompt if fits_by_prompt(mesh) else on_device,
        mesh=mesh,
        in_specs=(
            P("cfg", ("tok", "mlp"), None, None),
            P(("tok", "mlp"), None, "cfg"),
            P("cfg", None, None),
            P(),
            P("cfg", None),
            P(),
            P(),
            P(None, ("tok", "mlp")),
            P(None, "cfg", None, "mlp"),
            P(None, "cfg", "mlp"),
            P(),
            P(None, "mlp", "cfg"),
            P(None, "mlp", "cfg"),
            P(),
        ),
        out_specs=(
            P(("tok", "mlp"), None, "cfg"),
            P(("tok", "mlp"), None, "cfg"),
            P("cfg", ("tok", "mlp"), None, None),
        ),
        check_vma=False,
    )
```

```python
import functools
import math

import jax
import jax.numpy as jnp
import numpy as np
from jax import lax
from jax.experimental import pallas as pl
from jax.experimental.pallas import tpu as pltpu
from jax.sharding import PartitionSpec as P

LAYERS = 1
SIDE = 32
TXT = 512
STEPS = 28
PROMPTS = 4


EPSILON = 1e-06
ROPE_BASE = 10000.0
TIME_SHIFT = 3.0


def xor_swap(value, axis, apart):
    return lax.ppermute(value, axis, [(i, i ^ apart) for i in range(lax.axis_size(axis))])


def layer_norm(values):
    average = jnp.mean(values, axis=-1, keepdims=True)
    centred = values - average
    spread = jnp.mean(centred * centred, axis=-1, keepdims=True)
    return centred * lax.rsqrt(spread + EPSILON)


def rms_norm(values, gains):
    return values * lax.rsqrt(jnp.mean(values * values, axis=-1, keepdims=True) + EPSILON) * gains


def rope_table(tokens, head_size, text_count, side_count):
    pair_count = head_size // 2
    first_pairs = head_size // 16
    axis_pairs = (head_size - head_size // 8) // 4
    pair_index = jnp.arange(pair_count).astype(jnp.float32)
    in_rows = (pair_index >= first_pairs) & (pair_index < first_pairs + axis_pairs)
    in_cols = pair_index >= first_pairs + axis_pairs
    log_base = math.log(ROPE_BASE)
    freq_rows = jnp.where(
        in_rows, jnp.exp(-log_base * (pair_index - first_pairs) / axis_pairs), 0.0
    )
    freq_cols = jnp.where(
        in_cols, jnp.exp(-log_base * (pair_index - first_pairs - axis_pairs) / axis_pairs), 0.0
    )
    is_image = tokens >= text_count
    image_pos = jnp.where(is_image, tokens - text_count, 0)
    row_pos = (image_pos // side_count).astype(jnp.float32)
    col_pos = (image_pos % side_count).astype(jnp.float32)
    angles = row_pos[..., None] * freq_rows + col_pos[..., None] * freq_cols
    return (jnp.cos(angles), jnp.sin(angles))


def apply_rope(values, cosine, sine_table):
    even_part = values[..., 0::2]
    odd_part = values[..., 1::2]
    return jnp.concatenate(
        [even_part * cosine - odd_part * sine_table, even_part * sine_table + odd_part * cosine],
        axis=-1,
    )


def sigma_at(position, steps_total):
    remain = 1.0 - position / steps_total
    return TIME_SHIFT * remain / (1.0 + (TIME_SHIFT - 1.0) * remain)


def on_device(
    hidden,
    latents,
    vec,
    slot_token,
    text_len,
    step_index,
    guidance,
    w_mod,
    w_qkv,
    w_mlp_in,
    qk_gain,
    w_attn_out,
    w_mlp_out,
    w_final,
):
    rows_dev = hidden.shape[1]
    prompts = hidden.shape[2]
    model_width = hidden.shape[3]
    head_size = qk_gain.shape[-1]
    mlp_count = lax.axis_size("mlp")
    tile_rows = rows_dev * mlp_count
    tok_index = lax.axis_index("tok")
    mlp_index = lax.axis_index("mlp")
    half_index = lax.axis_index("cfg")
    stream = hidden[0]
    silu_vec = jax.nn.silu(vec[0]).astype(jnp.bfloat16)
    mod_part = jnp.dot(silu_vec, w_mod, preferred_element_type=jnp.float32)
    modulation = lax.all_gather(mod_part, ("tok", "mlp"), axis=1, tiled=True)
    key_valid = ((slot_token >= TXT) | (slot_token < text_len[0][:, None])).astype(jnp.float32)
    tile_tokens = lax.dynamic_slice_in_dim(slot_token, tok_index * tile_rows, tile_rows, 1).T
    cosine, sine_table = rope_table(tile_tokens, head_size, TXT, SIDE)
    shift_mod = modulation[:, 0:model_width]
    scale_mod = modulation[:, model_width : 2 * model_width]
    gate_mod = modulation[:, 2 * model_width : 3 * model_width]
    normed = (
        layer_norm(stream.astype(jnp.float32)) * (1.0 + scale_mod[None]) + shift_mod[None]
    ).astype(jnp.bfloat16)
    tile_input = lax.all_gather(normed, "mlp", axis=0, tiled=True)
    qkv_weight = w_qkv[0]
    unit_weight = w_mlp_in[0]
    qkv_cols = qkv_weight.shape[1] * qkv_weight.shape[2]
    pieces = (
        lax.all_gather(qkv_weight, "cfg", axis=0, tiled=True),
        lax.all_gather(unit_weight, "cfg", axis=0, tiled=True),
    )
    number = pieces[0].shape[0]
    qkv_piece = pieces[0].reshape(number, qkv_cols)
    qkv_pre = jnp.einsum("tpd,dk->tpk", tile_input, qkv_piece, preferred_element_type=jnp.float32)
    unit_pre = jnp.einsum("tpd,dk->tpk", tile_input, pieces[1], preferred_element_type=jnp.float32)
    heads_dev = qkv_weight.shape[2] // head_size
    projected = qkv_pre.reshape(tile_rows, prompts, 3, heads_dev, head_size)
    queries = apply_rope(
        rms_norm(projected[:, :, 0], qk_gain[0, 0]), cosine[:, :, None], sine_table[:, :, None]
    ).astype(jnp.bfloat16)
    keys_rot = apply_rope(
        rms_norm(projected[:, :, 1], qk_gain[0, 1]), cosine[:, :, None], sine_table[:, :, None]
    ).astype(jnp.bfloat16)
    values = projected[:, :, 2].astype(jnp.bfloat16)
    activation = jax.nn.gelu(unit_pre, approximate=True).astype(jnp.bfloat16)
    keys_piece = lax.all_gather(keys_rot, "tok", axis=0, tiled=True)
    values_piece = lax.all_gather(values, "tok", axis=0, tiled=True)
    scores = jnp.einsum(
        "sphe,tphe->phst", queries, keys_piece, preferred_element_type=jnp.float32
    ) / math.sqrt(head_size)
    softened = jnp.exp(scores) * key_valid[:, None, None, :]
    numerator = jnp.einsum(
        "phst,tphe->sphe",
        softened.astype(jnp.bfloat16),
        values_piece,
        preferred_element_type=jnp.float32,
    )
    numerator, denominator = (numerator, jnp.sum(softened, axis=-1))
    attended = (numerator / jnp.transpose(denominator, (2, 0, 1))[..., None]).astype(jnp.bfloat16)
    attended = attended.reshape(tile_rows, prompts, heads_dev * head_size)
    out_attn = lax.all_gather(w_attn_out[0], "cfg", axis=1, tiled=True)
    out_units = lax.all_gather(w_mlp_out[0], "cfg", axis=1, tiled=True)
    branch_out = lax.psum_scatter(
        (
            jnp.einsum("tpk,kd->tpd", attended, out_attn, preferred_element_type=jnp.float32)
            + jnp.einsum("tpk,kd->tpd", activation, out_units, preferred_element_type=jnp.float32)
        ).astype(jnp.bfloat16),
        "mlp",
        scatter_dimension=0,
        tiled=True,
    ).astype(jnp.float32)
    stream = (stream.astype(jnp.float32) + gate_mod[None] * branch_out).astype(jnp.bfloat16)
    final_lo = 3 * LAYERS * model_width
    final_shift = modulation[:, final_lo : final_lo + model_width]
    final_scale = modulation[:, final_lo + model_width : final_lo + 2 * model_width]
    final_normed = (
        layer_norm(stream.astype(jnp.float32)) * (1.0 + final_scale[None]) + final_shift[None]
    ).astype(jnp.bfloat16)
    own_first = (tok_index * mlp_count + mlp_index) * rows_dev
    own_tokens = lax.dynamic_slice_in_dim(slot_token, own_first, rows_dev, 1).T
    half_velocity = jnp.einsum(
        "rpd,dc->rpc", final_normed, w_final, preferred_element_type=jnp.float32
    )
    half_velocity = jnp.where((own_tokens >= TXT)[:, :, None], half_velocity, 0.0)
    return guided(half_velocity, half_index, latents, step_index, guidance) + (stream[None],)


VMEM_BYTES = 56 * 1024 * 1024
TILE = 512
SLOTS = 3
ANY = pl.BlockSpec(memory_space=pl.ANY)
VMEM = pl.BlockSpec(memory_space=pltpu.VMEM)
SMEM = pl.BlockSpec(memory_space=pltpu.SMEM)


def kernel_params():
    return pltpu.CompilerParams(vmem_limit_bytes=VMEM_BYTES)


def flip_by_bit(values, axis, bit):
    return jnp.where(bit, jnp.flip(values, axis), values)


def from_xor_order(values, axis, index, bits):
    shape = values.shape
    split = shape[:axis] + (2,) * bits + shape[axis + 1 :]
    values = values.reshape(split)
    for place in range(bits):
        bit = (index >> (bits - 1 - place)) & 1
        values = flip_by_bit(values, axis + place, bit == 1)
    return values.reshape(shape)


def xor_rows(count, index):
    places = jnp.arange(count)
    return (places[:, None] ^ index) == places[None, :]


def pick_kernel(place_ref, *refs):
    count = len(refs) // 2
    for j in range(count):
        refs[count + j][...] = refs[j][0]


def pick(place, states):
    count, rows, width = states.shape
    take = lambda j: lambda i, s: (s[0] ^ j, i, 0)
    return pl.pallas_call(
        pick_kernel,
        out_shape=(jax.ShapeDtypeStruct((rows, width), states.dtype),) * count,
        grid_spec=pltpu.PrefetchScalarGridSpec(
            num_scalar_prefetch=1,
            grid=(2,),
            in_specs=[pl.BlockSpec((1, rows // 2, width), take(j)) for j in range(count)],
            out_specs=[pl.BlockSpec((rows // 2, width), lambda i, s: (i, 0))] * count,
        ),
        compiler_params=kernel_params(),
        cost_estimate=pl.CostEstimate(flops=0, bytes_accessed=4 * states.size, transcendentals=0),
        name="pick",
    )(place, *([states] * count))


def tables_kernel(place_ref, len_ref, tokens, freqs, cosine, sine, bias):
    tok, mlp = place_ref[0], place_ref[1]
    own_len = len_ref[tok].astype(jnp.float32)
    blocks, rows = bias.shape
    wide = tokens.shape[1]
    odd = (lax.broadcasted_iota(jnp.int32, (rows, wide), 1) & 1) == 1

    @pl.loop(0, blocks)
    def _(index):
        source = tok * blocks + (tok ^ (index >> 2)) * 4 + (mlp ^ (index & 3))
        token = tokens[pl.ds(source, 1), :].astype(jnp.float32)
        seen = (token >= TXT) | (token < own_len)
        bias[pl.ds(index, 1), :] = jnp.where(seen, 0.0, -1e30)[:, :rows]
        place = jnp.where(token >= TXT, token - TXT, 0.0)
        row = jnp.floor(place * (1.0 / SIDE))
        down = lambda values: jnp.transpose(jnp.broadcast_to(values, (wide, wide)))[:rows]
        angles = down(row) * freqs[0:1, :] + down(place - row * SIDE) * freqs[1:2, :]
        to = pl.ds(pl.multiple_of(index * rows, 16), rows)
        cosine[to, :] = jnp.cos(angles)
        turned = jnp.sin(angles)
        sine[to, :] = jnp.where(odd, turned, -turned)


def tables(place, text_len, tokens, head):
    blocks, rows = tokens.shape[0] // text_len.shape[0], tokens.shape[1]
    first, count = head // 16, (head - head // 8) // 4
    pair = np.arange(head) // 2
    rates = [
        np.where(
            (pair >= lo) & (pair < lo + count), np.exp(-math.log(ROPE_BASE) * (pair - lo) / count), 0.0
        )
        for lo in (first, first + count)
    ]
    freqs = jnp.asarray(np.stack(rates).astype(np.float32))
    table = jax.ShapeDtypeStruct((blocks * rows, head), jnp.float32)
    return pl.pallas_call(
        tables_kernel,
        out_shape=(table, table, jax.ShapeDtypeStruct((blocks, rows), jnp.float32)),
        in_specs=[SMEM, SMEM, VMEM, VMEM],
        compiler_params=kernel_params(),
        cost_estimate=pl.CostEstimate(
            flops=100 * blocks * rows * head,
            bytes_accessed=8 * blocks * rows * head,
            transcendentals=2 * blocks * rows * head,
        ),
        name="tables",
    )(place, text_len, jnp.pad(tokens, ((0, 0), (0, head - rows))), freqs)


def project_kernel(
    half_ref,
    shift,
    scale,
    cos_ref,
    sin_ref,
    gain,
    x0,
    x1,
    x2,
    x3,
    wq_own,
    wq_other,
    wu_own,
    wu_other,
    q_out,
    k_out,
    v_out,
    act_out,
    landed,
    normed,
    held,
    ready,
    x_sem,
    w_sem,
    out_sem,
):
    half = half_ref[0]
    depth = wu_own.shape[0]
    head = gain.shape[1]
    pieces = (x0, x1, x2, x3)
    rows = x0.shape[0]
    units = wu_own.shape[1] // TILE

    def weights(column, slot):
        return [
            pltpu.make_async_copy(
                ref.at[:, pl.ds(column, TILE)], held.at[slot, side], w_sem.at[slot, side]
            )
            for side, ref in enumerate((wu_own, wu_other))
        ]

    def head_weights(part):
        return [
            pltpu.make_async_copy(ref.at[part], held.at[part, side], w_sem.at[part, side])
            for side, ref in enumerate((wq_own, wq_other))
        ]

    def result(out, column, slot):
        return pltpu.make_async_copy(
            ready.at[slot], out.at[:, pl.ds(column, TILE)], out_sem.at[slot]
        )

    loads = [pltpu.make_async_copy(ref, landed.at[i], x_sem.at[i]) for i, ref in enumerate(pieces)]
    loads[0].start()
    for copy in head_weights(0):
        copy.start()
    for load in loads[1:]:
        load.start()
    for part in (1, 2):
        for copy in head_weights(part):
            copy.start()

    for index, load in enumerate(loads):
        load.wait()
        block = layer_norm(landed[index].astype(jnp.float32))
        block = (block * scale[...] + shift[...]).astype(jnp.bfloat16)
        normed[0, index * rows : (index + 1) * rows, :] = block[:, :depth]
        normed[1, index * rows : (index + 1) * rows, :] = block[:, depth:]

    even = (lax.broadcasted_iota(jnp.int32, cos_ref.shape, 1) & 1) == 0

    def product(slot):
        return jnp.dot(
            normed[half], held[slot, 0], preferred_element_type=jnp.float32
        ) + jnp.dot(normed[1 - half], held[slot, 1], preferred_element_type=jnp.float32)

    for part, out in enumerate((q_out, k_out, v_out)):
        for copy in head_weights(part):
            copy.wait()
        values = product(part)
        if part == 2:
            result(out, 0, 0).wait()
            ready[0] = values.astype(jnp.bfloat16)
        else:
            for lo in range(0, TILE, head):
                turned = rms_norm(values[:, lo : lo + head], gain[part : part + 1, :])
                partner = jnp.where(even, pltpu.roll(turned, head - 1, 1), pltpu.roll(turned, 1, 1))
                turned = turned * cos_ref[...] + partner * sin_ref[...]
                ready[part, :, lo : lo + head] = turned.astype(jnp.bfloat16)
        result(out, 0, part % 2).start()
        for copy in weights(part * TILE, part):
            copy.start()

    @pl.loop(0, units)
    def _(index):
        slot = lax.rem(index, SLOTS)
        to = lax.rem(index + 1, 2)
        column = pl.multiple_of(index * TILE, TILE)
        for copy in weights(column, slot):
            copy.wait()
        values = jax.nn.gelu(product(slot), approximate=True).astype(jnp.bfloat16)
        result(act_out, column, to).wait()
        ready[to] = values
        result(act_out, column, to).start()

        @pl.when(index + SLOTS < units)
        def _():
            later = pl.multiple_of((index + SLOTS) * TILE, TILE)
            for copy in weights(later, slot):
                copy.start()

    for slot in range(2):
        result(act_out, 0, slot).wait()


def project(half, pieces, shift, scale, cos_rows, sin_rows, gain, wq_own, wq_other, wu_own, wu_other):
    rows = sum(piece.shape[0] for piece in pieces)
    width = pieces[0].shape[1]
    depth = wu_own.shape[0]
    units = wu_own.shape[1]
    head_out = jax.ShapeDtypeStruct((rows, TILE), jnp.bfloat16)
    return pl.pallas_call(
        project_kernel,
        out_shape=(head_out, head_out, head_out, jax.ShapeDtypeStruct((rows, units), jnp.bfloat16)),
        in_specs=[SMEM] + [VMEM] * 5 + [ANY] * 8,
        out_specs=[ANY] * 4,
        scratch_shapes=[
            pltpu.VMEM((len(pieces), rows // len(pieces), width), jnp.bfloat16),
            pltpu.VMEM((2, rows, depth), jnp.bfloat16),
            pltpu.VMEM((SLOTS, 2, depth, TILE), jnp.bfloat16),
            pltpu.VMEM((2, rows, TILE), jnp.bfloat16),
            pltpu.SemaphoreType.DMA((len(pieces),)),
            pltpu.SemaphoreType.DMA((SLOTS, 2)),
            pltpu.SemaphoreType.DMA((2,)),
        ],
        compiler_params=kernel_params(),
        cost_estimate=pl.CostEstimate(
            flops=2 * rows * width * (3 * TILE + units),
            bytes_accessed=2 * width * (3 * TILE + units) + 2 * rows * (width + 3 * TILE + units),
            transcendentals=rows * units,
        ),
        name="project",
    )(half, shift, scale, cos_rows, sin_rows, gain, *pieces, wq_own, wq_other, wu_own, wu_other)


def combine_kernel(
    half_ref,
    bias,
    q,
    k0,
    k1,
    k2,
    k3,
    v0,
    v1,
    v2,
    v3,
    act,
    wa_own,
    wa_other,
    wm_own,
    wm_other,
    p0,
    p1,
    p2,
    p3,
    attended,
    units,
    held_a,
    held_m,
    ready,
    act_sem,
    w_sem,
    out_sem,
):
    half = half_ref[0]
    keys, values, outs = (k0, k1, k2, k3), (v0, v1, v2, v3), (p0, p1, p2, p3)
    rows = q.shape[0]
    size = k0.shape[0]
    piece = p0.shape[0]
    head = 128
    steps = wa_own.shape[1] // TILE

    def weights(wa, wm, column, slot):
        return [
            pltpu.make_async_copy(wa.at[:, pl.ds(column, TILE)], held_a.at[slot], w_sem.at[slot, 0]),
            pltpu.make_async_copy(wm.at[:, pl.ds(column, TILE)], held_m.at[slot], w_sem.at[slot, 1]),
        ]

    def results(column, slot):
        return [
            pltpu.make_async_copy(
                ready.at[slot, pl.ds(i * piece, piece)],
                out.at[:, pl.ds(column, TILE)],
                out_sem.at[slot, i],
            )
            for i, out in enumerate(outs)
        ]

    load = pltpu.make_async_copy(act, units, act_sem)
    load.start()
    for slot in range(SLOTS):
        for copy in weights(wa_own, wm_own, slot * TILE, slot):
            copy.start()

    @pl.loop(0, q.shape[1] // head)
    def _(index):
        lanes = pl.ds(pl.multiple_of(index * head, head), head)
        total = jnp.zeros((rows, 1), jnp.float32)
        numerator = jnp.zeros((rows, head), jnp.float32)
        for part in range(len(keys)):
            scores = lax.dot_general(
                q[:, lanes],
                keys[part][:, lanes],
                (((1,), (1,)), ((), ())),
                preferred_element_type=jnp.float32,
            )
            soft = jnp.exp(
                scores * (1.0 / math.sqrt(head)) + bias[:, part * size : (part + 1) * size]
            )
            total += jnp.sum(soft, axis=-1, keepdims=True)
            numerator += jnp.dot(
                soft.astype(jnp.bfloat16), values[part][:, lanes], preferred_element_type=jnp.float32
            )
        attended[:, lanes] = (numerator / total).astype(jnp.bfloat16)

    load.wait()

    def write(index, slot, column, first, wa, wm):
        for copy in weights(wa, wm, 0, slot):
            copy.wait()
        partial = jnp.dot(attended[...], held_a[slot], preferred_element_type=jnp.float32)
        partial += jnp.dot(units[...], held_m[slot], preferred_element_type=jnp.float32)
        to = lax.rem(index, 2)

        @pl.when(index >= 2)
        def _():
            for copy in results(0, to):
                copy.wait()

        ready[to] = partial.astype(jnp.bfloat16)
        for copy in results(column, to):
            copy.start()

    @pl.loop(0, 2 * steps)
    def _(index):
        slot = lax.rem(index, SLOTS)
        place = lax.rem(index + steps * half, 2 * steps)
        write(index, slot, pl.multiple_of(place * TILE, TILE), 0, wa_own, wm_own)

        @pl.when(index + SLOTS < 2 * steps)
        def _():
            later = pl.multiple_of((index + SLOTS - steps) * TILE, TILE)
            for copy in weights(wa_other, wm_other, later, slot):
                copy.start()

    for slot in range(2):
        for copy in results(0, slot):
            copy.wait()


def combine(half, bias, q, keys, values, act, wa_own, wa_other, wm_own, wm_other):
    rows, heads = q.shape
    units = act.shape[1]
    slots = bias.shape[1]
    half_cols = wa_own.shape[1]
    assert half_cols == SLOTS * TILE
    pieces = len(keys)
    part = jax.ShapeDtypeStruct((rows // pieces, 2 * half_cols), jnp.bfloat16)
    return pl.pallas_call(
        combine_kernel,
        out_shape=(part,) * pieces,
        in_specs=[SMEM] + [VMEM] * (2 + 2 * pieces) + [ANY] * 5,
        out_specs=[ANY] * pieces,
        scratch_shapes=[
            pltpu.VMEM((rows, heads), jnp.bfloat16),
            pltpu.VMEM((rows, units), jnp.bfloat16),
            pltpu.VMEM((SLOTS, heads, TILE), jnp.bfloat16),
            pltpu.VMEM((SLOTS, units, TILE), jnp.bfloat16),
            pltpu.VMEM((2, rows, TILE), jnp.bfloat16),
            pltpu.SemaphoreType.DMA,
            pltpu.SemaphoreType.DMA((SLOTS, 2)),
            pltpu.SemaphoreType.DMA((2, pieces)),
        ],
        compiler_params=kernel_params(),
        cost_estimate=pl.CostEstimate(
            flops=4 * rows * (heads + units) * half_cols + 4 * rows * slots * heads,
            bytes_accessed=4 * (heads + units) * half_cols + 2 * rows * (heads + units + 2 * half_cols),
            transcendentals=rows * slots * heads // 128,
        ),
        name="combine",
    )(half, bias, q, *keys, *values, act, wa_own, wa_other, wm_own, wm_other)


def finish_kernel(*refs, terms, packed):
    parts, refs = refs[: 1 + terms], refs[1 + terms :]
    states, gate, shift, scale, w_final, *outs = refs
    branch = parts[0][...].astype(jnp.float32)
    for part in parts[1:]:
        branch = branch + part[...].astype(jnp.float32)
    stream = (states[...].astype(jnp.float32) + gate[...] * branch).astype(jnp.bfloat16)
    normed = (layer_norm(stream.astype(jnp.float32)) * scale[...] + shift[...]).astype(jnp.bfloat16)
    speed = lax.dot_general(
        normed, w_final[...], (((1,), (1,)), ((), ())), preferred_element_type=jnp.float32
    )
    width = stream.shape[1]
    outs[0][:, :width] = stream
    if packed:
        high = speed.astype(jnp.bfloat16)
        low = (speed - high.astype(jnp.float32)).astype(jnp.bfloat16)
        outs[0][:, width:] = jnp.concatenate([high, low], 1)
    else:
        outs[1][...] = speed


def finish(parts, states, gate, shift, scale, w_final, packed):
    rows, width = states.shape
    channels = w_final.shape[0]
    steps = 2
    by_rows = lambda cols: pl.BlockSpec((rows // steps, cols), lambda i: (i, 0))
    whole = lambda array: pl.BlockSpec(array.shape, lambda i: (0, 0))
    if packed:
        out_shape = (jax.ShapeDtypeStruct((rows, width + 2 * channels), jnp.bfloat16),)
    else:
        out_shape = (
            jax.ShapeDtypeStruct((rows, width), jnp.bfloat16),
            jax.ShapeDtypeStruct((rows, channels), jnp.float32),
        )
    return pl.pallas_call(
        functools.partial(finish_kernel, terms=len(parts) - 1, packed=packed),
        out_shape=out_shape,
        grid=(steps,),
        in_specs=[by_rows(width)] * (len(parts) + 1) + [whole(a) for a in (gate, shift, scale, w_final)],
        out_specs=[by_rows(out.shape[1]) for out in out_shape],
        compiler_params=kernel_params(),
        cost_estimate=pl.CostEstimate(
            flops=2 * states.size * channels,
            bytes_accessed=2 * states.size * (len(parts) + 2),
            transcendentals=0,
        ),
        name="finish",
    )(*parts, states, gate, shift, scale, w_final)


def add(left, right):
    return (left.astype(jnp.float32) + right.astype(jnp.float32)).astype(jnp.bfloat16)


def after(values, *done):
    return lax.optimization_barrier((values, *done))[0]


def by_prompt(
    hidden,
    latents,
    vec,
    slot_token,
    text_len,
    step_index,
    guidance,
    w_mod,
    w_qkv,
    w_mlp_in,
    qk_gain,
    w_attn_out,
    w_mlp_out,
    w_final,
):
    rows_dev, prompts, model_width = hidden.shape[1:]
    head_size = qk_gain.shape[-1]
    tok_index = lax.axis_index("tok")
    mlp_index = lax.axis_index("mlp")
    half_index = lax.axis_index("cfg")
    half = half_index[None].astype(jnp.int32)

    sends = pick(tok_index[None].astype(jnp.int32), jnp.transpose(hidden[0], (1, 0, 2)))

    silu_vec = jax.nn.silu(vec[0]).astype(jnp.bfloat16)
    silu_vec = jnp.dot(
        xor_rows(prompts, tok_index).astype(jnp.bfloat16), after(silu_vec, sends[0])
    ).astype(jnp.bfloat16)
    mod_part = jnp.dot(silu_vec, w_mod, preferred_element_type=jnp.float32)

    cosine, sine_table, bias = tables(
        jnp.stack([tok_index, mlp_index]).astype(jnp.int32),
        text_len[0],
        after(slot_token, mod_part).reshape(-1, rows_dev),
        head_size,
    )
    cosine = cosine.reshape(prompts, 4 * rows_dev, head_size)
    sine_table = sine_table.reshape(cosine.shape)
    bias = bias.reshape(1, -1)

    wq_own = jnp.transpose(w_qkv[0], (1, 0, 2))
    wu_own, wa_own, wm_own = w_mlp_in[0], w_attn_out[0], w_mlp_out[0]
    wq_other = xor_swap(wq_own, "cfg", 1)
    wu_other = xor_swap(after(wu_own, wq_other), "cfg", 1)
    gain = qk_gain[0]

    states_0, states_1 = sends[0], xor_swap(sends[1], "tok", 1)
    by_x, by_y = xor_swap(states_0, "mlp", 1), xor_swap(states_0, "mlp", 2)
    order = xor_rows(4 * prompts, 4 * tok_index + mlp_index)
    mods = jnp.stack([mod_part[0::2], xor_swap(mod_part[1::2], "tok", 1)], 1)
    mods = jnp.concatenate([mods[0], xor_swap(after(mods[1], cosine, wq_other), "tok", 2)], 0)
    mods = jnp.stack([mods, xor_swap(after(mods, by_x, by_y, states_1), "mlp", 1)], 1)
    cut = rows_dev // 2
    far_top, far_low = xor_swap(by_x[:cut], "mlp", 2), xor_swap(by_y[cut:], "mlp", 1)
    mods = jnp.concatenate([mods, xor_swap(after(mods, far_top, far_low), "mlp", 2)], 1)
    mods = jnp.dot(
        order.astype(jnp.float32), mods.reshape(order.shape[0], -1), precision=lax.Precision.HIGHEST
    )
    shift_mod, scale_mod, gate_mod, final_shift, final_scale = jnp.split(
        mods.reshape(1, 5 * model_width), 5, 1
    )
    scale_mod = 1.0 + scale_mod
    final_scale = 1.0 + final_scale
    wm_other = xor_swap(after(wm_own, shift_mod), "cfg", 1)
    wa_other = xor_swap(after(wa_own, wm_other), "cfg", 1)

    own, queries, keys, values, acts = [], [], [], [], []
    done = (far_top, far_low, shift_mod)
    for j in range(prompts):
        if j == 0:
            states, far = states_0, jnp.concatenate([far_top, far_low], 0)
        else:
            states = states_1 if j == 1 else xor_swap(after(sends[j], own[-1], *queries[: j - 2]), "tok", j)
            send = after(states, *done)
            by_x, by_y, far = [xor_swap(send, "mlp", k) for k in (1, 2, 3)]
        own.append(states)
        q, k, v, act = project(
            half,
            (states, by_x, by_y, far),
            shift_mod,
            scale_mod,
            cosine[j],
            sine_table[j],
            gain,
            wq_own,
            wq_other,
            wu_own,
            wu_other,
        )
        queries.append(q)
        keys.append(k)
        values.append(v)
        acts.append(act)
        if j:
            done = (queries[j - 1], by_x, by_y, far, wm_other if j == 1 else wa_other)

    streams, speeds, marks, parts = ([None] * prompts for _ in range(4))

    def straight(j):
        p0, p1, p2, p3 = parts[j]
        parts[j] = (p0, [xor_swap(p, "mlp", k) for k, p in ((1, p1), (2, p2), (3, p3))])

    def first_step(j, *done):
        p0, p1, p2, p3 = parts[j]
        p3 = after(p3, *done)
        if j == 0:
            top, low = xor_swap(p3[:cut], "mlp", 1), xor_swap(p3[cut:], "mlp", 2)
        elif j % 2:
            top, low = xor_swap(p3, "mlp", 1), None
        else:
            top, low = None, xor_swap(p3, "mlp", 2)
        parts[j] = (p0, p1, p2, top, low)

    def second_step(j, *done):
        p0, p1, p2, top, low = parts[j]
        if j == 0:
            low = after(low, *done)
            p1 = jnp.concatenate([p1[:cut], add(p1[cut:], low)], 0)
            p2 = jnp.concatenate([add(p2[:cut], top), p2[cut:]], 0)
        elif j % 2:
            p2 = add(p2, after(top, *done))
        else:
            p1 = add(p1, after(low, *done))
        parts[j] = (p0, [xor_swap(p1, "mlp", 1), xor_swap(p2, "mlp", 2)])
        return p2 if j % 2 else p1

    def sum_up(j, *done):
        p0, terms = parts[j]
        outs = finish(
            [after(p0, *done), *terms],
            own[j],
            gate_mod,
            final_shift,
            final_scale,
            w_final.T,
            packed=j > 0,
        )
        marks[j] = outs[0]
        if j:
            gone = xor_swap(outs[0], "tok", j)
            streams[j] = gone[:, :model_width]
            high, low = jnp.split(gone[:, model_width:].astype(jnp.float32), 2, 1)
            speeds[j] = high + low
        else:
            streams[j], speeds[j] = outs

    done = ()
    for j in reversed(range(prompts)):
        parts[j] = combine(
            half,
            bias,
            after(queries[j], *done),
            keys,
            values,
            acts[j],
            wa_own,
            wa_other,
            wm_own,
            wm_other,
        )
        mark, done = parts[j][0], ()
        if j + 1 == prompts:
            straight(j)
        elif j + 2 == prompts:
            first_step(j)
        else:
            sent = second_step(j + 1, mark)
            first_step(j, sent)
            sum_up(j + 2, sent)
            done = (marks[j + 2],)
    sum_up(1, marks[2])
    second_step(0, marks[2])
    sum_up(0, marks[1])

    stream = from_xor_order(jnp.stack(streams, 1), 1, tok_index, 2)
    half_velocity = from_xor_order(jnp.stack(speeds, 1), 1, tok_index, 2)
    own_first = (tok_index * 4 + mlp_index) * rows_dev
    own_tokens = lax.dynamic_slice_in_dim(slot_token, own_first, rows_dev, 1).T
    half_velocity = jnp.where((own_tokens >= TXT)[:, :, None], half_velocity, 0.0)
    return guided(half_velocity, half_index, latents, step_index, guidance) + (stream[None],)


def guided(half_velocity, half_index, latents, step_index, guidance):
    channel_half = latents.shape[2]
    own_part = lax.dynamic_slice_in_dim(half_velocity, half_index * channel_half, channel_half, 2)
    sent_part = lax.dynamic_slice_in_dim(
        half_velocity, (1 - half_index) * channel_half, channel_half, 2
    )
    partner = xor_swap(sent_part, "cfg", 1)
    first_half = half_index == 0
    cond_part = jnp.where(first_half, own_part, partner)
    uncond_part = jnp.where(first_half, partner, own_part)
    velocity = uncond_part + guidance[0] * (cond_part - uncond_part)
    current = step_index[0].astype(jnp.float32)
    step_size = sigma_at(current + 1.0, STEPS) - sigma_at(current, STEPS)
    return (velocity, latents + step_size * velocity)


def fits_by_prompt(mesh):
    return mesh.shape["cfg"] == 2 and mesh.shape["tok"] == PROMPTS and mesh.shape["mlp"] == 4


def solution(mesh):
    return jax.shard_map(
        by_prompt if fits_by_prompt(mesh) else on_device,
        mesh=mesh,
        in_specs=(
            P("cfg", ("tok", "mlp"), None, None),
            P(("tok", "mlp"), None, "cfg"),
            P("cfg", None, None),
            P(),
            P("cfg", None),
            P(),
            P(),
            P(None, ("tok", "mlp")),
            P(None, "cfg", None, "mlp"),
            P(None, "cfg", "mlp"),
            P(),
            P(None, "mlp", "cfg"),
            P(None, "mlp", "cfg"),
            P(),
        ),
        out_specs=(
            P(("tok", "mlp"), None, "cfg"),
            P(("tok", "mlp"), None, "cfg"),
            P("cfg", ("tok", "mlp"), None, None),
        ),
        check_vma=False,
    )
```

```python
import functools
import math

import jax
import jax.numpy as jnp
import numpy as np
from jax import lax
from jax.experimental import pallas as pl
from jax.experimental.pallas import tpu as pltpu
from jax.sharding import PartitionSpec as P

LAYERS = 1
SIDE = 32
TXT = 512
STEPS = 28
PROMPTS = 4


EPSILON = 1e-06
ROPE_BASE = 10000.0
TIME_SHIFT = 3.0


def xor_swap(value, axis, apart):
    return lax.ppermute(value, axis, [(i, i ^ apart) for i in range(lax.axis_size(axis))])


def layer_norm(values):
    average = jnp.mean(values, axis=-1, keepdims=True)
    centred = values - average
    spread = jnp.mean(centred * centred, axis=-1, keepdims=True)
    return centred * lax.rsqrt(spread + EPSILON)


def rms_norm(values, gains):
    return values * lax.rsqrt(jnp.mean(values * values, axis=-1, keepdims=True) + EPSILON) * gains


def rope_table(tokens, head_size, text_count, side_count):
    pair_count = head_size // 2
    first_pairs = head_size // 16
    axis_pairs = (head_size - head_size // 8) // 4
    pair_index = jnp.arange(pair_count).astype(jnp.float32)
    in_rows = (pair_index >= first_pairs) & (pair_index < first_pairs + axis_pairs)
    in_cols = pair_index >= first_pairs + axis_pairs
    log_base = math.log(ROPE_BASE)
    freq_rows = jnp.where(
        in_rows, jnp.exp(-log_base * (pair_index - first_pairs) / axis_pairs), 0.0
    )
    freq_cols = jnp.where(
        in_cols, jnp.exp(-log_base * (pair_index - first_pairs - axis_pairs) / axis_pairs), 0.0
    )
    is_image = tokens >= text_count
    image_pos = jnp.where(is_image, tokens - text_count, 0)
    row_pos = (image_pos // side_count).astype(jnp.float32)
    col_pos = (image_pos % side_count).astype(jnp.float32)
    angles = row_pos[..., None] * freq_rows + col_pos[..., None] * freq_cols
    return (jnp.cos(angles), jnp.sin(angles))


def apply_rope(values, cosine, sine_table):
    even_part = values[..., 0::2]
    odd_part = values[..., 1::2]
    return jnp.concatenate(
        [even_part * cosine - odd_part * sine_table, even_part * sine_table + odd_part * cosine],
        axis=-1,
    )


def sigma_at(position, steps_total):
    remain = 1.0 - position / steps_total
    return TIME_SHIFT * remain / (1.0 + (TIME_SHIFT - 1.0) * remain)


def on_device(
    hidden,
    latents,
    vec,
    slot_token,
    text_len,
    step_index,
    guidance,
    w_mod,
    w_qkv,
    w_mlp_in,
    qk_gain,
    w_attn_out,
    w_mlp_out,
    w_final,
):
    rows_dev = hidden.shape[1]
    prompts = hidden.shape[2]
    model_width = hidden.shape[3]
    head_size = qk_gain.shape[-1]
    mlp_count = lax.axis_size("mlp")
    tile_rows = rows_dev * mlp_count
    tok_index = lax.axis_index("tok")
    mlp_index = lax.axis_index("mlp")
    half_index = lax.axis_index("cfg")
    stream = hidden[0]
    silu_vec = jax.nn.silu(vec[0]).astype(jnp.bfloat16)
    mod_part = jnp.dot(silu_vec, w_mod, preferred_element_type=jnp.float32)
    modulation = lax.all_gather(mod_part, ("tok", "mlp"), axis=1, tiled=True)
    key_valid = ((slot_token >= TXT) | (slot_token < text_len[0][:, None])).astype(jnp.float32)
    tile_tokens = lax.dynamic_slice_in_dim(slot_token, tok_index * tile_rows, tile_rows, 1).T
    cosine, sine_table = rope_table(tile_tokens, head_size, TXT, SIDE)
    shift_mod = modulation[:, 0:model_width]
    scale_mod = modulation[:, model_width : 2 * model_width]
    gate_mod = modulation[:, 2 * model_width : 3 * model_width]
    normed = (
        layer_norm(stream.astype(jnp.float32)) * (1.0 + scale_mod[None]) + shift_mod[None]
    ).astype(jnp.bfloat16)
    tile_input = lax.all_gather(normed, "mlp", axis=0, tiled=True)
    qkv_weight = w_qkv[0]
    unit_weight = w_mlp_in[0]
    qkv_cols = qkv_weight.shape[1] * qkv_weight.shape[2]
    pieces = (
        lax.all_gather(qkv_weight, "cfg", axis=0, tiled=True),
        lax.all_gather(unit_weight, "cfg", axis=0, tiled=True),
    )
    number = pieces[0].shape[0]
    qkv_piece = pieces[0].reshape(number, qkv_cols)
    qkv_pre = jnp.einsum("tpd,dk->tpk", tile_input, qkv_piece, preferred_element_type=jnp.float32)
    unit_pre = jnp.einsum("tpd,dk->tpk", tile_input, pieces[1], preferred_element_type=jnp.float32)
    heads_dev = qkv_weight.shape[2] // head_size
    projected = qkv_pre.reshape(tile_rows, prompts, 3, heads_dev, head_size)
    queries = apply_rope(
        rms_norm(projected[:, :, 0], qk_gain[0, 0]), cosine[:, :, None], sine_table[:, :, None]
    ).astype(jnp.bfloat16)
    keys_rot = apply_rope(
        rms_norm(projected[:, :, 1], qk_gain[0, 1]), cosine[:, :, None], sine_table[:, :, None]
    ).astype(jnp.bfloat16)
    values = projected[:, :, 2].astype(jnp.bfloat16)
    activation = jax.nn.gelu(unit_pre, approximate=True).astype(jnp.bfloat16)
    keys_piece = lax.all_gather(keys_rot, "tok", axis=0, tiled=True)
    values_piece = lax.all_gather(values, "tok", axis=0, tiled=True)
    scores = jnp.einsum(
        "sphe,tphe->phst", queries, keys_piece, preferred_element_type=jnp.float32
    ) / math.sqrt(head_size)
    softened = jnp.exp(scores) * key_valid[:, None, None, :]
    numerator = jnp.einsum(
        "phst,tphe->sphe",
        softened.astype(jnp.bfloat16),
        values_piece,
        preferred_element_type=jnp.float32,
    )
    numerator, denominator = (numerator, jnp.sum(softened, axis=-1))
    attended = (numerator / jnp.transpose(denominator, (2, 0, 1))[..., None]).astype(jnp.bfloat16)
    attended = attended.reshape(tile_rows, prompts, heads_dev * head_size)
    out_attn = lax.all_gather(w_attn_out[0], "cfg", axis=1, tiled=True)
    out_units = lax.all_gather(w_mlp_out[0], "cfg", axis=1, tiled=True)
    branch_out = lax.psum_scatter(
        (
            jnp.einsum("tpk,kd->tpd", attended, out_attn, preferred_element_type=jnp.float32)
            + jnp.einsum("tpk,kd->tpd", activation, out_units, preferred_element_type=jnp.float32)
        ).astype(jnp.bfloat16),
        "mlp",
        scatter_dimension=0,
        tiled=True,
    ).astype(jnp.float32)
    stream = (stream.astype(jnp.float32) + gate_mod[None] * branch_out).astype(jnp.bfloat16)
    final_lo = 3 * LAYERS * model_width
    final_shift = modulation[:, final_lo : final_lo + model_width]
    final_scale = modulation[:, final_lo + model_width : final_lo + 2 * model_width]
    final_normed = (
        layer_norm(stream.astype(jnp.float32)) * (1.0 + final_scale[None]) + final_shift[None]
    ).astype(jnp.bfloat16)
    own_first = (tok_index * mlp_count + mlp_index) * rows_dev
    own_tokens = lax.dynamic_slice_in_dim(slot_token, own_first, rows_dev, 1).T
    half_velocity = jnp.einsum(
        "rpd,dc->rpc", final_normed, w_final, preferred_element_type=jnp.float32
    )
    half_velocity = jnp.where((own_tokens >= TXT)[:, :, None], half_velocity, 0.0)
    return guided(half_velocity, half_index, latents, step_index, guidance) + (stream[None],)


VMEM_BYTES = 56 * 1024 * 1024
TILE = 512
SLOTS = 3
ANY = pl.BlockSpec(memory_space=pl.ANY)
VMEM = pl.BlockSpec(memory_space=pltpu.VMEM)
SMEM = pl.BlockSpec(memory_space=pltpu.SMEM)


def kernel_params():
    return pltpu.CompilerParams(vmem_limit_bytes=VMEM_BYTES)


def flip_by_bit(values, axis, bit):
    return jnp.where(bit, jnp.flip(values, axis), values)


def from_xor_order(values, axis, index, bits):
    shape = values.shape
    split = shape[:axis] + (2,) * bits + shape[axis + 1 :]
    values = values.reshape(split)
    for place in range(bits):
        bit = (index >> (bits - 1 - place)) & 1
        values = flip_by_bit(values, axis + place, bit == 1)
    return values.reshape(shape)


def xor_rows(count, index):
    places = jnp.arange(count)
    return (places[:, None] ^ index) == places[None, :]


def pick_kernel(place_ref, *refs):
    count = len(refs) // 2
    for j in range(count):
        refs[count + j][...] = refs[j][0]


def pick(place, states):
    count, rows, width = states.shape
    take = lambda j: lambda i, s: (s[0] ^ j, i, 0)
    return pl.pallas_call(
        pick_kernel,
        out_shape=(jax.ShapeDtypeStruct((rows, width), states.dtype),) * count,
        grid_spec=pltpu.PrefetchScalarGridSpec(
            num_scalar_prefetch=1,
            grid=(2,),
            in_specs=[pl.BlockSpec((1, rows // 2, width), take(j)) for j in range(count)],
            out_specs=[pl.BlockSpec((rows // 2, width), lambda i, s: (i, 0))] * count,
        ),
        compiler_params=kernel_params(),
        cost_estimate=pl.CostEstimate(flops=0, bytes_accessed=4 * states.size, transcendentals=0),
        name="pick",
    )(place, *([states] * count))


def tables_kernel(place_ref, len_ref, tokens, freqs, bias, *outs):
    tok, mlp = place_ref[0], place_ref[1]
    own_len = len_ref[tok].astype(jnp.float32)
    blocks, rows = bias.shape
    wide = tokens.shape[1]
    odd = (lax.broadcasted_iota(jnp.int32, (rows, wide), 1) & 1) == 1

    def block(cosine, sine, chunk, index):
        source = tok * blocks + (tok ^ chunk) * 4 + (mlp ^ index)
        token = tokens[pl.ds(source, 1), :].astype(jnp.float32)
        seen = (token >= TXT) | (token < own_len)
        bias[pl.ds(chunk * 4 + index, 1), :] = jnp.where(seen, 0.0, -1e30)[:, :rows]
        place = jnp.where(token >= TXT, token - TXT, 0.0)
        row = jnp.floor(place * (1.0 / SIDE))
        down = lambda values: jnp.transpose(jnp.broadcast_to(values, (wide, wide)))[:rows]
        angles = down(row) * freqs[0:1, :] + down(place - row * SIDE) * freqs[1:2, :]
        to = pl.ds(pl.multiple_of(index * rows, 16), rows)
        cosine[to, :] = jnp.cos(angles)
        turned = jnp.sin(angles)
        sine[to, :] = jnp.where(odd, turned, -turned)

    count = len(outs) // 2
    for chunk in range(count):
        pl.loop(0, 4)(functools.partial(block, outs[chunk], outs[count + chunk], chunk))


def tables(place, text_len, tokens, head):
    chunks = text_len.shape[0]
    blocks, rows = tokens.shape[0] // chunks, tokens.shape[1]
    first, count = head // 16, (head - head // 8) // 4
    pair = np.arange(head) // 2
    rates = [
        np.where(
            (pair >= lo) & (pair < lo + count), np.exp(-math.log(ROPE_BASE) * (pair - lo) / count), 0.0
        )
        for lo in (first, first + count)
    ]
    freqs = jnp.asarray(np.stack(rates).astype(np.float32))
    table = jax.ShapeDtypeStruct((4 * rows, head), jnp.float32)
    bias, *outs = pl.pallas_call(
        tables_kernel,
        out_shape=(jax.ShapeDtypeStruct((blocks, rows), jnp.float32),) + (table,) * (2 * chunks),
        in_specs=[SMEM, SMEM, VMEM, VMEM],
        compiler_params=kernel_params(),
        cost_estimate=pl.CostEstimate(
            flops=100 * blocks * rows * head,
            bytes_accessed=8 * blocks * rows * head,
            transcendentals=2 * blocks * rows * head,
        ),
        name="tables",
    )(place, text_len, jnp.pad(tokens, ((0, 0), (0, head - rows))), freqs)
    return outs[:chunks], outs[chunks:], bias


def project_kernel(
    half_ref,
    shift,
    scale,
    cos_ref,
    sin_ref,
    gain,
    x0,
    x1,
    x2,
    x3,
    wq_own,
    wq_other,
    wu_own,
    wu_other,
    q_out,
    k_out,
    v_out,
    act_out,
    landed,
    normed,
    held,
    ready,
    x_sem,
    w_sem,
    out_sem,
):
    half = half_ref[0]
    depth = wu_own.shape[0]
    head = gain.shape[1]
    pieces = (x0, x1, x2, x3)
    rows = x0.shape[0]
    units = wu_own.shape[1] // TILE

    def weights(column, slot):
        return [
            pltpu.make_async_copy(
                ref.at[:, pl.ds(column, TILE)], held.at[slot, side], w_sem.at[slot, side]
            )
            for side, ref in enumerate((wu_own, wu_other))
        ]

    def head_weights(part):
        return [
            pltpu.make_async_copy(ref.at[part], held.at[part, side], w_sem.at[part, side])
            for side, ref in enumerate((wq_own, wq_other))
        ]

    def result(out, column, slot):
        return pltpu.make_async_copy(
            ready.at[slot], out.at[:, pl.ds(column, TILE)], out_sem.at[slot]
        )

    loads = [pltpu.make_async_copy(ref, landed.at[i], x_sem.at[i]) for i, ref in enumerate(pieces)]
    loads[0].start()
    for copy in head_weights(0):
        copy.start()
    for load in loads[1:]:
        load.start()
    for part in (1, 2):
        for copy in head_weights(part):
            copy.start()

    for index, load in enumerate(loads):
        load.wait()
        block = layer_norm(landed[index].astype(jnp.float32))
        block = (block * scale[...] + shift[...]).astype(jnp.bfloat16)
        normed[0, index * rows : (index + 1) * rows, :] = block[:, :depth]
        normed[1, index * rows : (index + 1) * rows, :] = block[:, depth:]

    even = (lax.broadcasted_iota(jnp.int32, cos_ref.shape, 1) & 1) == 0

    def product(slot):
        return jnp.dot(
            normed[half], held[slot, 0], preferred_element_type=jnp.float32
        ) + jnp.dot(normed[1 - half], held[slot, 1], preferred_element_type=jnp.float32)

    for part, out in enumerate((q_out, k_out, v_out)):
        for copy in head_weights(part):
            copy.wait()
        values = product(part)
        if part == 2:
            result(out, 0, 0).wait()
            ready[0] = values.astype(jnp.bfloat16)
        else:
            for lo in range(0, TILE, head):
                turned = rms_norm(values[:, lo : lo + head], gain[part : part + 1, :])
                partner = jnp.where(even, pltpu.roll(turned, head - 1, 1), pltpu.roll(turned, 1, 1))
                turned = turned * cos_ref[...] + partner * sin_ref[...]
                ready[part, :, lo : lo + head] = turned.astype(jnp.bfloat16)
        result(out, 0, part % 2).start()
        for copy in weights(part * TILE, part):
            copy.start()

    @pl.loop(0, units)
    def _(index):
        slot = lax.rem(index, SLOTS)
        to = lax.rem(index + 1, 2)
        column = pl.multiple_of(index * TILE, TILE)
        for copy in weights(column, slot):
            copy.wait()
        values = jax.nn.gelu(product(slot), approximate=True).astype(jnp.bfloat16)
        result(act_out, column, to).wait()
        ready[to] = values
        result(act_out, column, to).start()

        @pl.when(index + SLOTS < units)
        def _():
            later = pl.multiple_of((index + SLOTS) * TILE, TILE)
            for copy in weights(later, slot):
                copy.start()

    for slot in range(2):
        result(act_out, 0, slot).wait()


def project(half, pieces, shift, scale, cos_rows, sin_rows, gain, wq_own, wq_other, wu_own, wu_other):
    rows = sum(piece.shape[0] for piece in pieces)
    width = pieces[0].shape[1]
    depth = wu_own.shape[0]
    units = wu_own.shape[1]
    head_out = jax.ShapeDtypeStruct((rows, TILE), jnp.bfloat16)
    return pl.pallas_call(
        project_kernel,
        out_shape=(head_out, head_out, head_out, jax.ShapeDtypeStruct((rows, units), jnp.bfloat16)),
        in_specs=[SMEM] + [VMEM] * 5 + [ANY] * 8,
        out_specs=[ANY] * 4,
        scratch_shapes=[
            pltpu.VMEM((len(pieces), rows // len(pieces), width), jnp.bfloat16),
            pltpu.VMEM((2, rows, depth), jnp.bfloat16),
            pltpu.VMEM((SLOTS, 2, depth, TILE), jnp.bfloat16),
            pltpu.VMEM((2, rows, TILE), jnp.bfloat16),
            pltpu.SemaphoreType.DMA((len(pieces),)),
            pltpu.SemaphoreType.DMA((SLOTS, 2)),
            pltpu.SemaphoreType.DMA((2,)),
        ],
        compiler_params=kernel_params(),
        cost_estimate=pl.CostEstimate(
            flops=2 * rows * width * (3 * TILE + units),
            bytes_accessed=2 * width * (3 * TILE + units) + 2 * rows * (width + 3 * TILE + units),
            transcendentals=rows * units,
        ),
        name="project",
    )(half, shift, scale, cos_rows, sin_rows, gain, *pieces, wq_own, wq_other, wu_own, wu_other)


def combine_kernel(
    half_ref,
    bias,
    q,
    k0,
    k1,
    k2,
    k3,
    v0,
    v1,
    v2,
    v3,
    act,
    wa_own,
    wa_other,
    wm_own,
    wm_other,
    p0,
    p1,
    p2,
    p3,
    attended,
    units,
    held_a,
    held_m,
    ready,
    act_sem,
    w_sem,
    out_sem,
):
    half = half_ref[0]
    keys, values, outs = (k0, k1, k2, k3), (v0, v1, v2, v3), (p0, p1, p2, p3)
    rows = q.shape[0]
    size = k0.shape[0]
    piece = p0.shape[0]
    head = 128
    steps = wa_own.shape[1] // TILE

    def weights(wa, wm, column, slot):
        return [
            pltpu.make_async_copy(wa.at[:, pl.ds(column, TILE)], held_a.at[slot], w_sem.at[slot, 0]),
            pltpu.make_async_copy(wm.at[:, pl.ds(column, TILE)], held_m.at[slot], w_sem.at[slot, 1]),
        ]

    def results(column, slot):
        return [
            pltpu.make_async_copy(
                ready.at[slot, pl.ds(i * piece, piece)],
                out.at[:, pl.ds(column, TILE)],
                out_sem.at[slot, i],
            )
            for i, out in enumerate(outs)
        ]

    load = pltpu.make_async_copy(act, units, act_sem)
    load.start()
    for slot in range(SLOTS):
        for copy in weights(wa_own, wm_own, slot * TILE, slot):
            copy.start()

    @pl.loop(0, q.shape[1] // head)
    def _(index):
        lanes = pl.ds(pl.multiple_of(index * head, head), head)
        total = jnp.zeros((rows, 1), jnp.float32)
        numerator = jnp.zeros((rows, head), jnp.float32)
        for part in range(len(keys)):
            scores = lax.dot_general(
                q[:, lanes],
                keys[part][:, lanes],
                (((1,), (1,)), ((), ())),
                preferred_element_type=jnp.float32,
            )
            soft = jnp.exp(
                scores * (1.0 / math.sqrt(head)) + bias[:, part * size : (part + 1) * size]
            )
            total += jnp.sum(soft, axis=-1, keepdims=True)
            numerator += jnp.dot(
                soft.astype(jnp.bfloat16), values[part][:, lanes], preferred_element_type=jnp.float32
            )
        attended[:, lanes] = (numerator / total).astype(jnp.bfloat16)

    load.wait()

    def write(index, slot, column, first, wa, wm):
        for copy in weights(wa, wm, 0, slot):
            copy.wait()
        partial = jnp.dot(attended[...], held_a[slot], preferred_element_type=jnp.float32)
        partial += jnp.dot(units[...], held_m[slot], preferred_element_type=jnp.float32)
        to = lax.rem(index, 2)

        @pl.when(index >= 2)
        def _():
            for copy in results(0, to):
                copy.wait()

        ready[to] = partial.astype(jnp.bfloat16)
        for copy in results(column, to):
            copy.start()

    @pl.loop(0, 2 * steps)
    def _(index):
        slot = lax.rem(index, SLOTS)
        place = lax.rem(index + steps * half, 2 * steps)
        write(index, slot, pl.multiple_of(place * TILE, TILE), 0, wa_own, wm_own)

        @pl.when(index + SLOTS < 2 * steps)
        def _():
            later = pl.multiple_of((index + SLOTS - steps) * TILE, TILE)
            for copy in weights(wa_other, wm_other, later, slot):
                copy.start()

    for slot in range(2):
        for copy in results(0, slot):
            copy.wait()


def combine(half, bias, q, keys, values, act, wa_own, wa_other, wm_own, wm_other):
    rows, heads = q.shape
    units = act.shape[1]
    slots = bias.shape[1]
    half_cols = wa_own.shape[1]
    assert half_cols == SLOTS * TILE
    pieces = len(keys)
    part = jax.ShapeDtypeStruct((rows // pieces, 2 * half_cols), jnp.bfloat16)
    return pl.pallas_call(
        combine_kernel,
        out_shape=(part,) * pieces,
        in_specs=[SMEM] + [VMEM] * (2 + 2 * pieces) + [ANY] * 5,
        out_specs=[ANY] * pieces,
        scratch_shapes=[
            pltpu.VMEM((rows, heads), jnp.bfloat16),
            pltpu.VMEM((rows, units), jnp.bfloat16),
            pltpu.VMEM((SLOTS, heads, TILE), jnp.bfloat16),
            pltpu.VMEM((SLOTS, units, TILE), jnp.bfloat16),
            pltpu.VMEM((2, rows, TILE), jnp.bfloat16),
            pltpu.SemaphoreType.DMA,
            pltpu.SemaphoreType.DMA((SLOTS, 2)),
            pltpu.SemaphoreType.DMA((2, pieces)),
        ],
        compiler_params=kernel_params(),
        cost_estimate=pl.CostEstimate(
            flops=4 * rows * (heads + units) * half_cols + 4 * rows * slots * heads,
            bytes_accessed=4 * (heads + units) * half_cols + 2 * rows * (heads + units + 2 * half_cols),
            transcendentals=rows * slots * heads // 128,
        ),
        name="combine",
    )(half, bias, q, *keys, *values, act, wa_own, wa_other, wm_own, wm_other)


def finish_kernel(*refs, terms, packed):
    parts, refs = refs[: 1 + terms], refs[1 + terms :]
    states, gate, shift, scale, w_final, *outs = refs
    branch = parts[0][...].astype(jnp.float32)
    for part in parts[1:]:
        branch = branch + part[...].astype(jnp.float32)
    stream = (states[...].astype(jnp.float32) + gate[...] * branch).astype(jnp.bfloat16)
    normed = (layer_norm(stream.astype(jnp.float32)) * scale[...] + shift[...]).astype(jnp.bfloat16)
    speed = lax.dot_general(
        normed, w_final[...], (((1,), (1,)), ((), ())), preferred_element_type=jnp.float32
    )
    width = stream.shape[1]
    outs[0][:, :width] = stream
    if packed:
        high = speed.astype(jnp.bfloat16)
        low = (speed - high.astype(jnp.float32)).astype(jnp.bfloat16)
        outs[0][:, width:] = jnp.concatenate([high, low], 1)
    else:
        outs[1][...] = speed


def finish(parts, states, gate, shift, scale, w_final, packed):
    rows, width = states.shape
    channels = w_final.shape[0]
    steps = 2
    by_rows = lambda cols: pl.BlockSpec((rows // steps, cols), lambda i: (i, 0))
    whole = lambda array: pl.BlockSpec(array.shape, lambda i: (0, 0))
    if packed:
        out_shape = (jax.ShapeDtypeStruct((rows, width + 2 * channels), jnp.bfloat16),)
    else:
        out_shape = (
            jax.ShapeDtypeStruct((rows, width), jnp.bfloat16),
            jax.ShapeDtypeStruct((rows, channels), jnp.float32),
        )
    return pl.pallas_call(
        functools.partial(finish_kernel, terms=len(parts) - 1, packed=packed),
        out_shape=out_shape,
        grid=(steps,),
        in_specs=[by_rows(width)] * (len(parts) + 1) + [whole(a) for a in (gate, shift, scale, w_final)],
        out_specs=[by_rows(out.shape[1]) for out in out_shape],
        compiler_params=kernel_params(),
        cost_estimate=pl.CostEstimate(
            flops=2 * states.size * channels,
            bytes_accessed=2 * states.size * (len(parts) + 2),
            transcendentals=0,
        ),
        name="finish",
    )(*parts, states, gate, shift, scale, w_final)


def add(left, right):
    return (left.astype(jnp.float32) + right.astype(jnp.float32)).astype(jnp.bfloat16)


def after(values, *done):
    return lax.optimization_barrier((values, *done))[0]


def by_prompt(
    hidden,
    latents,
    vec,
    slot_token,
    text_len,
    step_index,
    guidance,
    w_mod,
    w_qkv,
    w_mlp_in,
    qk_gain,
    w_attn_out,
    w_mlp_out,
    w_final,
):
    rows_dev, prompts, model_width = hidden.shape[1:]
    head_size = qk_gain.shape[-1]
    tok_index = lax.axis_index("tok")
    mlp_index = lax.axis_index("mlp")
    half_index = lax.axis_index("cfg")
    half = half_index[None].astype(jnp.int32)

    sends = pick(tok_index[None].astype(jnp.int32), jnp.transpose(hidden[0], (1, 0, 2)))

    silu_vec = jax.nn.silu(vec[0]).astype(jnp.bfloat16)
    silu_vec = jnp.dot(
        xor_rows(prompts, tok_index).astype(jnp.bfloat16), after(silu_vec, sends[0])
    ).astype(jnp.bfloat16)
    mod_part = jnp.dot(silu_vec, w_mod, preferred_element_type=jnp.float32)

    cosine, sine_table, bias = tables(
        jnp.stack([tok_index, mlp_index]).astype(jnp.int32),
        text_len[0],
        after(slot_token, mod_part).reshape(-1, rows_dev),
        head_size,
    )
    tables_done = bias
    bias = bias.reshape(1, -1)

    wq_own = jnp.transpose(w_qkv[0], (1, 0, 2))
    wu_own, wa_own, wm_own = w_mlp_in[0], w_attn_out[0], w_mlp_out[0]
    wq_other = xor_swap(wq_own, "cfg", 1)
    wu_other = xor_swap(wu_own, "cfg", 1)
    gain = qk_gain[0]

    states_0, states_1 = sends[0], xor_swap(sends[1], "tok", 1)
    by_x, by_y = xor_swap(states_0, "mlp", 1), xor_swap(states_0, "mlp", 2)
    order = xor_rows(4 * prompts, 4 * tok_index + mlp_index)
    mods = jnp.stack([mod_part[0::2], xor_swap(after(mod_part[1::2], wq_other), "tok", 1)], 1)
    mods = jnp.concatenate([mods[0], xor_swap(after(mods[1], tables_done), "tok", 2)], 0)
    mods = jnp.stack([mods, xor_swap(after(mods, by_x, by_y, states_1), "mlp", 1)], 1)
    cut = rows_dev // 2
    far_top, far_low = xor_swap(by_x[:cut], "mlp", 2), xor_swap(by_y[cut:], "mlp", 1)
    mods = jnp.concatenate([mods, xor_swap(after(mods, far_top, far_low, wu_other), "mlp", 2)], 1)
    mods = jnp.dot(
        order.astype(jnp.float32), mods.reshape(order.shape[0], -1), precision=lax.Precision.HIGHEST
    )
    shift_mod, scale_mod, gate_mod, final_shift, final_scale = jnp.split(
        mods.reshape(1, 5 * model_width), 5, 1
    )
    scale_mod = 1.0 + scale_mod
    final_scale = 1.0 + final_scale

    wm_other = xor_swap(after(wm_own, shift_mod), "cfg", 1)

    own, queries, keys, values, acts = [], [], [], [], []
    done = (far_top, far_low, shift_mod)
    for j in range(prompts):
        if j == 0:
            states, far = states_0, jnp.concatenate([far_top, far_low], 0)
        else:
            states = states_1 if j == 1 else xor_swap(after(sends[j], own[-1], *queries[: j - 2]), "tok", j)
            send = after(states, *done)
            by_x, by_y, far = [xor_swap(send, "mlp", k) for k in (1, 2, 3)]
        own.append(states)
        q, k, v, act = project(
            half,
            (states, by_x, by_y, far),
            shift_mod,
            scale_mod,
            cosine[j],
            sine_table[j],
            gain,
            wq_own,
            wq_other,
            wu_own,
            wu_other,
        )
        queries.append(q)
        keys.append(k)
        values.append(v)
        acts.append(act)
        if j == 1:
            wa_other = xor_swap(after(wa_own, q, wm_other), "cfg", 1)
        if j:
            done = (queries[j - 1], by_x, by_y, far) + ((wm_other,) if j == 2 else ())

    streams, speeds, marks, parts = ([None] * prompts for _ in range(4))

    def first_step(j, *done):
        p0, p1, p2, p3 = parts[j]
        p3 = after(p3, *done)
        if j == 0:
            top, low = xor_swap(p3[:cut], "mlp", 1), xor_swap(p3[cut:], "mlp", 2)
        elif j % 2:
            top, low = xor_swap(p3, "mlp", 1), None
        else:
            top, low = None, xor_swap(p3, "mlp", 2)
        parts[j] = (p0, p1, p2, top, low)

    def second_step(j, *done):
        p0, p1, p2, top, low = parts[j]
        if j == 0:
            low = after(low, *done)
            p1 = jnp.concatenate([p1[:cut], add(p1[cut:], low)], 0)
            p2 = jnp.concatenate([add(p2[:cut], top), p2[cut:]], 0)
        elif j % 2:
            p2 = add(p2, after(top, *done))
            p1 = after(p1, p2)
        else:
            p1 = add(p1, after(low, *done))
            p2 = after(p2, p1)
        parts[j] = (p0, [xor_swap(p1, "mlp", 1), xor_swap(p2, "mlp", 2)])
        return p2 if j % 2 else p1

    def sum_up(j, *done):
        p0, terms = parts[j]
        outs = finish(
            [after(p0, *done), *terms],
            own[j],
            gate_mod,
            final_shift,
            final_scale,
            w_final.T,
            packed=j > 0,
        )
        marks[j] = outs[0]
        if j:
            gone = xor_swap(outs[0], "tok", j)
            streams[j] = gone[:, :model_width]
            high, low = jnp.split(gone[:, model_width:].astype(jnp.float32), 2, 1)
            speeds[j] = high + low
        else:
            streams[j], speeds[j] = outs

    done = ()
    for j in reversed(range(prompts)):
        parts[j] = combine(
            half,
            bias,
            after(queries[j], *done),
            keys,
            values,
            acts[j],
            wa_own,
            wa_other,
            wm_own,
            wm_other,
        )
        done = (parts[j][0],)
        sent = (second_step(j + 1, *done),) if j + 1 < prompts else ()
        if j + 2 < prompts:
            if j:
                sum_up(j + 2, *done)
            else:
                sent += tuple(parts[j + 2][1])
        first_step(j, *sent)
        done += sent
        if 0 < j < prompts - 2:
            done += (marks[j + 2],)
    sum_up(2, *sent)
    second_step(0, marks[2])
    sum_up(1, marks[2])
    sum_up(0, marks[1])

    stream = from_xor_order(jnp.stack(streams, 1), 1, tok_index, 2)
    half_velocity = from_xor_order(jnp.stack(speeds, 1), 1, tok_index, 2)
    own_first = (tok_index * 4 + mlp_index) * rows_dev
    own_tokens = lax.dynamic_slice_in_dim(slot_token, own_first, rows_dev, 1).T
    half_velocity = jnp.where((own_tokens >= TXT)[:, :, None], half_velocity, 0.0)
    return guided(half_velocity, half_index, latents, step_index, guidance) + (stream[None],)


def guided(half_velocity, half_index, latents, step_index, guidance):
    channel_half = latents.shape[2]
    own_part = lax.dynamic_slice_in_dim(half_velocity, half_index * channel_half, channel_half, 2)
    sent_part = lax.dynamic_slice_in_dim(
        half_velocity, (1 - half_index) * channel_half, channel_half, 2
    )
    partner = xor_swap(sent_part, "cfg", 1)
    first_half = half_index == 0
    cond_part = jnp.where(first_half, own_part, partner)
    uncond_part = jnp.where(first_half, partner, own_part)
    velocity = uncond_part + guidance[0] * (cond_part - uncond_part)
    current = step_index[0].astype(jnp.float32)
    step_size = sigma_at(current + 1.0, STEPS) - sigma_at(current, STEPS)
    return (velocity, latents + step_size * velocity)


def fits_by_prompt(mesh):
    return mesh.shape["cfg"] == 2 and mesh.shape["tok"] == PROMPTS and mesh.shape["mlp"] == 4


def solution(mesh):
    return jax.shard_map(
        by_prompt if fits_by_prompt(mesh) else on_device,
        mesh=mesh,
        in_specs=(
            P("cfg", ("tok", "mlp"), None, None),
            P(("tok", "mlp"), None, "cfg"),
            P("cfg", None, None),
            P(),
            P("cfg", None),
            P(),
            P(),
            P(None, ("tok", "mlp")),
            P(None, "cfg", None, "mlp"),
            P(None, "cfg", "mlp"),
            P(),
            P(None, "mlp", "cfg"),
            P(None, "mlp", "cfg"),
            P(),
        ),
        out_specs=(
            P(("tok", "mlp"), None, "cfg"),
            P(("tok", "mlp"), None, "cfg"),
            P("cfg", ("tok", "mlp"), None, None),
        ),
        check_vma=False,
    )
```

```python
import functools
import math

import jax
import jax.numpy as jnp
import numpy as np
from jax import lax
from jax.experimental import pallas as pl
from jax.experimental.pallas import tpu as pltpu
from jax.sharding import PartitionSpec as P

LAYERS = 1
SIDE = 32
TXT = 512
STEPS = 28
PROMPTS = 4


EPSILON = 1e-06
ROPE_BASE = 10000.0
TIME_SHIFT = 3.0


def xor_swap(value, axis, apart):
    return lax.ppermute(value, axis, [(i, i ^ apart) for i in range(lax.axis_size(axis))])


def layer_norm(values):
    average = jnp.mean(values, axis=-1, keepdims=True)
    centred = values - average
    spread = jnp.mean(centred * centred, axis=-1, keepdims=True)
    return centred * lax.rsqrt(spread + EPSILON)


def rms_norm(values, gains):
    return values * lax.rsqrt(jnp.mean(values * values, axis=-1, keepdims=True) + EPSILON) * gains


def rope_table(tokens, head_size, text_count, side_count):
    pair_count = head_size // 2
    first_pairs = head_size // 16
    axis_pairs = (head_size - head_size // 8) // 4
    pair_index = jnp.arange(pair_count).astype(jnp.float32)
    in_rows = (pair_index >= first_pairs) & (pair_index < first_pairs + axis_pairs)
    in_cols = pair_index >= first_pairs + axis_pairs
    log_base = math.log(ROPE_BASE)
    freq_rows = jnp.where(
        in_rows, jnp.exp(-log_base * (pair_index - first_pairs) / axis_pairs), 0.0
    )
    freq_cols = jnp.where(
        in_cols, jnp.exp(-log_base * (pair_index - first_pairs - axis_pairs) / axis_pairs), 0.0
    )
    is_image = tokens >= text_count
    image_pos = jnp.where(is_image, tokens - text_count, 0)
    row_pos = (image_pos // side_count).astype(jnp.float32)
    col_pos = (image_pos % side_count).astype(jnp.float32)
    angles = row_pos[..., None] * freq_rows + col_pos[..., None] * freq_cols
    return (jnp.cos(angles), jnp.sin(angles))


def apply_rope(values, cosine, sine_table):
    even_part = values[..., 0::2]
    odd_part = values[..., 1::2]
    return jnp.concatenate(
        [even_part * cosine - odd_part * sine_table, even_part * sine_table + odd_part * cosine],
        axis=-1,
    )


def sigma_at(position, steps_total):
    remain = 1.0 - position / steps_total
    return TIME_SHIFT * remain / (1.0 + (TIME_SHIFT - 1.0) * remain)


def on_device(
    hidden,
    latents,
    vec,
    slot_token,
    text_len,
    step_index,
    guidance,
    w_mod,
    w_qkv,
    w_mlp_in,
    qk_gain,
    w_attn_out,
    w_mlp_out,
    w_final,
):
    rows_dev = hidden.shape[1]
    prompts = hidden.shape[2]
    model_width = hidden.shape[3]
    head_size = qk_gain.shape[-1]
    mlp_count = lax.axis_size("mlp")
    tile_rows = rows_dev * mlp_count
    tok_index = lax.axis_index("tok")
    mlp_index = lax.axis_index("mlp")
    half_index = lax.axis_index("cfg")
    stream = hidden[0]
    silu_vec = jax.nn.silu(vec[0]).astype(jnp.bfloat16)
    mod_part = jnp.dot(silu_vec, w_mod, preferred_element_type=jnp.float32)
    modulation = lax.all_gather(mod_part, ("tok", "mlp"), axis=1, tiled=True)
    key_valid = ((slot_token >= TXT) | (slot_token < text_len[0][:, None])).astype(jnp.float32)
    tile_tokens = lax.dynamic_slice_in_dim(slot_token, tok_index * tile_rows, tile_rows, 1).T
    cosine, sine_table = rope_table(tile_tokens, head_size, TXT, SIDE)
    shift_mod = modulation[:, 0:model_width]
    scale_mod = modulation[:, model_width : 2 * model_width]
    gate_mod = modulation[:, 2 * model_width : 3 * model_width]
    normed = (
        layer_norm(stream.astype(jnp.float32)) * (1.0 + scale_mod[None]) + shift_mod[None]
    ).astype(jnp.bfloat16)
    tile_input = lax.all_gather(normed, "mlp", axis=0, tiled=True)
    qkv_weight = w_qkv[0]
    unit_weight = w_mlp_in[0]
    qkv_cols = qkv_weight.shape[1] * qkv_weight.shape[2]
    pieces = (
        lax.all_gather(qkv_weight, "cfg", axis=0, tiled=True),
        lax.all_gather(unit_weight, "cfg", axis=0, tiled=True),
    )
    number = pieces[0].shape[0]
    qkv_piece = pieces[0].reshape(number, qkv_cols)
    qkv_pre = jnp.einsum("tpd,dk->tpk", tile_input, qkv_piece, preferred_element_type=jnp.float32)
    unit_pre = jnp.einsum("tpd,dk->tpk", tile_input, pieces[1], preferred_element_type=jnp.float32)
    heads_dev = qkv_weight.shape[2] // head_size
    projected = qkv_pre.reshape(tile_rows, prompts, 3, heads_dev, head_size)
    queries = apply_rope(
        rms_norm(projected[:, :, 0], qk_gain[0, 0]), cosine[:, :, None], sine_table[:, :, None]
    ).astype(jnp.bfloat16)
    keys_rot = apply_rope(
        rms_norm(projected[:, :, 1], qk_gain[0, 1]), cosine[:, :, None], sine_table[:, :, None]
    ).astype(jnp.bfloat16)
    values = projected[:, :, 2].astype(jnp.bfloat16)
    activation = jax.nn.gelu(unit_pre, approximate=True).astype(jnp.bfloat16)
    keys_piece = lax.all_gather(keys_rot, "tok", axis=0, tiled=True)
    values_piece = lax.all_gather(values, "tok", axis=0, tiled=True)
    scores = jnp.einsum(
        "sphe,tphe->phst", queries, keys_piece, preferred_element_type=jnp.float32
    ) / math.sqrt(head_size)
    softened = jnp.exp(scores) * key_valid[:, None, None, :]
    numerator = jnp.einsum(
        "phst,tphe->sphe",
        softened.astype(jnp.bfloat16),
        values_piece,
        preferred_element_type=jnp.float32,
    )
    numerator, denominator = (numerator, jnp.sum(softened, axis=-1))
    attended = (numerator / jnp.transpose(denominator, (2, 0, 1))[..., None]).astype(jnp.bfloat16)
    attended = attended.reshape(tile_rows, prompts, heads_dev * head_size)
    out_attn = lax.all_gather(w_attn_out[0], "cfg", axis=1, tiled=True)
    out_units = lax.all_gather(w_mlp_out[0], "cfg", axis=1, tiled=True)
    branch_out = lax.psum_scatter(
        (
            jnp.einsum("tpk,kd->tpd", attended, out_attn, preferred_element_type=jnp.float32)
            + jnp.einsum("tpk,kd->tpd", activation, out_units, preferred_element_type=jnp.float32)
        ).astype(jnp.bfloat16),
        "mlp",
        scatter_dimension=0,
        tiled=True,
    ).astype(jnp.float32)
    stream = (stream.astype(jnp.float32) + gate_mod[None] * branch_out).astype(jnp.bfloat16)
    final_lo = 3 * LAYERS * model_width
    final_shift = modulation[:, final_lo : final_lo + model_width]
    final_scale = modulation[:, final_lo + model_width : final_lo + 2 * model_width]
    final_normed = (
        layer_norm(stream.astype(jnp.float32)) * (1.0 + final_scale[None]) + final_shift[None]
    ).astype(jnp.bfloat16)
    own_first = (tok_index * mlp_count + mlp_index) * rows_dev
    own_tokens = lax.dynamic_slice_in_dim(slot_token, own_first, rows_dev, 1).T
    half_velocity = jnp.einsum(
        "rpd,dc->rpc", final_normed, w_final, preferred_element_type=jnp.float32
    )
    half_velocity = jnp.where((own_tokens >= TXT)[:, :, None], half_velocity, 0.0)
    return guided(half_velocity, half_index, latents, step_index, guidance) + (stream[None],)


VMEM_BYTES = 56 * 1024 * 1024
TILE = 512
SLOTS = 3
ANY = pl.BlockSpec(memory_space=pl.ANY)
VMEM = pl.BlockSpec(memory_space=pltpu.VMEM)
SMEM = pl.BlockSpec(memory_space=pltpu.SMEM)


def kernel_params():
    return pltpu.CompilerParams(vmem_limit_bytes=VMEM_BYTES)


def flip_by_bit(values, axis, bit):
    return jnp.where(bit, jnp.flip(values, axis), values)


def from_xor_order(values, axis, index, bits):
    shape = values.shape
    split = shape[:axis] + (2,) * bits + shape[axis + 1 :]
    values = values.reshape(split)
    for place in range(bits):
        bit = (index >> (bits - 1 - place)) & 1
        values = flip_by_bit(values, axis + place, bit == 1)
    return values.reshape(shape)


def xor_rows(count, index):
    places = jnp.arange(count)
    return (places[:, None] ^ index) == places[None, :]


def pick_kernel(place_ref, *refs):
    count = len(refs) // 2
    for j in range(count):
        refs[count + j][...] = refs[j][0]


def pick(place, states):
    count, rows, width = states.shape
    take = lambda j: lambda i, s: (s[0] ^ j, i, 0)
    return pl.pallas_call(
        pick_kernel,
        out_shape=(jax.ShapeDtypeStruct((rows, width), states.dtype),) * count,
        grid_spec=pltpu.PrefetchScalarGridSpec(
            num_scalar_prefetch=1,
            grid=(2,),
            in_specs=[pl.BlockSpec((1, rows // 2, width), take(j)) for j in range(count)],
            out_specs=[pl.BlockSpec((rows // 2, width), lambda i, s: (i, 0))] * count,
        ),
        compiler_params=kernel_params(),
        cost_estimate=pl.CostEstimate(flops=0, bytes_accessed=4 * states.size, transcendentals=0),
        name="pick",
    )(place, *([states] * count))


def tables_kernel(place_ref, len_ref, tokens, freqs, bias, *outs):
    tok, mlp = place_ref[0], place_ref[1]
    own_len = len_ref[tok].astype(jnp.float32)
    blocks, rows = bias.shape
    wide = tokens.shape[1]
    odd = (lax.broadcasted_iota(jnp.int32, (rows, wide), 1) & 1) == 1

    def block(cosine, sine, chunk, index):
        source = tok * blocks + (tok ^ chunk) * 4 + (mlp ^ index)
        token = tokens[pl.ds(source, 1), :].astype(jnp.float32)
        seen = (token >= TXT) | (token < own_len)
        bias[pl.ds(chunk * 4 + index, 1), :] = jnp.where(seen, 0.0, -1e30)[:, :rows]
        place = jnp.where(token >= TXT, token - TXT, 0.0)
        row = jnp.floor(place * (1.0 / SIDE))
        down = lambda values: jnp.transpose(jnp.broadcast_to(values, (wide, wide)))[:rows]
        angles = down(row) * freqs[0:1, :] + down(place - row * SIDE) * freqs[1:2, :]
        to = pl.ds(pl.multiple_of(index * rows, 16), rows)
        cosine[to, :] = jnp.cos(angles)
        turned = jnp.sin(angles)
        sine[to, :] = jnp.where(odd, turned, -turned)

    count = len(outs) // 2
    for chunk in range(count):
        pl.loop(0, 4)(functools.partial(block, outs[chunk], outs[count + chunk], chunk))


def tables(place, text_len, tokens, head):
    chunks = text_len.shape[0]
    blocks, rows = tokens.shape[0] // chunks, tokens.shape[1]
    first, count = head // 16, (head - head // 8) // 4
    pair = np.arange(head) // 2
    rates = [
        np.where(
            (pair >= lo) & (pair < lo + count), np.exp(-math.log(ROPE_BASE) * (pair - lo) / count), 0.0
        )
        for lo in (first, first + count)
    ]
    freqs = jnp.asarray(np.stack(rates).astype(np.float32))
    table = jax.ShapeDtypeStruct((4 * rows, head), jnp.float32)
    bias, *outs = pl.pallas_call(
        tables_kernel,
        out_shape=(jax.ShapeDtypeStruct((blocks, rows), jnp.float32),) + (table,) * (2 * chunks),
        in_specs=[SMEM, SMEM, VMEM, VMEM],
        compiler_params=kernel_params(),
        cost_estimate=pl.CostEstimate(
            flops=100 * blocks * rows * head,
            bytes_accessed=8 * blocks * rows * head,
            transcendentals=2 * blocks * rows * head,
        ),
        name="tables",
    )(place, text_len, jnp.pad(tokens, ((0, 0), (0, head - rows))), freqs)
    return outs[:chunks], outs[chunks:], bias


def project_kernel(
    half_ref,
    shift,
    scale,
    cos_ref,
    sin_ref,
    gain,
    x0,
    x1,
    x2,
    x3,
    wq_own,
    wq_other,
    wu_own,
    wu_other,
    q_out,
    k_out,
    v_out,
    act_out,
    landed,
    normed,
    held,
    ready,
    x_sem,
    w_sem,
    out_sem,
):
    half = half_ref[0]
    depth = wu_own.shape[0]
    head = gain.shape[1]
    pieces = (x0, x1, x2, x3)
    rows = x0.shape[0]
    units = wu_own.shape[1] // TILE

    def weights(column, slot):
        return [
            pltpu.make_async_copy(
                ref.at[:, pl.ds(column, TILE)], held.at[slot, side], w_sem.at[slot, side]
            )
            for side, ref in enumerate((wu_own, wu_other))
        ]

    def head_weights(part):
        return [
            pltpu.make_async_copy(ref.at[part], held.at[part, side], w_sem.at[part, side])
            for side, ref in enumerate((wq_own, wq_other))
        ]

    def result(out, column, slot):
        return pltpu.make_async_copy(
            ready.at[slot], out.at[:, pl.ds(column, TILE)], out_sem.at[slot]
        )

    loads = [pltpu.make_async_copy(ref, landed.at[i], x_sem.at[i]) for i, ref in enumerate(pieces)]
    loads[0].start()
    for copy in head_weights(0):
        copy.start()
    for load in loads[1:]:
        load.start()
    for part in (1, 2):
        for copy in head_weights(part):
            copy.start()

    for index, load in enumerate(loads):
        load.wait()
        block = layer_norm(landed[index].astype(jnp.float32))
        block = (block * scale[...] + shift[...]).astype(jnp.bfloat16)
        normed[0, index * rows : (index + 1) * rows, :] = block[:, :depth]
        normed[1, index * rows : (index + 1) * rows, :] = block[:, depth:]

    even = (lax.broadcasted_iota(jnp.int32, cos_ref.shape, 1) & 1) == 0

    def product(slot):
        return jnp.dot(
            normed[half], held[slot, 0], preferred_element_type=jnp.float32
        ) + jnp.dot(normed[1 - half], held[slot, 1], preferred_element_type=jnp.float32)

    for part, out in enumerate((q_out, k_out, v_out)):
        for copy in head_weights(part):
            copy.wait()
        values = product(part)
        if part == 2:
            result(out, 0, 0).wait()
            ready[0] = values.astype(jnp.bfloat16)
        else:
            for lo in range(0, TILE, head):
                turned = rms_norm(values[:, lo : lo + head], gain[part : part + 1, :])
                partner = jnp.where(even, pltpu.roll(turned, head - 1, 1), pltpu.roll(turned, 1, 1))
                turned = turned * cos_ref[...] + partner * sin_ref[...]
                ready[part, :, lo : lo + head] = turned.astype(jnp.bfloat16)
        result(out, 0, part % 2).start()
        for copy in weights(part * TILE, part):
            copy.start()

    @pl.loop(0, units)
    def _(index):
        slot = lax.rem(index, SLOTS)
        to = lax.rem(index + 1, 2)
        column = pl.multiple_of(index * TILE, TILE)
        for copy in weights(column, slot):
            copy.wait()
        values = jax.nn.gelu(product(slot), approximate=True).astype(jnp.bfloat16)
        result(act_out, column, to).wait()
        ready[to] = values
        result(act_out, column, to).start()

        @pl.when(index + SLOTS < units)
        def _():
            later = pl.multiple_of((index + SLOTS) * TILE, TILE)
            for copy in weights(later, slot):
                copy.start()

    for slot in range(2):
        result(act_out, 0, slot).wait()


def project(half, pieces, shift, scale, cos_rows, sin_rows, gain, wq_own, wq_other, wu_own, wu_other):
    rows = sum(piece.shape[0] for piece in pieces)
    width = pieces[0].shape[1]
    depth = wu_own.shape[0]
    units = wu_own.shape[1]
    head_out = jax.ShapeDtypeStruct((rows, TILE), jnp.bfloat16)
    return pl.pallas_call(
        project_kernel,
        out_shape=(head_out, head_out, head_out, jax.ShapeDtypeStruct((rows, units), jnp.bfloat16)),
        in_specs=[SMEM] + [VMEM] * 5 + [ANY] * 8,
        out_specs=[ANY] * 4,
        scratch_shapes=[
            pltpu.VMEM((len(pieces), rows // len(pieces), width), jnp.bfloat16),
            pltpu.VMEM((2, rows, depth), jnp.bfloat16),
            pltpu.VMEM((SLOTS, 2, depth, TILE), jnp.bfloat16),
            pltpu.VMEM((2, rows, TILE), jnp.bfloat16),
            pltpu.SemaphoreType.DMA((len(pieces),)),
            pltpu.SemaphoreType.DMA((SLOTS, 2)),
            pltpu.SemaphoreType.DMA((2,)),
        ],
        compiler_params=kernel_params(),
        cost_estimate=pl.CostEstimate(
            flops=2 * rows * width * (3 * TILE + units),
            bytes_accessed=2 * width * (3 * TILE + units) + 2 * rows * (width + 3 * TILE + units),
            transcendentals=rows * units,
        ),
        name="project",
    )(half, shift, scale, cos_rows, sin_rows, gain, *pieces, wq_own, wq_other, wu_own, wu_other)


HEAD = 128


def attend(q, bias, keys, values, attended):
    rows = q.shape[0]
    size = keys[0].shape[0]

    @pl.loop(0, q.shape[1] // HEAD)
    def _(index):
        lanes = pl.ds(pl.multiple_of(index * HEAD, HEAD), HEAD)
        total = jnp.zeros((rows, 1), jnp.float32)
        numerator = jnp.zeros((rows, HEAD), jnp.float32)
        for part in range(len(keys)):
            scores = lax.dot_general(
                q[:, lanes],
                keys[part][:, lanes],
                (((1,), (1,)), ((), ())),
                preferred_element_type=jnp.float32,
            )
            soft = jnp.exp(
                scores * (1.0 / math.sqrt(HEAD)) + bias[:, part * size : (part + 1) * size]
            )
            total += jnp.sum(soft, axis=-1, keepdims=True)
            numerator += jnp.dot(
                soft.astype(jnp.bfloat16), values[part][:, lanes], preferred_element_type=jnp.float32
            )
        attended[:, lanes] = (numerator / total).astype(jnp.bfloat16)


def combine_kernel(half_ref, *refs, pieces, sides, first):
    refs = list(refs)
    take = lambda count: [refs.pop(0) for _ in range(count)]
    if first:
        bias, q = take(2)
        keys, values = take(pieces), take(pieces)
    else:
        (given,) = take(1)
    (act,) = take(1)
    weights_of = [take(2) for _ in range(sides)]
    outs = take(pieces)
    if first:
        (attended,) = take(1)
    else:
        attended = given
    units, held_a, held_m, ready, act_sem, w_sem, out_sem = refs
    half = half_ref[0]
    piece = outs[0].shape[0]
    steps = weights_of[0][0].shape[1] // TILE
    total = sides * steps

    def weights(side, column, slot):
        wa, wm = weights_of[side]
        return [
            pltpu.make_async_copy(wa.at[:, pl.ds(column, TILE)], held_a.at[slot], w_sem.at[slot, 0]),
            pltpu.make_async_copy(wm.at[:, pl.ds(column, TILE)], held_m.at[slot], w_sem.at[slot, 1]),
        ]

    def results(column, slot):
        return [
            pltpu.make_async_copy(
                ready.at[slot, pl.ds(i * piece, piece)],
                out.at[:, pl.ds(column, TILE)],
                out_sem.at[slot, i],
            )
            for i, out in enumerate(outs)
        ]

    load = pltpu.make_async_copy(act, units, act_sem)
    if first:
        load.start()
    for slot in range(SLOTS):
        for copy in weights(0, slot * TILE, slot):
            copy.start()
        if slot == 0 and not first:
            load.start()
    if first:
        attend(q, bias, keys, values, attended)
    load.wait()

    @pl.loop(0, total)
    def _(index):
        slot = lax.rem(index, SLOTS)
        to = lax.rem(index, 2)
        place = lax.rem(index + steps * half, total) if sides == 2 else index
        column = pl.multiple_of(place * TILE, TILE)
        for copy in weights(0, 0, slot):
            copy.wait()
        partial = jnp.dot(attended[...], held_a[slot], preferred_element_type=jnp.float32)
        partial += jnp.dot(units[...], held_m[slot], preferred_element_type=jnp.float32)

        @pl.when(index >= 2)
        def _():
            for copy in results(0, to):
                copy.wait()

        ready[to] = partial.astype(jnp.bfloat16)
        for copy in results(column, to):
            copy.start()

        if sides == 2:

            @pl.when(index + SLOTS < total)
            def _():
                later = pl.multiple_of((index + SLOTS - steps) * TILE, TILE)
                for copy in weights(1, later, slot):
                    copy.start()

    for slot in range(2):
        for copy in results(0, slot):
            copy.wait()


def combine(half, before, act, *weights, pieces):
    first = len(before) > 1
    sides = len(weights) // 2
    rows, units = act.shape
    heads, half_cols = weights[0].shape
    assert half_cols == SLOTS * TILE
    if first:
        bias, q, keys, values = before
        before = (bias, q, *keys, *values)
    part = jax.ShapeDtypeStruct((rows // pieces, sides * half_cols), jnp.bfloat16)
    out_shape, out_specs, scratch = [part] * pieces, [ANY] * pieces, []
    if first and sides == 1:
        out_shape.append(jax.ShapeDtypeStruct((rows, heads), jnp.bfloat16))
        out_specs.append(VMEM)
    elif first:
        scratch.append(pltpu.VMEM((rows, heads), jnp.bfloat16))
    work = 2 * rows * (heads + units) * half_cols * sides
    if first:
        work += 4 * rows * bias.shape[1] * heads
    return pl.pallas_call(
        functools.partial(combine_kernel, pieces=pieces, sides=sides, first=first),
        out_shape=tuple(out_shape),
        in_specs=[SMEM] + [VMEM] * len(before) + [ANY] * (1 + len(weights)),
        out_specs=out_specs,
        scratch_shapes=scratch
        + [
            pltpu.VMEM((rows, units), jnp.bfloat16),
            pltpu.VMEM((SLOTS, heads, TILE), jnp.bfloat16),
            pltpu.VMEM((SLOTS, units, TILE), jnp.bfloat16),
            pltpu.VMEM((2, rows, TILE), jnp.bfloat16),
            pltpu.SemaphoreType.DMA,
            pltpu.SemaphoreType.DMA((SLOTS, 2)),
            pltpu.SemaphoreType.DMA((2, pieces)),
        ],
        compiler_params=kernel_params(),
        cost_estimate=pl.CostEstimate(
            flops=work,
            bytes_accessed=2 * (heads + units) * half_cols * sides + 2 * rows * (units + 2 * half_cols),
            transcendentals=rows * rows * 4 * heads // HEAD if first else 0,
        ),
        name="combine",
    )(half, *before, act, *weights)


def finish_kernel(half_ref, *refs, terms, packed):
    parts, refs = refs[:terms], refs[terms:]
    states, gate, shift, scale, w_final, *outs = refs
    total = lambda some: sum((part[...].astype(jnp.float32) for part in some[1:]), some[0][...].astype(jnp.float32))
    if packed:
        branch = total(parts)
    else:
        *outs, sides = outs
        half = half_ref[0]
        sides[half] = total(parts[: terms // 2])
        sides[1 - half] = total(parts[terms // 2 :])
        branch = jnp.concatenate([sides[0], sides[1]], 1)
    stream = (states[...].astype(jnp.float32) + gate[...] * branch).astype(jnp.bfloat16)
    normed = (layer_norm(stream.astype(jnp.float32)) * scale[...] + shift[...]).astype(jnp.bfloat16)
    speed = lax.dot_general(
        normed, w_final[...], (((1,), (1,)), ((), ())), preferred_element_type=jnp.float32
    )
    width = stream.shape[1]
    outs[0][:, :width] = stream
    if packed:
        high = speed.astype(jnp.bfloat16)
        low = (speed - high.astype(jnp.float32)).astype(jnp.bfloat16)
        outs[0][:, width:] = jnp.concatenate([high, low], 1)
    else:
        outs[1][...] = speed


def finish(half, parts, states, gate, shift, scale, w_final, packed):
    rows, width = states.shape
    channels = w_final.shape[0]
    steps = 2
    by_rows = lambda cols: pl.BlockSpec((rows // steps, cols), lambda i: (i, 0))
    whole = lambda array: pl.BlockSpec(array.shape, lambda i: (0, 0))
    scratch = []
    if packed:
        out_shape = (jax.ShapeDtypeStruct((rows, width + 2 * channels), jnp.bfloat16),)
    else:
        out_shape = (
            jax.ShapeDtypeStruct((rows, width), jnp.bfloat16),
            jax.ShapeDtypeStruct((rows, channels), jnp.float32),
        )
        scratch.append(pltpu.VMEM((2, rows // steps, width // 2), jnp.float32))
    return pl.pallas_call(
        functools.partial(finish_kernel, terms=len(parts), packed=packed),
        out_shape=out_shape,
        grid=(steps,),
        in_specs=[SMEM]
        + [by_rows(part.shape[1]) for part in (*parts, states)]
        + [whole(a) for a in (gate, shift, scale, w_final)],
        out_specs=[by_rows(out.shape[1]) for out in out_shape],
        scratch_shapes=scratch,
        compiler_params=kernel_params(),
        cost_estimate=pl.CostEstimate(
            flops=2 * states.size * channels,
            bytes_accessed=2 * states.size * (len(parts) + 2),
            transcendentals=0,
        ),
        name="finish",
    )(half, *parts, states, gate, shift, scale, w_final)


def add(left, right):
    return (left.astype(jnp.float32) + right.astype(jnp.float32)).astype(jnp.bfloat16)


def after(values, *done):
    return lax.optimization_barrier((values, *done))[0]


def by_prompt(
    hidden,
    latents,
    vec,
    slot_token,
    text_len,
    step_index,
    guidance,
    w_mod,
    w_qkv,
    w_mlp_in,
    qk_gain,
    w_attn_out,
    w_mlp_out,
    w_final,
):
    rows_dev, prompts, model_width = hidden.shape[1:]
    head_size = qk_gain.shape[-1]
    tok_index = lax.axis_index("tok")
    mlp_index = lax.axis_index("mlp")
    half_index = lax.axis_index("cfg")
    half = half_index[None].astype(jnp.int32)

    silu_vec = jax.nn.silu(vec[0]).astype(jnp.bfloat16)
    silu_vec = jnp.dot(xor_rows(prompts, tok_index).astype(jnp.bfloat16), silu_vec).astype(jnp.bfloat16)
    mod_part = jnp.dot(silu_vec, w_mod, preferred_element_type=jnp.float32)

    sends = pick(
        tok_index[None].astype(jnp.int32),
        after(jnp.transpose(hidden[0], (1, 0, 2)), mod_part),
    )

    cosine, sine_table, bias = tables(
        jnp.stack([tok_index, mlp_index]).astype(jnp.int32),
        text_len[0],
        after(slot_token, sends[0]).reshape(-1, rows_dev),
        head_size,
    )
    tables_done = bias
    bias = bias.reshape(1, -1)

    wq_own = jnp.transpose(w_qkv[0], (1, 0, 2))
    wu_own, wa_own, wm_own = w_mlp_in[0], w_attn_out[0], w_mlp_out[0]
    wq_other = xor_swap(wq_own, "cfg", 1)
    wu_other = xor_swap(wu_own, "cfg", 1)
    gain = qk_gain[0]

    states_0 = sends[0]
    by_x, by_y = xor_swap(states_0, "mlp", 1), xor_swap(states_0, "mlp", 2)
    order = xor_rows(4 * prompts, 4 * tok_index + mlp_index)
    mods = jnp.stack([mod_part[0::2], xor_swap(after(mod_part[1::2], wq_other), "tok", 1)], 1)
    mods = jnp.concatenate([mods[0], xor_swap(after(mods[1], tables_done), "tok", 2)], 0)
    states_1 = xor_swap(sends[1], "tok", 1)
    mods = jnp.stack([mods, xor_swap(mods, "mlp", 1)], 1)
    cut = rows_dev // 2
    far_top, far_low = xor_swap(by_x[:cut], "mlp", 2), xor_swap(by_y[cut:], "mlp", 1)
    mods = jnp.concatenate([mods, xor_swap(after(mods, far_top, far_low, states_1, wu_other), "mlp", 2)], 1)
    mods = jnp.dot(
        order.astype(jnp.float32), mods.reshape(order.shape[0], -1), precision=lax.Precision.HIGHEST
    )
    shift_mod, scale_mod, gate_mod, final_shift, final_scale = jnp.split(
        mods.reshape(1, 5 * model_width), 5, 1
    )
    scale_mod = 1.0 + scale_mod
    final_scale = 1.0 + final_scale

    wm_other = xor_swap(after(wm_own, shift_mod), "cfg", 1)

    own, queries, keys, values, acts = [], [], [], [], []
    done = (far_top, far_low, shift_mod)
    for j in range(prompts):
        if j == 0:
            states, far = states_0, jnp.concatenate([far_top, far_low], 0)
        else:
            states = states_1 if j == 1 else xor_swap(after(sends[j], own[-1], *queries[: j - 2]), "tok", j)
            send = after(states, *done)
            by_x, by_y, far = [xor_swap(send, "mlp", k) for k in (1, 2, 3)]
        own.append(states)
        q, k, v, act = project(
            half,
            (states, by_x, by_y, far),
            shift_mod,
            scale_mod,
            cosine[j],
            sine_table[j],
            gain,
            wq_own,
            wq_other,
            wu_own,
            wu_other,
        )
        queries.append(q)
        keys.append(k)
        values.append(v)
        acts.append(act)
        if j == 1:
            wa_other = xor_swap(after(wa_own, q, wm_other), "cfg", 1)
        if j:
            done = (queries[j - 1], by_x, by_y, far) + ((wm_other,) if j == 2 else ())

    streams, speeds, marks, parts = ([None] * prompts for _ in range(4))

    def attention(j, *done):
        return (bias, after(queries[j], *done), keys, values)

    def first_step(j, *done):
        p0, p1, p2, p3 = parts[j]
        parts[j] = (p0, p1, p2, xor_swap(after(p3, *done), "mlp", 1 if j % 2 else 2))

    def second_step(j, *done):
        p0, p1, p2, far = parts[j]
        if j % 2:
            p2 = add(p2, after(far, *done))
            p1 = after(p1, p2)
        else:
            p1 = add(p1, after(far, *done))
            p2 = after(p2, p1)
        parts[j] = (p0, xor_swap(p1, "mlp", 1), xor_swap(p2, "mlp", 2))
        return p2 if j % 2 else p1

    def sum_up(j, first, *others):
        outs = finish(
            half,
            [first, *others],
            own[j],
            gate_mod,
            final_shift,
            final_scale,
            w_final.T,
            packed=j > 0,
        )
        marks[j] = outs[0]
        if j:
            gone = xor_swap(outs[0], "tok", j)
            streams[j] = gone[:, :model_width]
            high, low = jnp.split(gone[:, model_width:].astype(jnp.float32), 2, 1)
            speeds[j] = high + low
        else:
            streams[j], speeds[j] = outs

    both = (wa_own, wm_own, wa_other, wm_other)
    done = ()
    for j in (3, 2, 1):
        parts[j] = combine(half, attention(j, *done), acts[j], *both, pieces=4)
        done = (parts[j][0],)
        sent = (second_step(j + 1, *done),) if j + 1 < prompts else ()
        if j + 2 < prompts:
            p0, *others = parts[j + 2]
            sum_up(j + 2, after(p0, *done), *others)
            done += (marks[j + 2],)
        first_step(j, *sent)
        done += sent

    *last, att = combine(half, attention(0, *done), acts[0], wa_own, wm_own, pieces=4)
    sent = second_step(1, last[0])
    p0, *others = parts[2]
    far = xor_swap(after(last[3], sent, *others), "mlp", 1)
    rest = combine(half, (after(att, sent),), acts[0], wa_other, wm_other, pieces=4)
    rest_far = xor_swap(rest[3], "mlp", 2)
    turned = add(last[2], after(far, rest[0]))
    own_terms = [last[0], xor_swap(after(last[1], turned), "mlp", 1), xor_swap(turned, "mlp", 2)]
    sum_up(2, after(p0, turned), *others)
    turned = add(rest[1], after(rest_far, marks[2]))
    other_terms = [rest[0], xor_swap(turned, "mlp", 1), xor_swap(after(rest[2], turned), "mlp", 2)]
    p0, *others = parts[1]
    sum_up(1, after(p0, turned), *others)
    sum_up(0, after(own_terms[0], marks[1]), *own_terms[1:], *other_terms)

    stream = from_xor_order(jnp.stack(streams, 1), 1, tok_index, 2)
    half_velocity = from_xor_order(jnp.stack(speeds, 1), 1, tok_index, 2)
    own_first = (tok_index * 4 + mlp_index) * rows_dev
    own_tokens = lax.dynamic_slice_in_dim(slot_token, own_first, rows_dev, 1).T
    half_velocity = jnp.where((own_tokens >= TXT)[:, :, None], half_velocity, 0.0)
    return guided(half_velocity, half_index, latents, step_index, guidance) + (stream[None],)


def guided(half_velocity, half_index, latents, step_index, guidance):
    channel_half = latents.shape[2]
    own_part = lax.dynamic_slice_in_dim(half_velocity, half_index * channel_half, channel_half, 2)
    sent_part = lax.dynamic_slice_in_dim(
        half_velocity, (1 - half_index) * channel_half, channel_half, 2
    )
    partner = xor_swap(sent_part, "cfg", 1)
    first_half = half_index == 0
    cond_part = jnp.where(first_half, own_part, partner)
    uncond_part = jnp.where(first_half, partner, own_part)
    velocity = uncond_part + guidance[0] * (cond_part - uncond_part)
    current = step_index[0].astype(jnp.float32)
    step_size = sigma_at(current + 1.0, STEPS) - sigma_at(current, STEPS)
    return (velocity, latents + step_size * velocity)


def fits_by_prompt(mesh):
    return mesh.shape["cfg"] == 2 and mesh.shape["tok"] == PROMPTS and mesh.shape["mlp"] == 4


def solution(mesh):
    return jax.shard_map(
        by_prompt if fits_by_prompt(mesh) else on_device,
        mesh=mesh,
        in_specs=(
            P("cfg", ("tok", "mlp"), None, None),
            P(("tok", "mlp"), None, "cfg"),
            P("cfg", None, None),
            P(),
            P("cfg", None),
            P(),
            P(),
            P(None, ("tok", "mlp")),
            P(None, "cfg", None, "mlp"),
            P(None, "cfg", "mlp"),
            P(),
            P(None, "mlp", "cfg"),
            P(None, "mlp", "cfg"),
            P(),
        ),
        out_specs=(
            P(("tok", "mlp"), None, "cfg"),
            P(("tok", "mlp"), None, "cfg"),
            P("cfg", ("tok", "mlp"), None, None),
        ),
        check_vma=False,
    )
```

```python
import functools
import math

import jax
import jax.numpy as jnp
import numpy as np
from jax import lax
from jax.experimental import pallas as pl
from jax.experimental.pallas import tpu as pltpu
from jax.sharding import PartitionSpec as P

LAYERS = 1
SIDE = 32
TXT = 512
STEPS = 28
PROMPTS = 4


EPSILON = 1e-06
ROPE_BASE = 10000.0
TIME_SHIFT = 3.0


def xor_swap(value, axis, apart):
    return lax.ppermute(value, axis, [(i, i ^ apart) for i in range(lax.axis_size(axis))])


def layer_norm(values):
    average = jnp.mean(values, axis=-1, keepdims=True)
    centred = values - average
    spread = jnp.mean(centred * centred, axis=-1, keepdims=True)
    return centred * lax.rsqrt(spread + EPSILON)


def rms_norm(values, gains):
    return values * lax.rsqrt(jnp.mean(values * values, axis=-1, keepdims=True) + EPSILON) * gains


def rope_table(tokens, head_size, text_count, side_count):
    pair_count = head_size // 2
    first_pairs = head_size // 16
    axis_pairs = (head_size - head_size // 8) // 4
    pair_index = jnp.arange(pair_count).astype(jnp.float32)
    in_rows = (pair_index >= first_pairs) & (pair_index < first_pairs + axis_pairs)
    in_cols = pair_index >= first_pairs + axis_pairs
    log_base = math.log(ROPE_BASE)
    freq_rows = jnp.where(
        in_rows, jnp.exp(-log_base * (pair_index - first_pairs) / axis_pairs), 0.0
    )
    freq_cols = jnp.where(
        in_cols, jnp.exp(-log_base * (pair_index - first_pairs - axis_pairs) / axis_pairs), 0.0
    )
    is_image = tokens >= text_count
    image_pos = jnp.where(is_image, tokens - text_count, 0)
    row_pos = (image_pos // side_count).astype(jnp.float32)
    col_pos = (image_pos % side_count).astype(jnp.float32)
    angles = row_pos[..., None] * freq_rows + col_pos[..., None] * freq_cols
    return (jnp.cos(angles), jnp.sin(angles))


def apply_rope(values, cosine, sine_table):
    even_part = values[..., 0::2]
    odd_part = values[..., 1::2]
    return jnp.concatenate(
        [even_part * cosine - odd_part * sine_table, even_part * sine_table + odd_part * cosine],
        axis=-1,
    )


def sigma_at(position, steps_total):
    remain = 1.0 - position / steps_total
    return TIME_SHIFT * remain / (1.0 + (TIME_SHIFT - 1.0) * remain)


def on_device(
    hidden,
    latents,
    vec,
    slot_token,
    text_len,
    step_index,
    guidance,
    w_mod,
    w_qkv,
    w_mlp_in,
    qk_gain,
    w_attn_out,
    w_mlp_out,
    w_final,
):
    rows_dev = hidden.shape[1]
    prompts = hidden.shape[2]
    model_width = hidden.shape[3]
    head_size = qk_gain.shape[-1]
    mlp_count = lax.axis_size("mlp")
    tile_rows = rows_dev * mlp_count
    tok_index = lax.axis_index("tok")
    mlp_index = lax.axis_index("mlp")
    half_index = lax.axis_index("cfg")
    stream = hidden[0]
    silu_vec = jax.nn.silu(vec[0]).astype(jnp.bfloat16)
    mod_part = jnp.dot(silu_vec, w_mod, preferred_element_type=jnp.float32)
    modulation = lax.all_gather(mod_part, ("tok", "mlp"), axis=1, tiled=True)
    key_valid = ((slot_token >= TXT) | (slot_token < text_len[0][:, None])).astype(jnp.float32)
    tile_tokens = lax.dynamic_slice_in_dim(slot_token, tok_index * tile_rows, tile_rows, 1).T
    cosine, sine_table = rope_table(tile_tokens, head_size, TXT, SIDE)
    shift_mod = modulation[:, 0:model_width]
    scale_mod = modulation[:, model_width : 2 * model_width]
    gate_mod = modulation[:, 2 * model_width : 3 * model_width]
    normed = (
        layer_norm(stream.astype(jnp.float32)) * (1.0 + scale_mod[None]) + shift_mod[None]
    ).astype(jnp.bfloat16)
    tile_input = lax.all_gather(normed, "mlp", axis=0, tiled=True)
    qkv_weight = w_qkv[0]
    unit_weight = w_mlp_in[0]
    qkv_cols = qkv_weight.shape[1] * qkv_weight.shape[2]
    pieces = (
        lax.all_gather(qkv_weight, "cfg", axis=0, tiled=True),
        lax.all_gather(unit_weight, "cfg", axis=0, tiled=True),
    )
    number = pieces[0].shape[0]
    qkv_piece = pieces[0].reshape(number, qkv_cols)
    qkv_pre = jnp.einsum("tpd,dk->tpk", tile_input, qkv_piece, preferred_element_type=jnp.float32)
    unit_pre = jnp.einsum("tpd,dk->tpk", tile_input, pieces[1], preferred_element_type=jnp.float32)
    heads_dev = qkv_weight.shape[2] // head_size
    projected = qkv_pre.reshape(tile_rows, prompts, 3, heads_dev, head_size)
    queries = apply_rope(
        rms_norm(projected[:, :, 0], qk_gain[0, 0]), cosine[:, :, None], sine_table[:, :, None]
    ).astype(jnp.bfloat16)
    keys_rot = apply_rope(
        rms_norm(projected[:, :, 1], qk_gain[0, 1]), cosine[:, :, None], sine_table[:, :, None]
    ).astype(jnp.bfloat16)
    values = projected[:, :, 2].astype(jnp.bfloat16)
    activation = jax.nn.gelu(unit_pre, approximate=True).astype(jnp.bfloat16)
    keys_piece = lax.all_gather(keys_rot, "tok", axis=0, tiled=True)
    values_piece = lax.all_gather(values, "tok", axis=0, tiled=True)
    scores = jnp.einsum(
        "sphe,tphe->phst", queries, keys_piece, preferred_element_type=jnp.float32
    ) / math.sqrt(head_size)
    softened = jnp.exp(scores) * key_valid[:, None, None, :]
    numerator = jnp.einsum(
        "phst,tphe->sphe",
        softened.astype(jnp.bfloat16),
        values_piece,
        preferred_element_type=jnp.float32,
    )
    numerator, denominator = (numerator, jnp.sum(softened, axis=-1))
    attended = (numerator / jnp.transpose(denominator, (2, 0, 1))[..., None]).astype(jnp.bfloat16)
    attended = attended.reshape(tile_rows, prompts, heads_dev * head_size)
    out_attn = lax.all_gather(w_attn_out[0], "cfg", axis=1, tiled=True)
    out_units = lax.all_gather(w_mlp_out[0], "cfg", axis=1, tiled=True)
    branch_out = lax.psum_scatter(
        (
            jnp.einsum("tpk,kd->tpd", attended, out_attn, preferred_element_type=jnp.float32)
            + jnp.einsum("tpk,kd->tpd", activation, out_units, preferred_element_type=jnp.float32)
        ).astype(jnp.bfloat16),
        "mlp",
        scatter_dimension=0,
        tiled=True,
    ).astype(jnp.float32)
    stream = (stream.astype(jnp.float32) + gate_mod[None] * branch_out).astype(jnp.bfloat16)
    final_lo = 3 * LAYERS * model_width
    final_shift = modulation[:, final_lo : final_lo + model_width]
    final_scale = modulation[:, final_lo + model_width : final_lo + 2 * model_width]
    final_normed = (
        layer_norm(stream.astype(jnp.float32)) * (1.0 + final_scale[None]) + final_shift[None]
    ).astype(jnp.bfloat16)
    own_first = (tok_index * mlp_count + mlp_index) * rows_dev
    own_tokens = lax.dynamic_slice_in_dim(slot_token, own_first, rows_dev, 1).T
    half_velocity = jnp.einsum(
        "rpd,dc->rpc", final_normed, w_final, preferred_element_type=jnp.float32
    )
    half_velocity = jnp.where((own_tokens >= TXT)[:, :, None], half_velocity, 0.0)
    return guided(half_velocity, half_index, latents, step_index, guidance) + (stream[None],)


VMEM_BYTES = 63 * 1024 * 1024
TILE = 512
SLOTS = 3
ANY = pl.BlockSpec(memory_space=pl.ANY)
VMEM = pl.BlockSpec(memory_space=pltpu.VMEM)
SMEM = pl.BlockSpec(memory_space=pltpu.SMEM)


def kernel_params():
    return pltpu.CompilerParams(vmem_limit_bytes=VMEM_BYTES)


def flip_by_bit(values, axis, bit):
    return jnp.where(bit, jnp.flip(values, axis), values)


def from_xor_order(values, axis, index, bits):
    shape = values.shape
    split = shape[:axis] + (2,) * bits + shape[axis + 1 :]
    values = values.reshape(split)
    for place in range(bits):
        bit = (index >> (bits - 1 - place)) & 1
        values = flip_by_bit(values, axis + place, bit == 1)
    return values.reshape(shape)


def xor_rows(count, index):
    places = jnp.arange(count)
    return (places[:, None] ^ index) == places[None, :]


def pick_kernel(place_ref, *refs):
    count = len(refs) // 2
    for j in range(count):
        refs[count + j][...] = refs[j][0]


def pick(place, states):
    count, rows, width = states.shape
    take = lambda j: lambda i, s: (s[0] ^ j, i, 0)
    return pl.pallas_call(
        pick_kernel,
        out_shape=(jax.ShapeDtypeStruct((rows, width), states.dtype),) * count,
        grid_spec=pltpu.PrefetchScalarGridSpec(
            num_scalar_prefetch=1,
            grid=(2,),
            in_specs=[pl.BlockSpec((1, rows // 2, width), take(j)) for j in range(count)],
            out_specs=[pl.BlockSpec((rows // 2, width), lambda i, s: (i, 0))] * count,
        ),
        compiler_params=kernel_params(),
        cost_estimate=pl.CostEstimate(flops=0, bytes_accessed=4 * states.size, transcendentals=0),
        name="pick",
    )(place, *([states] * count))


def tables_kernel(place_ref, len_ref, tokens, freqs, bias, *outs):
    tok, mlp = place_ref[0], place_ref[1]
    own_len = len_ref[tok].astype(jnp.float32)
    blocks, rows = bias.shape
    wide = tokens.shape[1]
    odd = (lax.broadcasted_iota(jnp.int32, (rows, wide), 1) & 1) == 1

    def block(cosine, sine, chunk, index):
        source = tok * blocks + (tok ^ chunk) * 4 + (mlp ^ index)
        token = tokens[pl.ds(source, 1), :].astype(jnp.float32)
        seen = (token >= TXT) | (token < own_len)
        bias[pl.ds(chunk * 4 + index, 1), :] = jnp.where(seen, 0.0, -1e30)[:, :rows]
        place = jnp.where(token >= TXT, token - TXT, 0.0)
        row = jnp.floor(place * (1.0 / SIDE))
        down = lambda values: jnp.transpose(jnp.broadcast_to(values, (wide, wide)))[:rows]
        angles = down(row) * freqs[0:1, :] + down(place - row * SIDE) * freqs[1:2, :]
        to = pl.ds(pl.multiple_of(index * rows, 16), rows)
        cosine[to, :] = jnp.cos(angles)
        turned = jnp.sin(angles)
        sine[to, :] = jnp.where(odd, turned, -turned)

    count = len(outs) // 2
    for chunk in range(count):
        pl.loop(0, 4)(functools.partial(block, outs[chunk], outs[count + chunk], chunk))


def tables(place, text_len, tokens, head):
    chunks = text_len.shape[0]
    blocks, rows = tokens.shape[0] // chunks, tokens.shape[1]
    first, count = head // 16, (head - head // 8) // 4
    pair = np.arange(head) // 2
    rates = [
        np.where(
            (pair >= lo) & (pair < lo + count), np.exp(-math.log(ROPE_BASE) * (pair - lo) / count), 0.0
        )
        for lo in (first, first + count)
    ]
    freqs = jnp.asarray(np.stack(rates).astype(np.float32))
    table = jax.ShapeDtypeStruct((4 * rows, head), jnp.float32)
    bias, *outs = pl.pallas_call(
        tables_kernel,
        out_shape=(jax.ShapeDtypeStruct((blocks, rows), jnp.float32),) + (table,) * (2 * chunks),
        in_specs=[SMEM, SMEM, VMEM, VMEM],
        compiler_params=kernel_params(),
        cost_estimate=pl.CostEstimate(
            flops=100 * blocks * rows * head,
            bytes_accessed=8 * blocks * rows * head,
            transcendentals=2 * blocks * rows * head,
        ),
        name="tables",
    )(place, text_len, jnp.pad(tokens, ((0, 0), (0, head - rows))), freqs)
    return outs[:chunks], outs[chunks:], bias


def project_kernel(
    half_ref,
    shift,
    scale,
    cos_ref,
    sin_ref,
    gain,
    x0,
    x1,
    x2,
    x3,
    wq_own,
    wq_other,
    wu_own,
    wu_other,
    q_out,
    k_out,
    v_out,
    act_out,
    landed,
    normed,
    held,
    ready,
    x_sem,
    w_sem,
    out_sem,
):
    half = half_ref[0]
    depth = wu_own.shape[0]
    head = gain.shape[1]
    pieces = (x0, x1, x2, x3)
    rows = x0.shape[0]
    units = wu_own.shape[1] // TILE

    def weights(column, slot):
        return [
            pltpu.make_async_copy(
                ref.at[:, pl.ds(column, TILE)], held.at[slot, side], w_sem.at[slot, side]
            )
            for side, ref in enumerate((wu_own, wu_other))
        ]

    def head_weights(part):
        return [
            pltpu.make_async_copy(ref.at[part], held.at[part, side], w_sem.at[part, side])
            for side, ref in enumerate((wq_own, wq_other))
        ]

    def result(out, column, slot):
        return pltpu.make_async_copy(
            ready.at[slot], out.at[:, pl.ds(column, TILE)], out_sem.at[slot]
        )

    loads = [pltpu.make_async_copy(ref, landed.at[i], x_sem.at[i]) for i, ref in enumerate(pieces)]
    loads[0].start()
    for copy in head_weights(0):
        copy.start()
    for load in loads[1:]:
        load.start()
    for part in (1, 2):
        for copy in head_weights(part):
            copy.start()

    for index, load in enumerate(loads):
        load.wait()
        block = layer_norm(landed[index].astype(jnp.float32))
        block = (block * scale[...] + shift[...]).astype(jnp.bfloat16)
        normed[0, index * rows : (index + 1) * rows, :] = block[:, :depth]
        normed[1, index * rows : (index + 1) * rows, :] = block[:, depth:]

    even = (lax.broadcasted_iota(jnp.int32, cos_ref.shape, 1) & 1) == 0

    def product(slot):
        return jnp.dot(
            normed[half], held[slot, 0], preferred_element_type=jnp.float32
        ) + jnp.dot(normed[1 - half], held[slot, 1], preferred_element_type=jnp.float32)

    for part, out in enumerate((q_out, k_out, v_out)):
        for copy in head_weights(part):
            copy.wait()
        values = product(part)
        if part == 2:
            result(out, 0, 0).wait()
            ready[0] = values.astype(jnp.bfloat16)
        else:
            for lo in range(0, TILE, head):
                turned = rms_norm(values[:, lo : lo + head], gain[part : part + 1, :])
                partner = jnp.where(even, pltpu.roll(turned, head - 1, 1), pltpu.roll(turned, 1, 1))
                turned = turned * cos_ref[...] + partner * sin_ref[...]
                ready[part, :, lo : lo + head] = turned.astype(jnp.bfloat16)
        result(out, 0, part % 2).start()
        for copy in weights(part * TILE, part):
            copy.start()

    @pl.loop(0, units)
    def _(index):
        slot = lax.rem(index, SLOTS)
        to = lax.rem(index + 1, 2)
        column = pl.multiple_of(index * TILE, TILE)
        for copy in weights(column, slot):
            copy.wait()
        values = jax.nn.gelu(product(slot), approximate=True).astype(jnp.bfloat16)
        result(act_out, column, to).wait()
        ready[to] = values
        result(act_out, column, to).start()

        @pl.when(index + SLOTS < units)
        def _():
            later = pl.multiple_of((index + SLOTS) * TILE, TILE)
            for copy in weights(later, slot):
                copy.start()

    for slot in range(2):
        result(act_out, 0, slot).wait()


def project(half, pieces, shift, scale, cos_rows, sin_rows, gain, wq_own, wq_other, wu_own, wu_other):
    rows = sum(piece.shape[0] for piece in pieces)
    width = pieces[0].shape[1]
    depth = wu_own.shape[0]
    units = wu_own.shape[1]
    head_out = jax.ShapeDtypeStruct((rows, TILE), jnp.bfloat16)
    return pl.pallas_call(
        project_kernel,
        out_shape=(head_out, head_out, head_out, jax.ShapeDtypeStruct((rows, units), jnp.bfloat16)),
        in_specs=[SMEM] + [VMEM] * 5 + [ANY] * 8,
        out_specs=[ANY] * 4,
        scratch_shapes=[
            pltpu.VMEM((len(pieces), rows // len(pieces), width), jnp.bfloat16),
            pltpu.VMEM((2, rows, depth), jnp.bfloat16),
            pltpu.VMEM((SLOTS, 2, depth, TILE), jnp.bfloat16),
            pltpu.VMEM((2, rows, TILE), jnp.bfloat16),
            pltpu.SemaphoreType.DMA((len(pieces),)),
            pltpu.SemaphoreType.DMA((SLOTS, 2)),
            pltpu.SemaphoreType.DMA((2,)),
        ],
        compiler_params=kernel_params(),
        cost_estimate=pl.CostEstimate(
            flops=2 * rows * width * (3 * TILE + units),
            bytes_accessed=2 * width * (3 * TILE + units) + 2 * rows * (width + 3 * TILE + units),
            transcendentals=rows * units,
        ),
        name="project",
    )(half, shift, scale, cos_rows, sin_rows, gain, *pieces, wq_own, wq_other, wu_own, wu_other)


def combine_kernel(
    half_ref,
    bias,
    q,
    k0,
    k1,
    k2,
    k3,
    v0,
    v1,
    v2,
    v3,
    act,
    wa_own,
    wa_other,
    wm_own,
    wm_other,
    p0,
    p1,
    p2,
    p3,
    heads_in,
    attended,
    units,
    held_a,
    held_m,
    ready,
    head_sem,
    act_sem,
    w_sem,
    out_sem,
):
    half = half_ref[0]
    inputs, outs = (q, k0, k1, k2, k3, v0, v1, v2, v3), (p0, p1, p2, p3)
    rows, cols = q.shape
    size = k0.shape[0]
    piece = p0.shape[0]
    head = 128
    count = cols // head

    def head_loads(index, column):
        return [
            pltpu.make_async_copy(
                ref.at[:, pl.ds(column, head)], heads_in.at[index, i], head_sem.at[index, i]
            )
            for i, ref in enumerate(inputs)
        ]

    steps = wa_own.shape[1] // TILE

    def weights(wa, wm, column, slot):
        return [
            pltpu.make_async_copy(wa.at[:, pl.ds(column, TILE)], held_a.at[slot], w_sem.at[slot, 0]),
            pltpu.make_async_copy(wm.at[:, pl.ds(column, TILE)], held_m.at[slot], w_sem.at[slot, 1]),
        ]

    def results(column, slot):
        return [
            pltpu.make_async_copy(
                ready.at[slot, pl.ds(i * piece, piece)],
                out.at[:, pl.ds(column, TILE)],
                out_sem.at[slot, i],
            )
            for i, out in enumerate(outs)
        ]

    for index in range(count):
        for copy in head_loads(index, index * head):
            copy.start()
    load = pltpu.make_async_copy(act, units, act_sem)
    load.start()
    for slot in range(SLOTS):
        for copy in weights(wa_own, wm_own, slot * TILE, slot):
            copy.start()

    @pl.loop(0, count)
    def _(index):
        for copy in head_loads(index, 0):
            copy.wait()
        lanes = pl.ds(pl.multiple_of(index * head, head), head)
        total = jnp.zeros((rows, 1), jnp.float32)
        numerator = jnp.zeros((rows, head), jnp.float32)
        for part in range(4):
            scores = lax.dot_general(
                heads_in[index, 0],
                heads_in[index, 1 + part],
                (((1,), (1,)), ((), ())),
                preferred_element_type=jnp.float32,
            )
            soft = jnp.exp(
                scores * (1.0 / math.sqrt(head)) + bias[:, part * size : (part + 1) * size]
            )
            total += jnp.sum(soft, axis=-1, keepdims=True)
            numerator += jnp.dot(
                soft.astype(jnp.bfloat16), heads_in[index, 5 + part], preferred_element_type=jnp.float32
            )
        attended[:, lanes] = (numerator / total).astype(jnp.bfloat16)

    load.wait()

    def write(index, slot, column, first, wa, wm):
        for copy in weights(wa, wm, 0, slot):
            copy.wait()
        partial = jnp.dot(attended[...], held_a[slot], preferred_element_type=jnp.float32)
        partial += jnp.dot(units[...], held_m[slot], preferred_element_type=jnp.float32)
        to = lax.rem(index, 2)

        @pl.when(index >= 2)
        def _():
            for copy in results(0, to):
                copy.wait()

        ready[to] = partial.astype(jnp.bfloat16)
        for copy in results(column, to):
            copy.start()

    @pl.loop(0, 2 * steps)
    def _(index):
        slot = lax.rem(index, SLOTS)
        place = lax.rem(index + steps * half, 2 * steps)
        write(index, slot, pl.multiple_of(place * TILE, TILE), 0, wa_own, wm_own)

        @pl.when(index + SLOTS < 2 * steps)
        def _():
            later = pl.multiple_of((index + SLOTS - steps) * TILE, TILE)
            for copy in weights(wa_other, wm_other, later, slot):
                copy.start()

    for slot in range(2):
        for copy in results(0, slot):
            copy.wait()


def combine(half, bias, q, keys, values, act, wa_own, wa_other, wm_own, wm_other):
    rows, heads = q.shape
    units = act.shape[1]
    slots = bias.shape[1]
    half_cols = wa_own.shape[1]
    assert half_cols == SLOTS * TILE
    pieces = len(keys)
    part = jax.ShapeDtypeStruct((rows // pieces, 2 * half_cols), jnp.bfloat16)
    return pl.pallas_call(
        combine_kernel,
        out_shape=(part,) * pieces,
        in_specs=[SMEM, VMEM] + [ANY] * (6 + 2 * pieces),
        out_specs=[ANY] * pieces,
        scratch_shapes=[
            pltpu.VMEM((heads // 128, 1 + 2 * pieces, rows, 128), jnp.bfloat16),
            pltpu.VMEM((rows, heads), jnp.bfloat16),
            pltpu.VMEM((rows, units), jnp.bfloat16),
            pltpu.VMEM((SLOTS, heads, TILE), jnp.bfloat16),
            pltpu.VMEM((SLOTS, units, TILE), jnp.bfloat16),
            pltpu.VMEM((2, rows, TILE), jnp.bfloat16),
            pltpu.SemaphoreType.DMA((heads // 128, 1 + 2 * pieces)),
            pltpu.SemaphoreType.DMA,
            pltpu.SemaphoreType.DMA((SLOTS, 2)),
            pltpu.SemaphoreType.DMA((2, pieces)),
        ],
        compiler_params=kernel_params(),
        cost_estimate=pl.CostEstimate(
            flops=4 * rows * (heads + units) * half_cols + 4 * rows * slots * heads,
            bytes_accessed=4 * (heads + units) * half_cols + 2 * rows * (heads + units + 2 * half_cols),
            transcendentals=rows * slots * heads // 128,
        ),
        name="combine",
    )(half, bias, q, *keys, *values, act, wa_own, wa_other, wm_own, wm_other)


def finish_kernel(*refs, terms, packed):
    parts, refs = refs[: 1 + terms], refs[1 + terms :]
    states, gate, shift, scale, w_final, *outs = refs
    branch = parts[0][...].astype(jnp.float32)
    for part in parts[1:]:
        branch = branch + part[...].astype(jnp.float32)
    stream = (states[...].astype(jnp.float32) + gate[...] * branch).astype(jnp.bfloat16)
    normed = (layer_norm(stream.astype(jnp.float32)) * scale[...] + shift[...]).astype(jnp.bfloat16)
    speed = lax.dot_general(
        normed, w_final[...], (((1,), (1,)), ((), ())), preferred_element_type=jnp.float32
    )
    width = stream.shape[1]
    outs[0][:, :width] = stream
    if packed:
        high = speed.astype(jnp.bfloat16)
        low = (speed - high.astype(jnp.float32)).astype(jnp.bfloat16)
        outs[0][:, width:] = jnp.concatenate([high, low], 1)
    else:
        outs[1][...] = speed


def finish(parts, states, gate, shift, scale, w_final, packed):
    rows, width = states.shape
    channels = w_final.shape[0]
    steps = 2
    by_rows = lambda cols: pl.BlockSpec((rows // steps, cols), lambda i: (i, 0))
    whole = lambda array: pl.BlockSpec(array.shape, lambda i: (0, 0))
    if packed:
        out_shape = (jax.ShapeDtypeStruct((rows, width + 2 * channels), jnp.bfloat16),)
    else:
        out_shape = (
            jax.ShapeDtypeStruct((rows, width), jnp.bfloat16),
            jax.ShapeDtypeStruct((rows, channels), jnp.float32),
        )
    return pl.pallas_call(
        functools.partial(finish_kernel, terms=len(parts) - 1, packed=packed),
        out_shape=out_shape,
        grid=(steps,),
        in_specs=[by_rows(width)] * (len(parts) + 1) + [whole(a) for a in (gate, shift, scale, w_final)],
        out_specs=[by_rows(out.shape[1]) for out in out_shape],
        compiler_params=kernel_params(),
        cost_estimate=pl.CostEstimate(
            flops=2 * states.size * channels,
            bytes_accessed=2 * states.size * (len(parts) + 2),
            transcendentals=0,
        ),
        name="finish",
    )(*parts, states, gate, shift, scale, w_final)


def add(left, right):
    return (left.astype(jnp.float32) + right.astype(jnp.float32)).astype(jnp.bfloat16)


def after(values, *done):
    return lax.optimization_barrier((values, *done))[0]


def by_prompt(
    hidden,
    latents,
    vec,
    slot_token,
    text_len,
    step_index,
    guidance,
    w_mod,
    w_qkv,
    w_mlp_in,
    qk_gain,
    w_attn_out,
    w_mlp_out,
    w_final,
):
    rows_dev, prompts, model_width = hidden.shape[1:]
    head_size = qk_gain.shape[-1]
    tok_index = lax.axis_index("tok")
    mlp_index = lax.axis_index("mlp")
    half_index = lax.axis_index("cfg")
    half = half_index[None].astype(jnp.int32)

    sends = pick(tok_index[None].astype(jnp.int32), jnp.transpose(hidden[0], (1, 0, 2)))

    silu_vec = jax.nn.silu(vec[0]).astype(jnp.bfloat16)
    silu_vec = jnp.dot(
        xor_rows(prompts, tok_index).astype(jnp.bfloat16), after(silu_vec, sends[0])
    ).astype(jnp.bfloat16)
    mod_part = jnp.dot(silu_vec, w_mod, preferred_element_type=jnp.float32)

    cosine, sine_table, bias = tables(
        jnp.stack([tok_index, mlp_index]).astype(jnp.int32),
        text_len[0],
        after(slot_token, mod_part).reshape(-1, rows_dev),
        head_size,
    )
    tables_done = bias
    bias = bias.reshape(1, -1)

    wq_own = jnp.transpose(w_qkv[0], (1, 0, 2))
    wu_own, wa_own, wm_own = w_mlp_in[0], w_attn_out[0], w_mlp_out[0]
    wq_other = xor_swap(wq_own, "cfg", 1)
    wu_other = xor_swap(after(wu_own, wq_other, sends[0]), "cfg", 1)
    gain = qk_gain[0]

    states_0, states_1 = sends[0], xor_swap(sends[1], "tok", 1)
    by_x, by_y = xor_swap(states_0, "mlp", 1), xor_swap(states_0, "mlp", 2)
    order = xor_rows(4 * prompts, 4 * tok_index + mlp_index)
    mods = jnp.stack([mod_part[0::2], xor_swap(after(mod_part[1::2], wq_other), "tok", 1)], 1)
    mods = jnp.concatenate([mods[0], xor_swap(after(mods[1], tables_done), "tok", 2)], 0)
    mods = jnp.stack([mods, xor_swap(after(mods, by_x, by_y, states_1), "mlp", 1)], 1)
    cut = rows_dev // 2
    far_top, far_low = xor_swap(by_x[:cut], "mlp", 2), xor_swap(by_y[cut:], "mlp", 1)
    mods = jnp.concatenate([mods, xor_swap(after(mods, far_top, far_low, wu_other), "mlp", 2)], 1)
    mods = jnp.dot(
        order.astype(jnp.float32), mods.reshape(order.shape[0], -1), precision=lax.Precision.HIGHEST
    )
    shift_mod, scale_mod, gate_mod, final_shift, final_scale = jnp.split(
        mods.reshape(1, 5 * model_width), 5, 1
    )
    scale_mod = 1.0 + scale_mod
    final_scale = 1.0 + final_scale

    wm_other = xor_swap(after(wm_own, shift_mod), "cfg", 1)

    own, queries, keys, values, acts = [], [], [], [], []
    done = (far_top, far_low, shift_mod)
    for j in range(prompts):
        if j == 0:
            states, far = states_0, jnp.concatenate([far_top, far_low], 0)
        else:
            states = states_1 if j == 1 else xor_swap(after(sends[j], own[-1], *queries[: j - 2]), "tok", j)
            send = after(states, *done)
            by_x, by_y, far = [xor_swap(send, "mlp", k) for k in (1, 2, 3)]
        own.append(states)
        q, k, v, act = project(
            half,
            (states, by_x, by_y, far),
            shift_mod,
            scale_mod,
            cosine[j],
            sine_table[j],
            gain,
            wq_own,
            wq_other,
            wu_own,
            wu_other,
        )
        queries.append(q)
        keys.append(k)
        values.append(v)
        acts.append(act)
        if j == 1:
            wa_other = xor_swap(after(wa_own, q, wm_other), "cfg", 1)
        if j:
            done = (queries[j - 1], by_x, by_y, far) + ((wm_other,) if j == 2 else ())

    streams, speeds, marks, parts = ([None] * prompts for _ in range(4))

    def first_step(j, *done):
        p0, p1, p2, p3 = parts[j]
        p3 = after(p3, *done)
        if j == 0:
            top, low = xor_swap(p3[:cut], "mlp", 1), xor_swap(p3[cut:], "mlp", 2)
        elif j % 2:
            top, low = xor_swap(p3, "mlp", 1), None
        else:
            top, low = None, xor_swap(p3, "mlp", 2)
        parts[j] = (p0, p1, p2, top, low)

    def second_step(j, *done):
        p0, p1, p2, top, low = parts[j]
        if j == 0:
            low = after(low, *done)
            p1 = jnp.concatenate([p1[:cut], add(p1[cut:], low)], 0)
            p2 = jnp.concatenate([add(p2[:cut], top), p2[cut:]], 0)
        elif j % 2:
            p2 = add(p2, after(top, *done))
            p1 = after(p1, p2)
        else:
            p1 = add(p1, after(low, *done))
            p2 = after(p2, p1)
        parts[j] = (p0, [xor_swap(p1, "mlp", 1), xor_swap(p2, "mlp", 2)])
        return p2 if j % 2 else p1

    def sum_up(j, *done):
        p0, terms = parts[j]
        outs = finish(
            [after(p0, *done), *terms],
            own[j],
            gate_mod,
            final_shift,
            final_scale,
            w_final.T,
            packed=j > 0,
        )
        marks[j] = outs[0]
        if j:
            gone = xor_swap(outs[0], "tok", j)
            streams[j] = gone[:, :model_width]
            high, low = jnp.split(gone[:, model_width:].astype(jnp.float32), 2, 1)
            speeds[j] = high + low
        else:
            streams[j], speeds[j] = outs

    done = ()
    for j in reversed(range(prompts)):
        parts[j] = combine(
            half,
            bias,
            after(queries[j], *done),
            keys,
            values,
            acts[j],
            wa_own,
            wa_other,
            wm_own,
            wm_other,
        )
        done = (parts[j][0],)
        if j == 0:
            break
        sent = (second_step(j + 1, *done),) if j + 1 < prompts else ()
        if j + 2 < prompts:
            sum_up(j + 2, *done)
            done += (marks[j + 2],)
        first_step(j, *sent)
        done += sent
    first_step(0, *parts[2][1])
    sum_up(2, *done)
    sent = second_step(1, marks[2])
    second_step(0, sent)
    sum_up(1, sent)
    sum_up(0, marks[1])

    stream = from_xor_order(jnp.stack(streams, 1), 1, tok_index, 2)
    half_velocity = from_xor_order(jnp.stack(speeds, 1), 1, tok_index, 2)
    own_first = (tok_index * 4 + mlp_index) * rows_dev
    own_tokens = lax.dynamic_slice_in_dim(slot_token, own_first, rows_dev, 1).T
    half_velocity = jnp.where((own_tokens >= TXT)[:, :, None], half_velocity, 0.0)
    return guided(half_velocity, half_index, latents, step_index, guidance) + (stream[None],)


def guided(half_velocity, half_index, latents, step_index, guidance):
    channel_half = latents.shape[2]
    own_part = lax.dynamic_slice_in_dim(half_velocity, half_index * channel_half, channel_half, 2)
    sent_part = lax.dynamic_slice_in_dim(
        half_velocity, (1 - half_index) * channel_half, channel_half, 2
    )
    partner = xor_swap(sent_part, "cfg", 1)
    first_half = half_index == 0
    cond_part = jnp.where(first_half, own_part, partner)
    uncond_part = jnp.where(first_half, partner, own_part)
    velocity = uncond_part + guidance[0] * (cond_part - uncond_part)
    current = step_index[0].astype(jnp.float32)
    step_size = sigma_at(current + 1.0, STEPS) - sigma_at(current, STEPS)
    return (velocity, latents + step_size * velocity)


def fits_by_prompt(mesh):
    return mesh.shape["cfg"] == 2 and mesh.shape["tok"] == PROMPTS and mesh.shape["mlp"] == 4


def solution(mesh):
    return jax.shard_map(
        by_prompt if fits_by_prompt(mesh) else on_device,
        mesh=mesh,
        in_specs=(
            P("cfg", ("tok", "mlp"), None, None),
            P(("tok", "mlp"), None, "cfg"),
            P("cfg", None, None),
            P(),
            P("cfg", None),
            P(),
            P(),
            P(None, ("tok", "mlp")),
            P(None, "cfg", None, "mlp"),
            P(None, "cfg", "mlp"),
            P(),
            P(None, "mlp", "cfg"),
            P(None, "mlp", "cfg"),
            P(),
        ),
        out_specs=(
            P(("tok", "mlp"), None, "cfg"),
            P(("tok", "mlp"), None, "cfg"),
            P("cfg", ("tok", "mlp"), None, None),
        ),
        check_vma=False,
    )
```

```python
import functools
import math

import jax
import jax.numpy as jnp
import numpy as np
from jax import lax
from jax.experimental import pallas as pl
from jax.experimental.pallas import tpu as pltpu
from jax.sharding import PartitionSpec as P

LAYERS = 1
SIDE = 32
TXT = 512
STEPS = 28
PROMPTS = 4


EPSILON = 1e-06
ROPE_BASE = 10000.0
TIME_SHIFT = 3.0


def xor_swap(value, axis, apart):
    return lax.ppermute(value, axis, [(i, i ^ apart) for i in range(lax.axis_size(axis))])


def layer_norm(values):
    average = jnp.mean(values, axis=-1, keepdims=True)
    centred = values - average
    spread = jnp.mean(centred * centred, axis=-1, keepdims=True)
    return centred * lax.rsqrt(spread + EPSILON)


def rms_norm(values, gains):
    return values * lax.rsqrt(jnp.mean(values * values, axis=-1, keepdims=True) + EPSILON) * gains


def rope_table(tokens, head_size, text_count, side_count):
    pair_count = head_size // 2
    first_pairs = head_size // 16
    axis_pairs = (head_size - head_size // 8) // 4
    pair_index = jnp.arange(pair_count).astype(jnp.float32)
    in_rows = (pair_index >= first_pairs) & (pair_index < first_pairs + axis_pairs)
    in_cols = pair_index >= first_pairs + axis_pairs
    log_base = math.log(ROPE_BASE)
    freq_rows = jnp.where(
        in_rows, jnp.exp(-log_base * (pair_index - first_pairs) / axis_pairs), 0.0
    )
    freq_cols = jnp.where(
        in_cols, jnp.exp(-log_base * (pair_index - first_pairs - axis_pairs) / axis_pairs), 0.0
    )
    is_image = tokens >= text_count
    image_pos = jnp.where(is_image, tokens - text_count, 0)
    row_pos = (image_pos // side_count).astype(jnp.float32)
    col_pos = (image_pos % side_count).astype(jnp.float32)
    angles = row_pos[..., None] * freq_rows + col_pos[..., None] * freq_cols
    return (jnp.cos(angles), jnp.sin(angles))


def apply_rope(values, cosine, sine_table):
    even_part = values[..., 0::2]
    odd_part = values[..., 1::2]
    return jnp.concatenate(
        [even_part * cosine - odd_part * sine_table, even_part * sine_table + odd_part * cosine],
        axis=-1,
    )


def sigma_at(position, steps_total):
    remain = 1.0 - position / steps_total
    return TIME_SHIFT * remain / (1.0 + (TIME_SHIFT - 1.0) * remain)


def on_device(
    hidden,
    latents,
    vec,
    slot_token,
    text_len,
    step_index,
    guidance,
    w_mod,
    w_qkv,
    w_mlp_in,
    qk_gain,
    w_attn_out,
    w_mlp_out,
    w_final,
):
    rows_dev = hidden.shape[1]
    prompts = hidden.shape[2]
    model_width = hidden.shape[3]
    head_size = qk_gain.shape[-1]
    mlp_count = lax.axis_size("mlp")
    tile_rows = rows_dev * mlp_count
    tok_index = lax.axis_index("tok")
    mlp_index = lax.axis_index("mlp")
    half_index = lax.axis_index("cfg")
    stream = hidden[0]
    silu_vec = jax.nn.silu(vec[0]).astype(jnp.bfloat16)
    mod_part = jnp.dot(silu_vec, w_mod, preferred_element_type=jnp.float32)
    modulation = lax.all_gather(mod_part, ("tok", "mlp"), axis=1, tiled=True)
    key_valid = ((slot_token >= TXT) | (slot_token < text_len[0][:, None])).astype(jnp.float32)
    tile_tokens = lax.dynamic_slice_in_dim(slot_token, tok_index * tile_rows, tile_rows, 1).T
    cosine, sine_table = rope_table(tile_tokens, head_size, TXT, SIDE)
    shift_mod = modulation[:, 0:model_width]
    scale_mod = modulation[:, model_width : 2 * model_width]
    gate_mod = modulation[:, 2 * model_width : 3 * model_width]
    normed = (
        layer_norm(stream.astype(jnp.float32)) * (1.0 + scale_mod[None]) + shift_mod[None]
    ).astype(jnp.bfloat16)
    tile_input = lax.all_gather(normed, "mlp", axis=0, tiled=True)
    qkv_weight = w_qkv[0]
    unit_weight = w_mlp_in[0]
    qkv_cols = qkv_weight.shape[1] * qkv_weight.shape[2]
    pieces = (
        lax.all_gather(qkv_weight, "cfg", axis=0, tiled=True),
        lax.all_gather(unit_weight, "cfg", axis=0, tiled=True),
    )
    number = pieces[0].shape[0]
    qkv_piece = pieces[0].reshape(number, qkv_cols)
    qkv_pre = jnp.einsum("tpd,dk->tpk", tile_input, qkv_piece, preferred_element_type=jnp.float32)
    unit_pre = jnp.einsum("tpd,dk->tpk", tile_input, pieces[1], preferred_element_type=jnp.float32)
    heads_dev = qkv_weight.shape[2] // head_size
    projected = qkv_pre.reshape(tile_rows, prompts, 3, heads_dev, head_size)
    queries = apply_rope(
        rms_norm(projected[:, :, 0], qk_gain[0, 0]), cosine[:, :, None], sine_table[:, :, None]
    ).astype(jnp.bfloat16)
    keys_rot = apply_rope(
        rms_norm(projected[:, :, 1], qk_gain[0, 1]), cosine[:, :, None], sine_table[:, :, None]
    ).astype(jnp.bfloat16)
    values = projected[:, :, 2].astype(jnp.bfloat16)
    activation = jax.nn.gelu(unit_pre, approximate=True).astype(jnp.bfloat16)
    keys_piece = lax.all_gather(keys_rot, "tok", axis=0, tiled=True)
    values_piece = lax.all_gather(values, "tok", axis=0, tiled=True)
    scores = jnp.einsum(
        "sphe,tphe->phst", queries, keys_piece, preferred_element_type=jnp.float32
    ) / math.sqrt(head_size)
    softened = jnp.exp(scores) * key_valid[:, None, None, :]
    numerator = jnp.einsum(
        "phst,tphe->sphe",
        softened.astype(jnp.bfloat16),
        values_piece,
        preferred_element_type=jnp.float32,
    )
    numerator, denominator = (numerator, jnp.sum(softened, axis=-1))
    attended = (numerator / jnp.transpose(denominator, (2, 0, 1))[..., None]).astype(jnp.bfloat16)
    attended = attended.reshape(tile_rows, prompts, heads_dev * head_size)
    out_attn = lax.all_gather(w_attn_out[0], "cfg", axis=1, tiled=True)
    out_units = lax.all_gather(w_mlp_out[0], "cfg", axis=1, tiled=True)
    branch_out = lax.psum_scatter(
        (
            jnp.einsum("tpk,kd->tpd", attended, out_attn, preferred_element_type=jnp.float32)
            + jnp.einsum("tpk,kd->tpd", activation, out_units, preferred_element_type=jnp.float32)
        ).astype(jnp.bfloat16),
        "mlp",
        scatter_dimension=0,
        tiled=True,
    ).astype(jnp.float32)
    stream = (stream.astype(jnp.float32) + gate_mod[None] * branch_out).astype(jnp.bfloat16)
    final_lo = 3 * LAYERS * model_width
    final_shift = modulation[:, final_lo : final_lo + model_width]
    final_scale = modulation[:, final_lo + model_width : final_lo + 2 * model_width]
    final_normed = (
        layer_norm(stream.astype(jnp.float32)) * (1.0 + final_scale[None]) + final_shift[None]
    ).astype(jnp.bfloat16)
    own_first = (tok_index * mlp_count + mlp_index) * rows_dev
    own_tokens = lax.dynamic_slice_in_dim(slot_token, own_first, rows_dev, 1).T
    half_velocity = jnp.einsum(
        "rpd,dc->rpc", final_normed, w_final, preferred_element_type=jnp.float32
    )
    half_velocity = jnp.where((own_tokens >= TXT)[:, :, None], half_velocity, 0.0)
    return guided(half_velocity, half_index, latents, step_index, guidance) + (stream[None],)


VMEM_BYTES = 63 * 1024 * 1024
TILE = 512
SLOTS = 3
ANY = pl.BlockSpec(memory_space=pl.ANY)
VMEM = pl.BlockSpec(memory_space=pltpu.VMEM)
SMEM = pl.BlockSpec(memory_space=pltpu.SMEM)


def kernel_params():
    return pltpu.CompilerParams(vmem_limit_bytes=VMEM_BYTES)


def flip_by_bit(values, axis, bit):
    return jnp.where(bit, jnp.flip(values, axis), values)


def from_xor_order(values, axis, index, bits):
    shape = values.shape
    split = shape[:axis] + (2,) * bits + shape[axis + 1 :]
    values = values.reshape(split)
    for place in range(bits):
        bit = (index >> (bits - 1 - place)) & 1
        values = flip_by_bit(values, axis + place, bit == 1)
    return values.reshape(shape)


def xor_rows(count, index):
    places = jnp.arange(count)
    return (places[:, None] ^ index) == places[None, :]


def pick_kernel(place_ref, *refs):
    count = len(refs) // 2
    for j in range(count):
        refs[count + j][...] = refs[j][0]


def pick(place, states):
    count, rows, width = states.shape
    take = lambda j: lambda i, s: (s[0] ^ j, i, 0)
    return pl.pallas_call(
        pick_kernel,
        out_shape=(jax.ShapeDtypeStruct((rows, width), states.dtype),) * count,
        grid_spec=pltpu.PrefetchScalarGridSpec(
            num_scalar_prefetch=1,
            grid=(2,),
            in_specs=[pl.BlockSpec((1, rows // 2, width), take(j)) for j in range(count)],
            out_specs=[pl.BlockSpec((rows // 2, width), lambda i, s: (i, 0))] * count,
        ),
        compiler_params=kernel_params(),
        cost_estimate=pl.CostEstimate(flops=0, bytes_accessed=4 * states.size, transcendentals=0),
        name="pick",
    )(place, *([states] * count))


def tables_kernel(place_ref, len_ref, tokens, freqs, bias, *outs):
    tok, mlp = place_ref[0], place_ref[1]
    own_len = len_ref[tok].astype(jnp.float32)
    blocks, rows = bias.shape
    wide = tokens.shape[1]
    odd = (lax.broadcasted_iota(jnp.int32, (rows, wide), 1) & 1) == 1

    def block(cosine, sine, chunk, index):
        source = tok * blocks + (tok ^ chunk) * 4 + (mlp ^ index)
        token = tokens[pl.ds(source, 1), :].astype(jnp.float32)
        seen = (token >= TXT) | (token < own_len)
        bias[pl.ds(chunk * 4 + index, 1), :] = jnp.where(seen, 0.0, -1e30)[:, :rows]
        place = jnp.where(token >= TXT, token - TXT, 0.0)
        row = jnp.floor(place * (1.0 / SIDE))
        down = lambda values: jnp.transpose(jnp.broadcast_to(values, (wide, wide)))[:rows]
        angles = down(row) * freqs[0:1, :] + down(place - row * SIDE) * freqs[1:2, :]
        to = pl.ds(pl.multiple_of(index * rows, 16), rows)
        cosine[to, :] = jnp.cos(angles)
        turned = jnp.sin(angles)
        sine[to, :] = jnp.where(odd, turned, -turned)

    count = len(outs) // 2
    for chunk in range(count):
        pl.loop(0, 4)(functools.partial(block, outs[chunk], outs[count + chunk], chunk))


def tables(place, text_len, tokens, head):
    chunks = text_len.shape[0]
    blocks, rows = tokens.shape[0] // chunks, tokens.shape[1]
    first, count = head // 16, (head - head // 8) // 4
    pair = np.arange(head) // 2
    rates = [
        np.where(
            (pair >= lo) & (pair < lo + count), np.exp(-math.log(ROPE_BASE) * (pair - lo) / count), 0.0
        )
        for lo in (first, first + count)
    ]
    freqs = jnp.asarray(np.stack(rates).astype(np.float32))
    table = jax.ShapeDtypeStruct((4 * rows, head), jnp.float32)
    bias, *outs = pl.pallas_call(
        tables_kernel,
        out_shape=(jax.ShapeDtypeStruct((blocks, rows), jnp.float32),) + (table,) * (2 * chunks),
        in_specs=[SMEM, SMEM, VMEM, VMEM],
        compiler_params=kernel_params(),
        cost_estimate=pl.CostEstimate(
            flops=100 * blocks * rows * head,
            bytes_accessed=8 * blocks * rows * head,
            transcendentals=2 * blocks * rows * head,
        ),
        name="tables",
    )(place, text_len, jnp.pad(tokens, ((0, 0), (0, head - rows))), freqs)
    return outs[:chunks], outs[chunks:], bias


def project_kernel(
    half_ref,
    shift,
    scale,
    cos_ref,
    sin_ref,
    gain,
    x0,
    x1,
    x2,
    x3,
    wq_own,
    wq_other,
    wu_own,
    wu_other,
    q_out,
    k_out,
    v_out,
    act_out,
    landed,
    normed,
    held,
    ready,
    x_sem,
    w_sem,
    out_sem,
):
    half = half_ref[0]
    depth = wu_own.shape[0]
    head = gain.shape[1]
    pieces = (x0, x1, x2, x3)
    rows = x0.shape[0]
    units = wu_own.shape[1] // TILE

    def weights(column, slot):
        return [
            pltpu.make_async_copy(
                ref.at[:, pl.ds(column, TILE)], held.at[slot, side], w_sem.at[slot, side]
            )
            for side, ref in enumerate((wu_own, wu_other))
        ]

    def head_weights(part):
        return [
            pltpu.make_async_copy(ref.at[part], held.at[part, side], w_sem.at[part, side])
            for side, ref in enumerate((wq_own, wq_other))
        ]

    def result(out, column, slot):
        return pltpu.make_async_copy(
            ready.at[slot], out.at[:, pl.ds(column, TILE)], out_sem.at[slot]
        )

    loads = [pltpu.make_async_copy(ref, landed.at[i], x_sem.at[i]) for i, ref in enumerate(pieces)]
    loads[0].start()
    for copy in head_weights(0):
        copy.start()
    for load in loads[1:]:
        load.start()
    for part in (1, 2):
        for copy in head_weights(part):
            copy.start()

    for index, load in enumerate(loads):
        load.wait()
        block = layer_norm(landed[index].astype(jnp.float32))
        block = (block * scale[...] + shift[...]).astype(jnp.bfloat16)
        normed[0, index * rows : (index + 1) * rows, :] = block[:, :depth]
        normed[1, index * rows : (index + 1) * rows, :] = block[:, depth:]

    even = (lax.broadcasted_iota(jnp.int32, cos_ref.shape, 1) & 1) == 0

    def product(slot):
        return jnp.dot(
            normed[half], held[slot, 0], preferred_element_type=jnp.float32
        ) + jnp.dot(normed[1 - half], held[slot, 1], preferred_element_type=jnp.float32)

    for part, out in enumerate((q_out, k_out, v_out)):
        for copy in head_weights(part):
            copy.wait()
        values = product(part)
        if part == 2:
            result(out, 0, 0).wait()
            ready[0] = values.astype(jnp.bfloat16)
        else:
            for lo in range(0, TILE, head):
                turned = rms_norm(values[:, lo : lo + head], gain[part : part + 1, :])
                partner = jnp.where(even, pltpu.roll(turned, head - 1, 1), pltpu.roll(turned, 1, 1))
                turned = turned * cos_ref[...] + partner * sin_ref[...]
                ready[part, :, lo : lo + head] = turned.astype(jnp.bfloat16)
        result(out, 0, part % 2).start()
        for copy in weights(part * TILE, part):
            copy.start()

    @pl.loop(0, units)
    def _(index):
        slot = lax.rem(index, SLOTS)
        to = lax.rem(index + 1, 2)
        column = pl.multiple_of(index * TILE, TILE)
        for copy in weights(column, slot):
            copy.wait()
        values = jax.nn.gelu(product(slot), approximate=True).astype(jnp.bfloat16)
        result(act_out, column, to).wait()
        ready[to] = values
        result(act_out, column, to).start()

        @pl.when(index + SLOTS < units)
        def _():
            later = pl.multiple_of((index + SLOTS) * TILE, TILE)
            for copy in weights(later, slot):
                copy.start()

    for slot in range(2):
        result(act_out, 0, slot).wait()


def project(half, pieces, shift, scale, cos_rows, sin_rows, gain, wq_own, wq_other, wu_own, wu_other):
    rows = sum(piece.shape[0] for piece in pieces)
    width = pieces[0].shape[1]
    depth = wu_own.shape[0]
    units = wu_own.shape[1]
    head_out = jax.ShapeDtypeStruct((rows, TILE), jnp.bfloat16)
    return pl.pallas_call(
        project_kernel,
        out_shape=(head_out, head_out, head_out, jax.ShapeDtypeStruct((rows, units), jnp.bfloat16)),
        in_specs=[SMEM] + [VMEM] * 5 + [ANY] * 8,
        out_specs=[ANY] * 4,
        scratch_shapes=[
            pltpu.VMEM((len(pieces), rows // len(pieces), width), jnp.bfloat16),
            pltpu.VMEM((2, rows, depth), jnp.bfloat16),
            pltpu.VMEM((SLOTS, 2, depth, TILE), jnp.bfloat16),
            pltpu.VMEM((2, rows, TILE), jnp.bfloat16),
            pltpu.SemaphoreType.DMA((len(pieces),)),
            pltpu.SemaphoreType.DMA((SLOTS, 2)),
            pltpu.SemaphoreType.DMA((2,)),
        ],
        compiler_params=kernel_params(),
        cost_estimate=pl.CostEstimate(
            flops=2 * rows * width * (3 * TILE + units),
            bytes_accessed=2 * width * (3 * TILE + units) + 2 * rows * (width + 3 * TILE + units),
            transcendentals=rows * units,
        ),
        name="project",
    )(half, shift, scale, cos_rows, sin_rows, gain, *pieces, wq_own, wq_other, wu_own, wu_other)


def combine_kernel(
    half_ref,
    bias,
    q,
    k0,
    k1,
    k2,
    k3,
    v0,
    v1,
    v2,
    v3,
    act,
    wa_own,
    wa_other,
    wm_own,
    wm_other,
    *refs,
):
    outs = refs[:-8]
    attended, units, held_a, held_m, ready, act_sem, w_sem, out_sem = refs[-8:]
    half = half_ref[0]
    keys, values = (k0, k1, k2, k3), (v0, v1, v2, v3)
    rows = q.shape[0]
    size = k0.shape[0]
    head = 128
    steps = wa_own.shape[1] // TILE

    def weights(wa, wm, column, slot):
        return [
            pltpu.make_async_copy(wa.at[:, pl.ds(column, TILE)], held_a.at[slot], w_sem.at[slot, 0]),
            pltpu.make_async_copy(wm.at[:, pl.ds(column, TILE)], held_m.at[slot], w_sem.at[slot, 1]),
        ]

    def results(column, slot):
        copies, first = [], 0
        for i, out in enumerate(outs):
            copies.append(
                pltpu.make_async_copy(
                    ready.at[slot, pl.ds(first, out.shape[0])],
                    out.at[:, pl.ds(column, TILE)],
                    out_sem.at[slot, i],
                )
            )
            first += out.shape[0]
        return copies

    load = pltpu.make_async_copy(act, units, act_sem)
    load.start()
    for slot in range(SLOTS):
        for copy in weights(wa_own, wm_own, slot * TILE, slot):
            copy.start()

    @pl.loop(0, q.shape[1] // head)
    def _(index):
        lanes = pl.ds(pl.multiple_of(index * head, head), head)
        total = jnp.zeros((rows, 1), jnp.float32)
        numerator = jnp.zeros((rows, head), jnp.float32)
        for part in range(len(keys)):
            scores = lax.dot_general(
                q[:, lanes],
                keys[part][:, lanes],
                (((1,), (1,)), ((), ())),
                preferred_element_type=jnp.float32,
            )
            soft = jnp.exp(
                scores * (1.0 / math.sqrt(head)) + bias[:, part * size : (part + 1) * size]
            )
            total += jnp.sum(soft, axis=-1, keepdims=True)
            numerator += jnp.dot(
                soft.astype(jnp.bfloat16), values[part][:, lanes], preferred_element_type=jnp.float32
            )
        attended[:, lanes] = (numerator / total).astype(jnp.bfloat16)

    load.wait()

    def write(index, slot, column, first, wa, wm):
        for copy in weights(wa, wm, 0, slot):
            copy.wait()
        partial = jnp.dot(attended[...], held_a[slot], preferred_element_type=jnp.float32)
        partial += jnp.dot(units[...], held_m[slot], preferred_element_type=jnp.float32)
        to = lax.rem(index, 2)

        @pl.when(index >= 2)
        def _():
            for copy in results(0, to):
                copy.wait()

        ready[to] = partial.astype(jnp.bfloat16)
        for copy in results(column, to):
            copy.start()

    @pl.loop(0, 2 * steps)
    def _(index):
        slot = lax.rem(index, SLOTS)
        place = lax.rem(index + steps * half, 2 * steps)
        write(index, slot, pl.multiple_of(place * TILE, TILE), 0, wa_own, wm_own)

        @pl.when(index + SLOTS < 2 * steps)
        def _():
            later = pl.multiple_of((index + SLOTS - steps) * TILE, TILE)
            for copy in weights(wa_other, wm_other, later, slot):
                copy.start()

    for slot in range(2):
        for copy in results(0, slot):
            copy.wait()


def combine(half, bias, q, keys, values, act, wa_own, wa_other, wm_own, wm_other, out_rows):
    rows, heads = q.shape
    units = act.shape[1]
    slots = bias.shape[1]
    half_cols = wa_own.shape[1]
    assert half_cols == SLOTS * TILE
    pieces = len(keys)
    parts = [jax.ShapeDtypeStruct((n, 2 * half_cols), jnp.bfloat16) for n in out_rows]
    return pl.pallas_call(
        combine_kernel,
        out_shape=tuple(parts),
        in_specs=[SMEM] + [VMEM] * (2 + 2 * pieces) + [ANY] * 5,
        out_specs=[ANY] * len(parts),
        scratch_shapes=[
            pltpu.VMEM((rows, heads), jnp.bfloat16),
            pltpu.VMEM((rows, units), jnp.bfloat16),
            pltpu.VMEM((SLOTS, heads, TILE), jnp.bfloat16),
            pltpu.VMEM((SLOTS, units, TILE), jnp.bfloat16),
            pltpu.VMEM((2, rows, TILE), jnp.bfloat16),
            pltpu.SemaphoreType.DMA,
            pltpu.SemaphoreType.DMA((SLOTS, 2)),
            pltpu.SemaphoreType.DMA((2, len(parts))),
        ],
        compiler_params=kernel_params(),
        cost_estimate=pl.CostEstimate(
            flops=4 * rows * (heads + units) * half_cols + 4 * rows * slots * heads,
            bytes_accessed=4 * (heads + units) * half_cols + 2 * rows * (heads + units + 2 * half_cols),
            transcendentals=rows * slots * heads // 128,
        ),
        name="combine",
    )(half, bias, q, *keys, *values, act, wa_own, wa_other, wm_own, wm_other)


def finish_kernel(*refs, terms, packed):
    parts, refs = refs[: 1 + terms], refs[1 + terms :]
    states, gate, shift, scale, w_final, *outs = refs
    branch = parts[0][...].astype(jnp.float32)
    for part in parts[1:]:
        branch = branch + part[...].astype(jnp.float32)
    stream = (states[...].astype(jnp.float32) + gate[...] * branch).astype(jnp.bfloat16)
    normed = (layer_norm(stream.astype(jnp.float32)) * scale[...] + shift[...]).astype(jnp.bfloat16)
    speed = lax.dot_general(
        normed, w_final[...], (((1,), (1,)), ((), ())), preferred_element_type=jnp.float32
    )
    width = stream.shape[1]
    outs[0][:, :width] = stream
    if packed:
        high = speed.astype(jnp.bfloat16)
        low = (speed - high.astype(jnp.float32)).astype(jnp.bfloat16)
        outs[0][:, width:] = jnp.concatenate([high, low], 1)
    else:
        outs[1][...] = speed


def finish(parts, states, gate, shift, scale, w_final, packed):
    rows, width = states.shape
    channels = w_final.shape[0]
    steps = 2
    by_rows = lambda cols: pl.BlockSpec((rows // steps, cols), lambda i: (i, 0))
    whole = lambda array: pl.BlockSpec(array.shape, lambda i: (0, 0))
    if packed:
        out_shape = (jax.ShapeDtypeStruct((rows, width + 2 * channels), jnp.bfloat16),)
    else:
        out_shape = (
            jax.ShapeDtypeStruct((rows, width), jnp.bfloat16),
            jax.ShapeDtypeStruct((rows, channels), jnp.float32),
        )
    return pl.pallas_call(
        functools.partial(finish_kernel, terms=len(parts) - 1, packed=packed),
        out_shape=out_shape,
        grid=(steps,),
        in_specs=[by_rows(width)] * (len(parts) + 1) + [whole(a) for a in (gate, shift, scale, w_final)],
        out_specs=[by_rows(out.shape[1]) for out in out_shape],
        compiler_params=kernel_params(),
        cost_estimate=pl.CostEstimate(
            flops=2 * states.size * channels,
            bytes_accessed=2 * states.size * (len(parts) + 2),
            transcendentals=0,
        ),
        name="finish",
    )(*parts, states, gate, shift, scale, w_final)


def add(left, right):
    return (left.astype(jnp.float32) + right.astype(jnp.float32)).astype(jnp.bfloat16)


def after(values, *done):
    return lax.optimization_barrier((values, *done))[0]


def by_prompt(
    hidden,
    latents,
    vec,
    slot_token,
    text_len,
    step_index,
    guidance,
    w_mod,
    w_qkv,
    w_mlp_in,
    qk_gain,
    w_attn_out,
    w_mlp_out,
    w_final,
):
    rows_dev, prompts, model_width = hidden.shape[1:]
    head_size = qk_gain.shape[-1]
    tok_index = lax.axis_index("tok")
    mlp_index = lax.axis_index("mlp")
    half_index = lax.axis_index("cfg")
    half = half_index[None].astype(jnp.int32)

    silu_vec = jax.nn.silu(vec[0]).astype(jnp.bfloat16)
    silu_vec = jnp.dot(xor_rows(prompts, tok_index).astype(jnp.bfloat16), silu_vec).astype(jnp.bfloat16)
    mod_part = jnp.dot(silu_vec, w_mod, preferred_element_type=jnp.float32)
    mod_near = xor_swap(mod_part[1::2], "tok", 1)

    states = jnp.transpose(after(hidden[0], mod_part), (1, 0, 2))
    sends = pick(tok_index[None].astype(jnp.int32), after(states, mod_near))

    cosine, sine_table, bias = tables(
        jnp.stack([tok_index, mlp_index]).astype(jnp.int32),
        text_len[0],
        after(slot_token, sends[0]).reshape(-1, rows_dev),
        head_size,
    )
    tables_done = bias

    wq_own = jnp.transpose(w_qkv[0], (1, 0, 2))
    wu_own, wa_own, wm_own = w_mlp_in[0], w_attn_out[0], w_mlp_out[0]
    wq_other = xor_swap(wq_own, "cfg", 1)
    wu_other = xor_swap(after(wu_own, wq_other, sends[0]), "cfg", 1)
    gain = qk_gain[0]

    states_0, states_1 = sends[0], xor_swap(sends[1], "tok", 1)
    by_x, by_y = xor_swap(states_0, "mlp", 1), xor_swap(states_0, "mlp", 2)
    order = xor_rows(4 * prompts, 4 * tok_index + mlp_index)
    mods = jnp.stack([mod_part[0::2], mod_near], 1)
    mods = jnp.concatenate([mods[0], xor_swap(after(mods[1], sends[0]), "tok", 2)], 0)
    mods = jnp.stack([mods, xor_swap(after(mods, tables_done), "mlp", 1)], 1)
    cut = rows_dev // 2
    far_top, far_low = xor_swap(by_x[:cut], "mlp", 2), xor_swap(by_y[cut:], "mlp", 1)
    mods = jnp.concatenate([mods, xor_swap(after(mods, states_1, by_x, by_y), "mlp", 2)], 1)
    mods = after(mods, far_top, far_low)
    mods = jnp.dot(
        order.astype(jnp.float32), mods.reshape(order.shape[0], -1), precision=lax.Precision.HIGHEST
    )
    shift_mod, scale_mod, gate_mod, final_shift, final_scale = jnp.split(
        mods.reshape(1, 5 * model_width), 5, 1
    )
    scale_mod = 1.0 + scale_mod
    final_scale = 1.0 + final_scale

    wm_other = xor_swap(after(wm_own, shift_mod), "cfg", 1)

    own, queries, keys, values, acts = [], [], [], [], []
    done = (far_top, far_low, shift_mod)
    for j in range(prompts):
        if j == 0:
            states, far = states_0, jnp.concatenate([far_top, far_low], 0)
        else:
            states = states_1 if j == 1 else xor_swap(after(sends[j], own[-1], *queries[: j - 2]), "tok", j)
            send = after(states, *done)
            by_x, by_y, far = [xor_swap(send, "mlp", k) for k in (1, 2, 3)]
        own.append(states)
        q, k, v, act = project(
            half,
            (states, by_x, by_y, far),
            shift_mod,
            scale_mod,
            cosine[j],
            sine_table[j],
            gain,
            wq_own,
            wq_other,
            wu_own,
            wu_other,
        )
        if j == 0:
            bias = after(tables_done, q).reshape(1, -1)
        queries.append(q)
        keys.append(k)
        values.append(v)
        acts.append(act)
        if j == 1:
            wa_other = xor_swap(after(wa_own, q, wm_other), "cfg", 1)
        if j:
            done = (queries[j - 1], by_x, by_y, far) + ((wm_other,) if j == 2 else ())

    streams, speeds, marks, parts = ([None] * prompts for _ in range(4))

    def first_step(j, *done):
        if j == 0:
            p0, p1_top, p1_low, p2_top, p2_low, top, low = parts[0]
            top, low = xor_swap(after(top, *done), "mlp", 1), xor_swap(after(low, *done), "mlp", 2)
            parts[0] = (p0, (p1_top, p1_low), (p2_top, p2_low), top, low)
            return
        p0, p1, p2, p3 = parts[j]
        p3 = after(p3, *done)
        if j % 2:
            top, low = xor_swap(p3, "mlp", 1), None
        else:
            top, low = None, xor_swap(p3, "mlp", 2)
        parts[j] = (p0, p1, p2, top, low)

    def second_step(j, *done):
        p0, p1, p2, top, low = parts[j]
        if j == 0:
            low = after(low, *done)
            p1 = jnp.concatenate([p1[0], add(p1[1], low)], 0)
            p2 = jnp.concatenate([add(p2[0], top), p2[1]], 0)
        elif j % 2:
            p2 = add(p2, after(top, *done))
            p1 = after(p1, p2)
        else:
            p1 = add(p1, after(low, *done))
            p2 = after(p2, p1)
        parts[j] = (p0, [xor_swap(p1, "mlp", 1), xor_swap(p2, "mlp", 2)])
        return p2 if j % 2 else p1

    def sum_up(j, *done):
        p0, terms = parts[j]
        outs = finish(
            [after(p0, *done), *terms],
            own[j],
            gate_mod,
            final_shift,
            final_scale,
            w_final.T,
            packed=j > 0,
        )
        marks[j] = outs[0]
        if j:
            gone = xor_swap(outs[0], "tok", j)
            streams[j] = gone[:, :model_width]
            high, low = jnp.split(gone[:, model_width:].astype(jnp.float32), 2, 1)
            speeds[j] = high + low
        else:
            streams[j], speeds[j] = outs

    done = ()
    for j in reversed(range(prompts)):
        parts[j] = combine(
            half,
            bias,
            after(queries[j], *done),
            keys,
            values,
            acts[j],
            wa_own,
            wa_other,
            wm_own,
            wm_other,
            (rows_dev,) * 4 if j else (rows_dev,) + (cut,) * 6,
        )
        done = (parts[j][0],)
        if j == 0:
            break
        sent = (second_step(j + 1, *done),) if j + 1 < prompts else ()
        if j + 2 < prompts:
            sum_up(j + 2, *done)
            done += (marks[j + 2],)
        first_step(j, *sent)
        done += sent
    first_step(0, *parts[2][1])
    sum_up(2, *done)
    sent = second_step(1, marks[2])
    second_step(0, sent)
    sum_up(1, sent)
    sum_up(0, marks[1])

    stream = from_xor_order(jnp.stack(streams, 1), 1, tok_index, 2)
    half_velocity = from_xor_order(jnp.stack(speeds, 1), 1, tok_index, 2)
    own_first = (tok_index * 4 + mlp_index) * rows_dev
    own_tokens = lax.dynamic_slice_in_dim(slot_token, own_first, rows_dev, 1).T
    half_velocity = jnp.where((own_tokens >= TXT)[:, :, None], half_velocity, 0.0)
    return guided(half_velocity, half_index, latents, step_index, guidance) + (stream[None],)


def guided(half_velocity, half_index, latents, step_index, guidance):
    channel_half = latents.shape[2]
    own_part = lax.dynamic_slice_in_dim(half_velocity, half_index * channel_half, channel_half, 2)
    sent_part = lax.dynamic_slice_in_dim(
        half_velocity, (1 - half_index) * channel_half, channel_half, 2
    )
    partner = xor_swap(sent_part, "cfg", 1)
    first_half = half_index == 0
    cond_part = jnp.where(first_half, own_part, partner)
    uncond_part = jnp.where(first_half, partner, own_part)
    velocity = uncond_part + guidance[0] * (cond_part - uncond_part)
    current = step_index[0].astype(jnp.float32)
    step_size = sigma_at(current + 1.0, STEPS) - sigma_at(current, STEPS)
    return (velocity, latents + step_size * velocity)


def fits_by_prompt(mesh):
    return mesh.shape["cfg"] == 2 and mesh.shape["tok"] == PROMPTS and mesh.shape["mlp"] == 4


def solution(mesh):
    return jax.shard_map(
        by_prompt if fits_by_prompt(mesh) else on_device,
        mesh=mesh,
        in_specs=(
            P("cfg", ("tok", "mlp"), None, None),
            P(("tok", "mlp"), None, "cfg"),
            P("cfg", None, None),
            P(),
            P("cfg", None),
            P(),
            P(),
            P(None, ("tok", "mlp")),
            P(None, "cfg", None, "mlp"),
            P(None, "cfg", "mlp"),
            P(),
            P(None, "mlp", "cfg"),
            P(None, "mlp", "cfg"),
            P(),
        ),
        out_specs=(
            P(("tok", "mlp"), None, "cfg"),
            P(("tok", "mlp"), None, "cfg"),
            P("cfg", ("tok", "mlp"), None, None),
        ),
        check_vma=False,
    )
```

```python
import functools
import math

import jax
import jax.numpy as jnp
import numpy as np
from jax import lax
from jax.experimental import pallas as pl
from jax.experimental.pallas import tpu as pltpu
from jax.sharding import PartitionSpec as P

LAYERS = 1
SIDE = 32
TXT = 512
STEPS = 28
PROMPTS = 4


EPSILON = 1e-06
ROPE_BASE = 10000.0
TIME_SHIFT = 3.0


def xor_swap(value, axis, apart):
    return lax.ppermute(value, axis, [(i, i ^ apart) for i in range(lax.axis_size(axis))])


def layer_norm(values):
    average = jnp.mean(values, axis=-1, keepdims=True)
    centred = values - average
    spread = jnp.mean(centred * centred, axis=-1, keepdims=True)
    return centred * lax.rsqrt(spread + EPSILON)


def rms_norm(values, gains):
    return values * lax.rsqrt(jnp.mean(values * values, axis=-1, keepdims=True) + EPSILON) * gains


def rope_table(tokens, head_size, text_count, side_count):
    pair_count = head_size // 2
    first_pairs = head_size // 16
    axis_pairs = (head_size - head_size // 8) // 4
    pair_index = jnp.arange(pair_count).astype(jnp.float32)
    in_rows = (pair_index >= first_pairs) & (pair_index < first_pairs + axis_pairs)
    in_cols = pair_index >= first_pairs + axis_pairs
    log_base = math.log(ROPE_BASE)
    freq_rows = jnp.where(
        in_rows, jnp.exp(-log_base * (pair_index - first_pairs) / axis_pairs), 0.0
    )
    freq_cols = jnp.where(
        in_cols, jnp.exp(-log_base * (pair_index - first_pairs - axis_pairs) / axis_pairs), 0.0
    )
    is_image = tokens >= text_count
    image_pos = jnp.where(is_image, tokens - text_count, 0)
    row_pos = (image_pos // side_count).astype(jnp.float32)
    col_pos = (image_pos % side_count).astype(jnp.float32)
    angles = row_pos[..., None] * freq_rows + col_pos[..., None] * freq_cols
    return (jnp.cos(angles), jnp.sin(angles))


def apply_rope(values, cosine, sine_table):
    even_part = values[..., 0::2]
    odd_part = values[..., 1::2]
    return jnp.concatenate(
        [even_part * cosine - odd_part * sine_table, even_part * sine_table + odd_part * cosine],
        axis=-1,
    )


def sigma_at(position, steps_total):
    remain = 1.0 - position / steps_total
    return TIME_SHIFT * remain / (1.0 + (TIME_SHIFT - 1.0) * remain)


def on_device(
    hidden,
    latents,
    vec,
    slot_token,
    text_len,
    step_index,
    guidance,
    w_mod,
    w_qkv,
    w_mlp_in,
    qk_gain,
    w_attn_out,
    w_mlp_out,
    w_final,
):
    rows_dev = hidden.shape[1]
    prompts = hidden.shape[2]
    model_width = hidden.shape[3]
    head_size = qk_gain.shape[-1]
    mlp_count = lax.axis_size("mlp")
    tile_rows = rows_dev * mlp_count
    tok_index = lax.axis_index("tok")
    mlp_index = lax.axis_index("mlp")
    half_index = lax.axis_index("cfg")
    stream = hidden[0]
    silu_vec = jax.nn.silu(vec[0]).astype(jnp.bfloat16)
    mod_part = jnp.dot(silu_vec, w_mod, preferred_element_type=jnp.float32)
    modulation = lax.all_gather(mod_part, ("tok", "mlp"), axis=1, tiled=True)
    key_valid = ((slot_token >= TXT) | (slot_token < text_len[0][:, None])).astype(jnp.float32)
    tile_tokens = lax.dynamic_slice_in_dim(slot_token, tok_index * tile_rows, tile_rows, 1).T
    cosine, sine_table = rope_table(tile_tokens, head_size, TXT, SIDE)
    shift_mod = modulation[:, 0:model_width]
    scale_mod = modulation[:, model_width : 2 * model_width]
    gate_mod = modulation[:, 2 * model_width : 3 * model_width]
    normed = (
        layer_norm(stream.astype(jnp.float32)) * (1.0 + scale_mod[None]) + shift_mod[None]
    ).astype(jnp.bfloat16)
    tile_input = lax.all_gather(normed, "mlp", axis=0, tiled=True)
    qkv_weight = w_qkv[0]
    unit_weight = w_mlp_in[0]
    qkv_cols = qkv_weight.shape[1] * qkv_weight.shape[2]
    pieces = (
        lax.all_gather(qkv_weight, "cfg", axis=0, tiled=True),
        lax.all_gather(unit_weight, "cfg", axis=0, tiled=True),
    )
    number = pieces[0].shape[0]
    qkv_piece = pieces[0].reshape(number, qkv_cols)
    qkv_pre = jnp.einsum("tpd,dk->tpk", tile_input, qkv_piece, preferred_element_type=jnp.float32)
    unit_pre = jnp.einsum("tpd,dk->tpk", tile_input, pieces[1], preferred_element_type=jnp.float32)
    heads_dev = qkv_weight.shape[2] // head_size
    projected = qkv_pre.reshape(tile_rows, prompts, 3, heads_dev, head_size)
    queries = apply_rope(
        rms_norm(projected[:, :, 0], qk_gain[0, 0]), cosine[:, :, None], sine_table[:, :, None]
    ).astype(jnp.bfloat16)
    keys_rot = apply_rope(
        rms_norm(projected[:, :, 1], qk_gain[0, 1]), cosine[:, :, None], sine_table[:, :, None]
    ).astype(jnp.bfloat16)
    values = projected[:, :, 2].astype(jnp.bfloat16)
    activation = jax.nn.gelu(unit_pre, approximate=True).astype(jnp.bfloat16)
    keys_piece = lax.all_gather(keys_rot, "tok", axis=0, tiled=True)
    values_piece = lax.all_gather(values, "tok", axis=0, tiled=True)
    scores = jnp.einsum(
        "sphe,tphe->phst", queries, keys_piece, preferred_element_type=jnp.float32
    ) / math.sqrt(head_size)
    softened = jnp.exp(scores) * key_valid[:, None, None, :]
    numerator = jnp.einsum(
        "phst,tphe->sphe",
        softened.astype(jnp.bfloat16),
        values_piece,
        preferred_element_type=jnp.float32,
    )
    numerator, denominator = (numerator, jnp.sum(softened, axis=-1))
    attended = (numerator / jnp.transpose(denominator, (2, 0, 1))[..., None]).astype(jnp.bfloat16)
    attended = attended.reshape(tile_rows, prompts, heads_dev * head_size)
    out_attn = lax.all_gather(w_attn_out[0], "cfg", axis=1, tiled=True)
    out_units = lax.all_gather(w_mlp_out[0], "cfg", axis=1, tiled=True)
    branch_out = lax.psum_scatter(
        (
            jnp.einsum("tpk,kd->tpd", attended, out_attn, preferred_element_type=jnp.float32)
            + jnp.einsum("tpk,kd->tpd", activation, out_units, preferred_element_type=jnp.float32)
        ).astype(jnp.bfloat16),
        "mlp",
        scatter_dimension=0,
        tiled=True,
    ).astype(jnp.float32)
    stream = (stream.astype(jnp.float32) + gate_mod[None] * branch_out).astype(jnp.bfloat16)
    final_lo = 3 * LAYERS * model_width
    final_shift = modulation[:, final_lo : final_lo + model_width]
    final_scale = modulation[:, final_lo + model_width : final_lo + 2 * model_width]
    final_normed = (
        layer_norm(stream.astype(jnp.float32)) * (1.0 + final_scale[None]) + final_shift[None]
    ).astype(jnp.bfloat16)
    own_first = (tok_index * mlp_count + mlp_index) * rows_dev
    own_tokens = lax.dynamic_slice_in_dim(slot_token, own_first, rows_dev, 1).T
    half_velocity = jnp.einsum(
        "rpd,dc->rpc", final_normed, w_final, preferred_element_type=jnp.float32
    )
    half_velocity = jnp.where((own_tokens >= TXT)[:, :, None], half_velocity, 0.0)
    return guided(half_velocity, half_index, latents, step_index, guidance) + (stream[None],)


VMEM_BYTES = 63 * 1024 * 1024
TILE = 512
UNIT_TILE = 1024
OUT_TILE = 768
ANY = pl.BlockSpec(memory_space=pl.ANY)
VMEM = pl.BlockSpec(memory_space=pltpu.VMEM)
SMEM = pl.BlockSpec(memory_space=pltpu.SMEM)


def kernel_params():
    return pltpu.CompilerParams(vmem_limit_bytes=VMEM_BYTES)


def flip_by_bit(values, axis, bit):
    return jnp.where(bit, jnp.flip(values, axis), values)


def from_xor_order(values, axis, index, bits):
    shape = values.shape
    split = shape[:axis] + (2,) * bits + shape[axis + 1 :]
    values = values.reshape(split)
    for place in range(bits):
        bit = (index >> (bits - 1 - place)) & 1
        values = flip_by_bit(values, axis + place, bit == 1)
    return values.reshape(shape)


def xor_rows(count, index):
    places = jnp.arange(count)
    return (places[:, None] ^ index) == places[None, :]


def pick_kernel(place_ref, *refs):
    count = len(refs) // 2
    for j in range(count):
        refs[count + j][...] = refs[j][0]


def pick(place, states):
    count, rows, width = states.shape
    take = lambda j: lambda i, s: (s[0] ^ j, i, 0)
    return pl.pallas_call(
        pick_kernel,
        out_shape=(jax.ShapeDtypeStruct((rows, width), states.dtype),) * count,
        grid_spec=pltpu.PrefetchScalarGridSpec(
            num_scalar_prefetch=1,
            grid=(2,),
            in_specs=[pl.BlockSpec((1, rows // 2, width), take(j)) for j in range(count)],
            out_specs=[pl.BlockSpec((rows // 2, width), lambda i, s: (i, 0))] * count,
        ),
        compiler_params=kernel_params(),
        cost_estimate=pl.CostEstimate(flops=0, bytes_accessed=4 * states.size, transcendentals=0),
        name="pick",
    )(place, *([states] * count))


def tables_kernel(place_ref, len_ref, tokens, freqs, bias, *outs):
    tok, mlp = place_ref[0], place_ref[1]
    own_len = len_ref[tok].astype(jnp.float32)
    blocks, rows = bias.shape
    wide = tokens.shape[1]
    odd = (lax.broadcasted_iota(jnp.int32, (rows, wide), 1) & 1) == 1

    def block(cosine, sine, chunk, index):
        source = tok * blocks + (tok ^ chunk) * 4 + (mlp ^ index)
        token = tokens[pl.ds(source, 1), :].astype(jnp.float32)
        seen = (token >= TXT) | (token < own_len)
        bias[pl.ds(chunk * 4 + index, 1), :] = jnp.where(seen, 0.0, -1e30)[:, :rows]
        place = jnp.where(token >= TXT, token - TXT, 0.0)
        row = jnp.floor(place * (1.0 / SIDE))
        down = lambda values: jnp.transpose(jnp.broadcast_to(values, (wide, wide)))[:rows]
        angles = down(row) * freqs[0:1, :] + down(place - row * SIDE) * freqs[1:2, :]
        to = pl.ds(pl.multiple_of(index * rows, 16), rows)
        cosine[to, :] = jnp.cos(angles)
        turned = jnp.sin(angles)
        sine[to, :] = jnp.where(odd, turned, -turned)

    count = len(outs) // 2
    for chunk in range(count):
        pl.loop(0, 4)(functools.partial(block, outs[chunk], outs[count + chunk], chunk))


def tables(place, text_len, tokens, head):
    chunks = text_len.shape[0]
    blocks, rows = tokens.shape[0] // chunks, tokens.shape[1]
    first, count = head // 16, (head - head // 8) // 4
    pair = np.arange(head) // 2
    rates = [
        np.where(
            (pair >= lo) & (pair < lo + count), np.exp(-math.log(ROPE_BASE) * (pair - lo) / count), 0.0
        )
        for lo in (first, first + count)
    ]
    freqs = jnp.asarray(np.stack(rates).astype(np.float32))
    table = jax.ShapeDtypeStruct((4 * rows, head), jnp.float32)
    bias, *outs = pl.pallas_call(
        tables_kernel,
        out_shape=(jax.ShapeDtypeStruct((blocks, rows), jnp.float32),) + (table,) * (2 * chunks),
        in_specs=[SMEM, SMEM, VMEM, VMEM],
        compiler_params=kernel_params(),
        cost_estimate=pl.CostEstimate(
            flops=100 * blocks * rows * head,
            bytes_accessed=8 * blocks * rows * head,
            transcendentals=2 * blocks * rows * head,
        ),
        name="tables",
    )(place, text_len, jnp.pad(tokens, ((0, 0), (0, head - rows))), freqs)
    return outs[:chunks], outs[chunks:], bias


def project_kernel(
    half_ref,
    shift,
    scale,
    cos_ref,
    sin_ref,
    gain,
    x0,
    x1,
    x2,
    x3,
    wq_own,
    wq_other,
    wu_own,
    wu_other,
    q_out,
    k_out,
    v_out,
    act_out,
    landed,
    normed,
    held,
    held_units,
    ready,
    ready_units,
    x_sem,
    w_sem,
    unit_sem,
    out_sem,
    act_sem,
):
    half = half_ref[0]
    depth = wu_own.shape[0]
    head = gain.shape[1]
    pieces = (x0, x1, x2, x3)
    rows = x0.shape[0]
    units = wu_own.shape[1] // UNIT_TILE

    def unit_weights(index):
        return [
            pltpu.make_async_copy(
                ref.at[:, pl.ds(pl.multiple_of(index * UNIT_TILE, UNIT_TILE), UNIT_TILE)],
                held_units.at[index, side],
                unit_sem.at[index, side],
            )
            for side, ref in enumerate((wu_own, wu_other))
        ]

    def head_weights(part):
        return [
            pltpu.make_async_copy(ref.at[part], held.at[part, side], w_sem.at[part, side])
            for side, ref in enumerate((wq_own, wq_other))
        ]

    def head_result(part):
        out = (q_out, k_out, v_out)[part]
        return pltpu.make_async_copy(ready.at[part], out, out_sem.at[part])

    def unit_result(index, slot):
        column = pl.multiple_of(index * UNIT_TILE, UNIT_TILE)
        return pltpu.make_async_copy(
            ready_units.at[slot], act_out.at[:, pl.ds(column, UNIT_TILE)], act_sem.at[slot]
        )

    loads = [pltpu.make_async_copy(ref, landed.at[i], x_sem.at[i]) for i, ref in enumerate(pieces)]
    loads[0].start()
    for copy in head_weights(0):
        copy.start()
    for load in loads[1:]:
        load.start()
    for part in (1, 2):
        for copy in head_weights(part):
            copy.start()

    for index, load in enumerate(loads):
        load.wait()
        block = layer_norm(landed[index].astype(jnp.float32))
        block = (block * scale[...] + shift[...]).astype(jnp.bfloat16)
        normed[0, index * rows : (index + 1) * rows, :] = block[:, :depth]
        normed[1, index * rows : (index + 1) * rows, :] = block[:, depth:]

    even = (lax.broadcasted_iota(jnp.int32, cos_ref.shape, 1) & 1) == 0

    def product(own, other):
        return jnp.dot(normed[half], own, preferred_element_type=jnp.float32) + jnp.dot(
            normed[1 - half], other, preferred_element_type=jnp.float32
        )

    for part in range(3):
        for copy in head_weights(part):
            copy.wait()
        if part < units:
            for copy in unit_weights(part):
                copy.start()
        values = product(held[part, 0], held[part, 1])
        if part == 2:
            ready[part] = values.astype(jnp.bfloat16)
        else:
            for lo in range(0, TILE, head):
                turned = rms_norm(values[:, lo : lo + head], gain[part : part + 1, :])
                partner = jnp.where(even, pltpu.roll(turned, head - 1, 1), pltpu.roll(turned, 1, 1))
                turned = turned * cos_ref[...] + partner * sin_ref[...]
                ready[part, :, lo : lo + head] = turned.astype(jnp.bfloat16)
        head_result(part).start()

    @pl.loop(0, units)
    def _(index):
        slot = lax.rem(index, 2)
        for copy in unit_weights(index):
            copy.wait()
        values = product(held_units[index, 0], held_units[index, 1])
        values = jax.nn.gelu(values, approximate=True).astype(jnp.bfloat16)

        @pl.when(index >= 2)
        def _():
            unit_result(index, slot).wait()

        ready_units[slot] = values
        unit_result(index, slot).start()

    for part in range(3):
        head_result(part).wait()
    for slot in range(2):
        unit_result(0, slot).wait()


def project(half, pieces, shift, scale, cos_rows, sin_rows, gain, wq_own, wq_other, wu_own, wu_other):
    rows = sum(piece.shape[0] for piece in pieces)
    width = pieces[0].shape[1]
    depth = wu_own.shape[0]
    units = wu_own.shape[1]
    unit_steps = units // UNIT_TILE
    assert unit_steps == 3
    head_out = jax.ShapeDtypeStruct((rows, TILE), jnp.bfloat16)
    return pl.pallas_call(
        project_kernel,
        out_shape=(head_out, head_out, head_out, jax.ShapeDtypeStruct((rows, units), jnp.bfloat16)),
        in_specs=[SMEM] + [VMEM] * 5 + [ANY] * 8,
        out_specs=[ANY] * 4,
        scratch_shapes=[
            pltpu.VMEM((len(pieces), rows // len(pieces), width), jnp.bfloat16),
            pltpu.VMEM((2, rows, depth), jnp.bfloat16),
            pltpu.VMEM((3, 2, depth, TILE), jnp.bfloat16),
            pltpu.VMEM((unit_steps, 2, depth, UNIT_TILE), jnp.bfloat16),
            pltpu.VMEM((3, rows, TILE), jnp.bfloat16),
            pltpu.VMEM((2, rows, UNIT_TILE), jnp.bfloat16),
            pltpu.SemaphoreType.DMA((len(pieces),)),
            pltpu.SemaphoreType.DMA((3, 2)),
            pltpu.SemaphoreType.DMA((unit_steps, 2)),
            pltpu.SemaphoreType.DMA((3,)),
            pltpu.SemaphoreType.DMA((2,)),
        ],
        compiler_params=kernel_params(),
        cost_estimate=pl.CostEstimate(
            flops=2 * rows * width * (3 * TILE + units),
            bytes_accessed=2 * width * (3 * TILE + units) + 2 * rows * (width + 3 * TILE + units),
            transcendentals=rows * units,
        ),
        name="project",
    )(half, shift, scale, cos_rows, sin_rows, gain, *pieces, wq_own, wq_other, wu_own, wu_other)


def combine_kernel(
    half_ref,
    bias,
    q,
    k0,
    k1,
    k2,
    k3,
    v0,
    v1,
    v2,
    v3,
    act,
    wa_own,
    wa_other,
    wm_own,
    wm_other,
    *refs,
):
    outs = refs[:-8]
    attended, units, held_a, held_m, ready, act_sem, w_sem, out_sem = refs[-8:]
    half = half_ref[0]
    keys, values = (k0, k1, k2, k3), (v0, v1, v2, v3)
    rows = q.shape[0]
    size = k0.shape[0]
    head = 128
    steps = wa_own.shape[1] // OUT_TILE

    def weights(tile):
        wa, wm = (wa_own, wm_own) if tile < steps else (wa_other, wm_other)
        columns = pl.ds(tile % steps * OUT_TILE, OUT_TILE)
        return [
            pltpu.make_async_copy(wa.at[:, columns], held_a.at[tile], w_sem.at[tile, 0]),
            pltpu.make_async_copy(wm.at[:, columns], held_m.at[tile], w_sem.at[tile, 1]),
        ]

    def landed(index):
        columns = pl.ds(0, OUT_TILE)
        return [
            pltpu.make_async_copy(wa_own.at[:, columns], held_a.at[index], w_sem.at[index, 0]),
            pltpu.make_async_copy(wm_own.at[:, columns], held_m.at[index], w_sem.at[index, 1]),
        ]

    def results(column, slot):
        copies, first = [], 0
        for i, out in enumerate(outs):
            copies.append(
                pltpu.make_async_copy(
                    ready.at[slot, pl.ds(first, out.shape[0])],
                    out.at[:, pl.ds(column, OUT_TILE)],
                    out_sem.at[slot, i],
                )
            )
            first += out.shape[0]
        return copies

    load = pltpu.make_async_copy(act, units, act_sem)
    load.start()
    for tile in range(steps):
        for copy in weights(tile):
            copy.start()

    @pl.loop(0, q.shape[1] // head)
    def _(index):
        lanes = pl.ds(pl.multiple_of(index * head, head), head)
        total = jnp.zeros((rows, 1), jnp.float32)
        numerator = jnp.zeros((rows, head), jnp.float32)
        for part in range(len(keys)):
            scores = lax.dot_general(
                q[:, lanes],
                keys[part][:, lanes],
                (((1,), (1,)), ((), ())),
                preferred_element_type=jnp.float32,
            )
            soft = jnp.exp(
                scores * (1.0 / math.sqrt(head)) + bias[:, part * size : (part + 1) * size]
            )
            total += jnp.sum(soft, axis=-1, keepdims=True)
            numerator += jnp.dot(
                soft.astype(jnp.bfloat16), values[part][:, lanes], preferred_element_type=jnp.float32
            )
        attended[:, lanes] = (numerator / total).astype(jnp.bfloat16)

    for tile in range(steps, 2 * steps):
        for copy in weights(tile):
            copy.start()
    load.wait()

    @pl.loop(0, 2 * steps)
    def _(index):
        to = lax.rem(index, 2)
        place = lax.rem(index + steps * half, 2 * steps)
        for copy in landed(index):
            copy.wait()
        partial = jnp.dot(attended[...], held_a[index], preferred_element_type=jnp.float32)
        partial += jnp.dot(units[...], held_m[index], preferred_element_type=jnp.float32)

        @pl.when(index >= 2)
        def _():
            for copy in results(0, to):
                copy.wait()

        ready[to] = partial.astype(jnp.bfloat16)
        for copy in results(pl.multiple_of(place * OUT_TILE, OUT_TILE), to):
            copy.start()

    for slot in range(2):
        for copy in results(0, slot):
            copy.wait()


def combine(half, bias, q, keys, values, act, wa_own, wa_other, wm_own, wm_other, out_rows):
    rows, heads = q.shape
    units = act.shape[1]
    slots = bias.shape[1]
    half_cols = wa_own.shape[1]
    tiles = 2 * (half_cols // OUT_TILE)
    pieces = len(keys)
    parts = [jax.ShapeDtypeStruct((n, 2 * half_cols), jnp.bfloat16) for n in out_rows]
    return pl.pallas_call(
        combine_kernel,
        out_shape=tuple(parts),
        in_specs=[SMEM] + [VMEM] * (2 + 2 * pieces) + [ANY] * 5,
        out_specs=[ANY] * len(parts),
        scratch_shapes=[
            pltpu.VMEM((rows, heads), jnp.bfloat16),
            pltpu.VMEM((rows, units), jnp.bfloat16),
            pltpu.VMEM((tiles, heads, OUT_TILE), jnp.bfloat16),
            pltpu.VMEM((tiles, units, OUT_TILE), jnp.bfloat16),
            pltpu.VMEM((2, rows, OUT_TILE), jnp.bfloat16),
            pltpu.SemaphoreType.DMA,
            pltpu.SemaphoreType.DMA((tiles, 2)),
            pltpu.SemaphoreType.DMA((2, len(parts))),
        ],
        compiler_params=kernel_params(),
        cost_estimate=pl.CostEstimate(
            flops=4 * rows * (heads + units) * half_cols + 4 * rows * slots * heads,
            bytes_accessed=4 * (heads + units) * half_cols + 2 * rows * (heads + units + 2 * half_cols),
            transcendentals=rows * slots * heads // 128,
        ),
        name="combine",
    )(half, bias, q, *keys, *values, act, wa_own, wa_other, wm_own, wm_other)


def finish_kernel(*refs, terms, packed):
    parts, refs = refs[: 1 + terms], refs[1 + terms :]
    states, gate, shift, scale, w_final, *outs = refs
    branch = parts[0][...].astype(jnp.float32)
    for part in parts[1:]:
        branch = branch + part[...].astype(jnp.float32)
    stream = (states[...].astype(jnp.float32) + gate[...] * branch).astype(jnp.bfloat16)
    normed = (layer_norm(stream.astype(jnp.float32)) * scale[...] + shift[...]).astype(jnp.bfloat16)
    speed = lax.dot_general(
        normed, w_final[...], (((1,), (1,)), ((), ())), preferred_element_type=jnp.float32
    )
    width = stream.shape[1]
    outs[0][:, :width] = stream
    if packed:
        high = speed.astype(jnp.bfloat16)
        low = (speed - high.astype(jnp.float32)).astype(jnp.bfloat16)
        outs[0][:, width:] = jnp.concatenate([high, low], 1)
    else:
        outs[1][...] = speed


def finish(parts, states, gate, shift, scale, w_final, packed):
    rows, width = states.shape
    channels = w_final.shape[0]
    steps = 2
    by_rows = lambda cols: pl.BlockSpec((rows // steps, cols), lambda i: (i, 0))
    whole = lambda array: pl.BlockSpec(array.shape, lambda i: (0, 0))
    if packed:
        out_shape = (jax.ShapeDtypeStruct((rows, width + 2 * channels), jnp.bfloat16),)
    else:
        out_shape = (
            jax.ShapeDtypeStruct((rows, width), jnp.bfloat16),
            jax.ShapeDtypeStruct((rows, channels), jnp.float32),
        )
    return pl.pallas_call(
        functools.partial(finish_kernel, terms=len(parts) - 1, packed=packed),
        out_shape=out_shape,
        grid=(steps,),
        in_specs=[by_rows(width)] * (len(parts) + 1) + [whole(a) for a in (gate, shift, scale, w_final)],
        out_specs=[by_rows(out.shape[1]) for out in out_shape],
        compiler_params=kernel_params(),
        cost_estimate=pl.CostEstimate(
            flops=2 * states.size * channels,
            bytes_accessed=2 * states.size * (len(parts) + 2),
            transcendentals=0,
        ),
        name="finish",
    )(*parts, states, gate, shift, scale, w_final)


def add(left, right):
    return (left.astype(jnp.float32) + right.astype(jnp.float32)).astype(jnp.bfloat16)


def after(values, *done):
    return lax.optimization_barrier((values, *done))[0]


def by_prompt(
    hidden,
    latents,
    vec,
    slot_token,
    text_len,
    step_index,
    guidance,
    w_mod,
    w_qkv,
    w_mlp_in,
    qk_gain,
    w_attn_out,
    w_mlp_out,
    w_final,
):
    rows_dev, prompts, model_width = hidden.shape[1:]
    head_size = qk_gain.shape[-1]
    tok_index = lax.axis_index("tok")
    mlp_index = lax.axis_index("mlp")
    half_index = lax.axis_index("cfg")
    half = half_index[None].astype(jnp.int32)

    silu_vec = jax.nn.silu(vec[0]).astype(jnp.bfloat16)
    silu_vec = jnp.dot(xor_rows(prompts, tok_index).astype(jnp.bfloat16), silu_vec).astype(jnp.bfloat16)
    mod_part = jnp.dot(silu_vec, w_mod, preferred_element_type=jnp.float32)
    mod_near = xor_swap(mod_part[1::2], "tok", 1)

    states = jnp.transpose(after(hidden[0], mod_part), (1, 0, 2))
    sends = pick(tok_index[None].astype(jnp.int32), after(states, mod_near))

    cosine, sine_table, bias = tables(
        jnp.stack([tok_index, mlp_index]).astype(jnp.int32),
        text_len[0],
        after(slot_token, sends[0]).reshape(-1, rows_dev),
        head_size,
    )
    tables_done = bias

    wq_own = jnp.transpose(w_qkv[0], (1, 0, 2))
    wu_own, wa_own, wm_own = w_mlp_in[0], w_attn_out[0], w_mlp_out[0]
    wq_other = xor_swap(wq_own, "cfg", 1)
    wu_other = xor_swap(after(wu_own, wq_other, sends[0]), "cfg", 1)
    gain = qk_gain[0]

    states_0, states_1 = sends[0], xor_swap(sends[1], "tok", 1)
    by_x, by_y = xor_swap(states_0, "mlp", 1), xor_swap(states_0, "mlp", 2)
    order = xor_rows(4 * prompts, 4 * tok_index + mlp_index)
    mods = jnp.stack([mod_part[0::2], mod_near], 1)
    mods = jnp.concatenate([mods[0], xor_swap(after(mods[1], sends[0]), "tok", 2)], 0)
    mods = jnp.stack([mods, xor_swap(after(mods, tables_done), "mlp", 1)], 1)
    cut = rows_dev // 2
    far_top, far_low = xor_swap(by_x[:cut], "mlp", 2), xor_swap(by_y[cut:], "mlp", 1)
    mods = jnp.concatenate([mods, xor_swap(after(mods, states_1, by_x, by_y), "mlp", 2)], 1)
    mods = after(mods, far_top, far_low)
    mods = jnp.dot(
        order.astype(jnp.float32), mods.reshape(order.shape[0], -1), precision=lax.Precision.HIGHEST
    )
    shift_mod, scale_mod, gate_mod, final_shift, final_scale = jnp.split(
        mods.reshape(1, 5 * model_width), 5, 1
    )
    scale_mod = 1.0 + scale_mod
    final_scale = 1.0 + final_scale

    wm_other = xor_swap(after(wm_own, shift_mod), "cfg", 1)

    own, queries, keys, values, acts = [], [], [], [], []
    done = (far_top, far_low, shift_mod)
    for j in range(prompts):
        if j == 0:
            states, far = states_0, jnp.concatenate([far_top, far_low], 0)
        else:
            states = states_1 if j == 1 else xor_swap(after(sends[j], own[-1], *queries[: j - 2]), "tok", j)
            send = after(states, *done)
            by_x, by_y, far = [xor_swap(send, "mlp", k) for k in (1, 2, 3)]
        own.append(states)
        q, k, v, act = project(
            half,
            (states, by_x, by_y, far),
            shift_mod,
            scale_mod,
            cosine[j],
            sine_table[j],
            gain,
            wq_own,
            wq_other,
            wu_own,
            wu_other,
        )
        if j == 0:
            bias = after(tables_done, q).reshape(1, -1)
        queries.append(q)
        keys.append(k)
        values.append(v)
        acts.append(act)
        if j == 1:
            wa_other = xor_swap(after(wa_own, q, wm_other), "cfg", 1)
        if j:
            done = (queries[j - 1], by_x, by_y, far) + ((wm_other,) if j == 2 else ())

    streams, speeds, marks, parts = ([None] * prompts for _ in range(4))

    def first_step(j, *done):
        if j == 0:
            p0, p1_top, p1_low, p2_top, p2_low, top, low = parts[0]
            top, low = xor_swap(after(top, *done), "mlp", 1), xor_swap(after(low, *done), "mlp", 2)
            parts[0] = (p0, (p1_top, p1_low), (p2_top, p2_low), top, low)
            return
        p0, p1, p2, p3 = parts[j]
        p3 = after(p3, *done)
        if j % 2:
            top, low = xor_swap(p3, "mlp", 1), None
        else:
            top, low = None, xor_swap(p3, "mlp", 2)
        parts[j] = (p0, p1, p2, top, low)

    def second_step(j, *done):
        p0, p1, p2, top, low = parts[j]
        if j == 0:
            low = after(low, *done)
            p1 = jnp.concatenate([p1[0], add(p1[1], low)], 0)
            p2 = jnp.concatenate([add(p2[0], top), p2[1]], 0)
        elif j % 2:
            p2 = add(p2, after(top, *done))
            p1 = after(p1, p2)
        else:
            p1 = add(p1, after(low, *done))
            p2 = after(p2, p1)
        parts[j] = (p0, [xor_swap(p1, "mlp", 1), xor_swap(p2, "mlp", 2)])
        return p2 if j % 2 else p1

    def sum_up(j, *done):
        p0, terms = parts[j]
        outs = finish(
            [after(p0, *done), *terms],
            own[j],
            gate_mod,
            final_shift,
            final_scale,
            w_final.T,
            packed=j > 0,
        )
        marks[j] = outs[0]
        if j:
            gone = xor_swap(outs[0], "tok", j)
            streams[j] = gone[:, :model_width]
            high, low = jnp.split(gone[:, model_width:].astype(jnp.float32), 2, 1)
            speeds[j] = high + low
        else:
            streams[j], speeds[j] = outs

    done = ()
    for j in reversed(range(prompts)):
        parts[j] = combine(
            half,
            bias,
            after(queries[j], *done),
            keys,
            values,
            acts[j],
            wa_own,
            wa_other,
            wm_own,
            wm_other,
            (rows_dev,) * 4 if j else (rows_dev,) + (cut,) * 6,
        )
        done = (parts[j][0],)
        if j == 0:
            break
        sent = (second_step(j + 1, *done),) if j + 1 < prompts else ()
        if j + 2 < prompts:
            sum_up(j + 2, *done)
            done += (marks[j + 2],)
        first_step(j, *sent)
        done += sent
    first_step(0, *parts[2][1])
    sum_up(2, *done)
    sent = second_step(1, marks[2])
    second_step(0, sent)
    sum_up(1, sent)
    sum_up(0, marks[1])

    stream = from_xor_order(jnp.stack(streams, 1), 1, tok_index, 2)
    half_velocity = from_xor_order(jnp.stack(speeds, 1), 1, tok_index, 2)
    own_first = (tok_index * 4 + mlp_index) * rows_dev
    own_tokens = lax.dynamic_slice_in_dim(slot_token, own_first, rows_dev, 1).T
    half_velocity = jnp.where((own_tokens >= TXT)[:, :, None], half_velocity, 0.0)
    return guided(half_velocity, half_index, latents, step_index, guidance) + (stream[None],)


def guided(half_velocity, half_index, latents, step_index, guidance):
    channel_half = latents.shape[2]
    own_part = lax.dynamic_slice_in_dim(half_velocity, half_index * channel_half, channel_half, 2)
    sent_part = lax.dynamic_slice_in_dim(
        half_velocity, (1 - half_index) * channel_half, channel_half, 2
    )
    partner = xor_swap(sent_part, "cfg", 1)
    first_half = half_index == 0
    cond_part = jnp.where(first_half, own_part, partner)
    uncond_part = jnp.where(first_half, partner, own_part)
    velocity = uncond_part + guidance[0] * (cond_part - uncond_part)
    current = step_index[0].astype(jnp.float32)
    step_size = sigma_at(current + 1.0, STEPS) - sigma_at(current, STEPS)
    return (velocity, latents + step_size * velocity)


def fits_by_prompt(mesh):
    return mesh.shape["cfg"] == 2 and mesh.shape["tok"] == PROMPTS and mesh.shape["mlp"] == 4


def solution(mesh):
    return jax.shard_map(
        by_prompt if fits_by_prompt(mesh) else on_device,
        mesh=mesh,
        in_specs=(
            P("cfg", ("tok", "mlp"), None, None),
            P(("tok", "mlp"), None, "cfg"),
            P("cfg", None, None),
            P(),
            P("cfg", None),
            P(),
            P(),
            P(None, ("tok", "mlp")),
            P(None, "cfg", None, "mlp"),
            P(None, "cfg", "mlp"),
            P(),
            P(None, "mlp", "cfg"),
            P(None, "mlp", "cfg"),
            P(),
        ),
        out_specs=(
            P(("tok", "mlp"), None, "cfg"),
            P(("tok", "mlp"), None, "cfg"),
            P("cfg", ("tok", "mlp"), None, None),
        ),
        check_vma=False,
    )
```

```python
import functools
import math

import jax
import jax.numpy as jnp
import numpy as np
from jax import lax
from jax.experimental import pallas as pl
from jax.experimental.pallas import tpu as pltpu
from jax.sharding import PartitionSpec as P

LAYERS = 1
SIDE = 32
TXT = 512
STEPS = 28
PROMPTS = 4


EPSILON = 1e-06
ROPE_BASE = 10000.0
TIME_SHIFT = 3.0


def xor_swap(value, axis, apart):
    return lax.ppermute(value, axis, [(i, i ^ apart) for i in range(lax.axis_size(axis))])


def layer_norm(values):
    average = jnp.mean(values, axis=-1, keepdims=True)
    centred = values - average
    spread = jnp.mean(centred * centred, axis=-1, keepdims=True)
    return centred * lax.rsqrt(spread + EPSILON)


def rms_norm(values, gains):
    return values * lax.rsqrt(jnp.mean(values * values, axis=-1, keepdims=True) + EPSILON) * gains


def rope_table(tokens, head_size, text_count, side_count):
    pair_count = head_size // 2
    first_pairs = head_size // 16
    axis_pairs = (head_size - head_size // 8) // 4
    pair_index = jnp.arange(pair_count).astype(jnp.float32)
    in_rows = (pair_index >= first_pairs) & (pair_index < first_pairs + axis_pairs)
    in_cols = pair_index >= first_pairs + axis_pairs
    log_base = math.log(ROPE_BASE)
    freq_rows = jnp.where(
        in_rows, jnp.exp(-log_base * (pair_index - first_pairs) / axis_pairs), 0.0
    )
    freq_cols = jnp.where(
        in_cols, jnp.exp(-log_base * (pair_index - first_pairs - axis_pairs) / axis_pairs), 0.0
    )
    is_image = tokens >= text_count
    image_pos = jnp.where(is_image, tokens - text_count, 0)
    row_pos = (image_pos // side_count).astype(jnp.float32)
    col_pos = (image_pos % side_count).astype(jnp.float32)
    angles = row_pos[..., None] * freq_rows + col_pos[..., None] * freq_cols
    return (jnp.cos(angles), jnp.sin(angles))


def apply_rope(values, cosine, sine_table):
    even_part = values[..., 0::2]
    odd_part = values[..., 1::2]
    return jnp.concatenate(
        [even_part * cosine - odd_part * sine_table, even_part * sine_table + odd_part * cosine],
        axis=-1,
    )


def sigma_at(position, steps_total):
    remain = 1.0 - position / steps_total
    return TIME_SHIFT * remain / (1.0 + (TIME_SHIFT - 1.0) * remain)


def on_device(
    hidden,
    latents,
    vec,
    slot_token,
    text_len,
    step_index,
    guidance,
    w_mod,
    w_qkv,
    w_mlp_in,
    qk_gain,
    w_attn_out,
    w_mlp_out,
    w_final,
):
    rows_dev = hidden.shape[1]
    prompts = hidden.shape[2]
    model_width = hidden.shape[3]
    head_size = qk_gain.shape[-1]
    mlp_count = lax.axis_size("mlp")
    tile_rows = rows_dev * mlp_count
    tok_index = lax.axis_index("tok")
    mlp_index = lax.axis_index("mlp")
    half_index = lax.axis_index("cfg")
    stream = hidden[0]
    silu_vec = jax.nn.silu(vec[0]).astype(jnp.bfloat16)
    mod_part = jnp.dot(silu_vec, w_mod, preferred_element_type=jnp.float32)
    modulation = lax.all_gather(mod_part, ("tok", "mlp"), axis=1, tiled=True)
    key_valid = ((slot_token >= TXT) | (slot_token < text_len[0][:, None])).astype(jnp.float32)
    tile_tokens = lax.dynamic_slice_in_dim(slot_token, tok_index * tile_rows, tile_rows, 1).T
    cosine, sine_table = rope_table(tile_tokens, head_size, TXT, SIDE)
    shift_mod = modulation[:, 0:model_width]
    scale_mod = modulation[:, model_width : 2 * model_width]
    gate_mod = modulation[:, 2 * model_width : 3 * model_width]
    normed = (
        layer_norm(stream.astype(jnp.float32)) * (1.0 + scale_mod[None]) + shift_mod[None]
    ).astype(jnp.bfloat16)
    tile_input = lax.all_gather(normed, "mlp", axis=0, tiled=True)
    qkv_weight = w_qkv[0]
    unit_weight = w_mlp_in[0]
    qkv_cols = qkv_weight.shape[1] * qkv_weight.shape[2]
    pieces = (
        lax.all_gather(qkv_weight, "cfg", axis=0, tiled=True),
        lax.all_gather(unit_weight, "cfg", axis=0, tiled=True),
    )
    number = pieces[0].shape[0]
    qkv_piece = pieces[0].reshape(number, qkv_cols)
    qkv_pre = jnp.einsum("tpd,dk->tpk", tile_input, qkv_piece, preferred_element_type=jnp.float32)
    unit_pre = jnp.einsum("tpd,dk->tpk", tile_input, pieces[1], preferred_element_type=jnp.float32)
    heads_dev = qkv_weight.shape[2] // head_size
    projected = qkv_pre.reshape(tile_rows, prompts, 3, heads_dev, head_size)
    queries = apply_rope(
        rms_norm(projected[:, :, 0], qk_gain[0, 0]), cosine[:, :, None], sine_table[:, :, None]
    ).astype(jnp.bfloat16)
    keys_rot = apply_rope(
        rms_norm(projected[:, :, 1], qk_gain[0, 1]), cosine[:, :, None], sine_table[:, :, None]
    ).astype(jnp.bfloat16)
    values = projected[:, :, 2].astype(jnp.bfloat16)
    activation = jax.nn.gelu(unit_pre, approximate=True).astype(jnp.bfloat16)
    keys_piece = lax.all_gather(keys_rot, "tok", axis=0, tiled=True)
    values_piece = lax.all_gather(values, "tok", axis=0, tiled=True)
    scores = jnp.einsum(
        "sphe,tphe->phst", queries, keys_piece, preferred_element_type=jnp.float32
    ) / math.sqrt(head_size)
    softened = jnp.exp(scores) * key_valid[:, None, None, :]
    numerator = jnp.einsum(
        "phst,tphe->sphe",
        softened.astype(jnp.bfloat16),
        values_piece,
        preferred_element_type=jnp.float32,
    )
    numerator, denominator = (numerator, jnp.sum(softened, axis=-1))
    attended = (numerator / jnp.transpose(denominator, (2, 0, 1))[..., None]).astype(jnp.bfloat16)
    attended = attended.reshape(tile_rows, prompts, heads_dev * head_size)
    out_attn = lax.all_gather(w_attn_out[0], "cfg", axis=1, tiled=True)
    out_units = lax.all_gather(w_mlp_out[0], "cfg", axis=1, tiled=True)
    branch_out = lax.psum_scatter(
        (
            jnp.einsum("tpk,kd->tpd", attended, out_attn, preferred_element_type=jnp.float32)
            + jnp.einsum("tpk,kd->tpd", activation, out_units, preferred_element_type=jnp.float32)
        ).astype(jnp.bfloat16),
        "mlp",
        scatter_dimension=0,
        tiled=True,
    ).astype(jnp.float32)
    stream = (stream.astype(jnp.float32) + gate_mod[None] * branch_out).astype(jnp.bfloat16)
    final_lo = 3 * LAYERS * model_width
    final_shift = modulation[:, final_lo : final_lo + model_width]
    final_scale = modulation[:, final_lo + model_width : final_lo + 2 * model_width]
    final_normed = (
        layer_norm(stream.astype(jnp.float32)) * (1.0 + final_scale[None]) + final_shift[None]
    ).astype(jnp.bfloat16)
    own_first = (tok_index * mlp_count + mlp_index) * rows_dev
    own_tokens = lax.dynamic_slice_in_dim(slot_token, own_first, rows_dev, 1).T
    half_velocity = jnp.einsum(
        "rpd,dc->rpc", final_normed, w_final, preferred_element_type=jnp.float32
    )
    half_velocity = jnp.where((own_tokens >= TXT)[:, :, None], half_velocity, 0.0)
    return guided(half_velocity, half_index, latents, step_index, guidance) + (stream[None],)


VMEM_BYTES = 63 * 1024 * 1024
TILE = 512
UNIT_TILE = 1024
OUT_TILE = 768
ANY = pl.BlockSpec(memory_space=pl.ANY)
VMEM = pl.BlockSpec(memory_space=pltpu.VMEM)
SMEM = pl.BlockSpec(memory_space=pltpu.SMEM)


def kernel_params():
    return pltpu.CompilerParams(vmem_limit_bytes=VMEM_BYTES)


def flip_by_bit(values, axis, bit):
    return jnp.where(bit, jnp.flip(values, axis), values)


def from_xor_order(values, axis, index, bits):
    shape = values.shape
    split = shape[:axis] + (2,) * bits + shape[axis + 1 :]
    values = values.reshape(split)
    for place in range(bits):
        bit = (index >> (bits - 1 - place)) & 1
        values = flip_by_bit(values, axis + place, bit == 1)
    return values.reshape(shape)


def xor_rows(count, index):
    places = jnp.arange(count)
    return (places[:, None] ^ index) == places[None, :]


def pick_kernel(place_ref, *refs):
    count = len(refs) // 2
    for j in range(count):
        refs[count + j][...] = refs[j][0]


def pick(place, states):
    count, rows, width = states.shape
    take = lambda j: lambda i, s: (s[0] ^ j, i, 0)
    return pl.pallas_call(
        pick_kernel,
        out_shape=(jax.ShapeDtypeStruct((rows, width), states.dtype),) * count,
        grid_spec=pltpu.PrefetchScalarGridSpec(
            num_scalar_prefetch=1,
            grid=(2,),
            in_specs=[pl.BlockSpec((1, rows // 2, width), take(j)) for j in range(count)],
            out_specs=[pl.BlockSpec((rows // 2, width), lambda i, s: (i, 0))] * count,
        ),
        compiler_params=kernel_params(),
        cost_estimate=pl.CostEstimate(flops=0, bytes_accessed=4 * states.size, transcendentals=0),
        name="pick",
    )(place, *([states] * count))


def tables_kernel(place_ref, len_ref, tokens, freqs, bias, *outs):
    tok, mlp = place_ref[0], place_ref[1]
    own_len = len_ref[tok].astype(jnp.float32)
    blocks, rows = bias.shape
    wide = tokens.shape[1]
    odd = (lax.broadcasted_iota(jnp.int32, (rows, wide), 1) & 1) == 1

    def block(cosine, sine, chunk, index):
        source = tok * blocks + (tok ^ chunk) * 4 + (mlp ^ index)
        token = tokens[pl.ds(source, 1), :].astype(jnp.float32)
        seen = (token >= TXT) | (token < own_len)
        bias[pl.ds(chunk * 4 + index, 1), :] = jnp.where(seen, 0.0, -1e30)[:, :rows]
        place = jnp.where(token >= TXT, token - TXT, 0.0)
        row = jnp.floor(place * (1.0 / SIDE))
        down = lambda values: jnp.transpose(jnp.broadcast_to(values, (wide, wide)))[:rows]
        angles = down(row) * freqs[0:1, :] + down(place - row * SIDE) * freqs[1:2, :]
        to = pl.ds(pl.multiple_of(index * rows, 16), rows)
        cosine[to, :] = jnp.cos(angles)
        turned = jnp.sin(angles)
        sine[to, :] = jnp.where(odd, turned, -turned)

    count = len(outs) // 2
    for chunk in range(count):
        pl.loop(0, 4)(functools.partial(block, outs[chunk], outs[count + chunk], chunk))


def tables(place, text_len, tokens, head):
    chunks = text_len.shape[0]
    blocks, rows = tokens.shape[0] // chunks, tokens.shape[1]
    first, count = head // 16, (head - head // 8) // 4
    pair = np.arange(head) // 2
    rates = [
        np.where(
            (pair >= lo) & (pair < lo + count), np.exp(-math.log(ROPE_BASE) * (pair - lo) / count), 0.0
        )
        for lo in (first, first + count)
    ]
    freqs = jnp.asarray(np.stack(rates).astype(np.float32))
    table = jax.ShapeDtypeStruct((4 * rows, head), jnp.float32)
    bias, *outs = pl.pallas_call(
        tables_kernel,
        out_shape=(jax.ShapeDtypeStruct((blocks, rows), jnp.float32),) + (table,) * (2 * chunks),
        in_specs=[SMEM, SMEM, VMEM, VMEM],
        compiler_params=kernel_params(),
        cost_estimate=pl.CostEstimate(
            flops=100 * blocks * rows * head,
            bytes_accessed=8 * blocks * rows * head,
            transcendentals=2 * blocks * rows * head,
        ),
        name="tables",
    )(place, text_len, jnp.pad(tokens, ((0, 0), (0, head - rows))), freqs)
    return outs[:chunks], outs[chunks:], bias


def project_kernel(
    half_ref,
    shift,
    scale,
    cos_ref,
    sin_ref,
    gain,
    x0,
    x1,
    x2,
    x3,
    wq_own,
    wq_other,
    wu_own,
    wu_other,
    q_out,
    k_out,
    v_out,
    act_out,
    landed,
    normed,
    held,
    held_units,
    ready,
    ready_units,
    x_sem,
    w_sem,
    unit_sem,
    out_sem,
    act_sem,
):
    half = half_ref[0]
    depth = wu_own.shape[0]
    head = gain.shape[1]
    pieces = (x0, x1, x2, x3)
    rows = x0.shape[0]
    units = wu_own.shape[1] // UNIT_TILE

    def unit_weights(index):
        return [
            pltpu.make_async_copy(
                ref.at[:, pl.ds(pl.multiple_of(index * UNIT_TILE, UNIT_TILE), UNIT_TILE)],
                held_units.at[index, side],
                unit_sem.at[index, side],
            )
            for side, ref in enumerate((wu_own, wu_other))
        ]

    def head_weights(part):
        return [
            pltpu.make_async_copy(ref.at[part], held.at[part, side], w_sem.at[part, side])
            for side, ref in enumerate((wq_own, wq_other))
        ]

    def head_result(part):
        out = (q_out, k_out, v_out)[part]
        return pltpu.make_async_copy(ready.at[part], out, out_sem.at[part])

    def unit_result(index, slot):
        column = pl.multiple_of(index * UNIT_TILE, UNIT_TILE)
        return pltpu.make_async_copy(
            ready_units.at[slot], act_out.at[:, pl.ds(column, UNIT_TILE)], act_sem.at[slot]
        )

    loads = [pltpu.make_async_copy(ref, landed.at[i], x_sem.at[i]) for i, ref in enumerate(pieces)]
    loads[0].start()
    for copy in head_weights(0):
        copy.start()
    for load in loads[1:]:
        load.start()
    for part in (1, 2):
        for copy in head_weights(part):
            copy.start()

    for index, load in enumerate(loads):
        load.wait()
        block = layer_norm(landed[index].astype(jnp.float32))
        block = (block * scale[...] + shift[...]).astype(jnp.bfloat16)
        normed[0, index * rows : (index + 1) * rows, :] = block[:, :depth]
        normed[1, index * rows : (index + 1) * rows, :] = block[:, depth:]

    even = (lax.broadcasted_iota(jnp.int32, cos_ref.shape, 1) & 1) == 0

    def product(own, other):
        return jnp.dot(normed[half], own, preferred_element_type=jnp.float32) + jnp.dot(
            normed[1 - half], other, preferred_element_type=jnp.float32
        )

    for part in range(3):
        for copy in head_weights(part):
            copy.wait()
        if part < units:
            for copy in unit_weights(part):
                copy.start()
        values = product(held[part, 0], held[part, 1])
        if part == 2:
            ready[part] = values.astype(jnp.bfloat16)
        else:
            for lo in range(0, TILE, head):
                turned = rms_norm(values[:, lo : lo + head], gain[part : part + 1, :])
                partner = jnp.where(even, pltpu.roll(turned, head - 1, 1), pltpu.roll(turned, 1, 1))
                turned = turned * cos_ref[...] + partner * sin_ref[...]
                ready[part, :, lo : lo + head] = turned.astype(jnp.bfloat16)
        head_result(part).start()

    @pl.loop(0, units)
    def _(index):
        slot = lax.rem(index, 2)
        for copy in unit_weights(index):
            copy.wait()
        values = product(held_units[index, 0], held_units[index, 1])
        values = jax.nn.gelu(values, approximate=True).astype(jnp.bfloat16)

        @pl.when(index >= 2)
        def _():
            unit_result(index, slot).wait()

        ready_units[slot] = values
        unit_result(index, slot).start()

    for part in range(3):
        head_result(part).wait()
    for slot in range(2):
        unit_result(0, slot).wait()


def project(half, pieces, shift, scale, cos_rows, sin_rows, gain, wq_own, wq_other, wu_own, wu_other):
    rows = sum(piece.shape[0] for piece in pieces)
    width = pieces[0].shape[1]
    depth = wu_own.shape[0]
    units = wu_own.shape[1]
    unit_steps = units // UNIT_TILE
    assert unit_steps == 3
    head_out = jax.ShapeDtypeStruct((rows, TILE), jnp.bfloat16)
    return pl.pallas_call(
        project_kernel,
        out_shape=(head_out, head_out, head_out, jax.ShapeDtypeStruct((rows, units), jnp.bfloat16)),
        in_specs=[SMEM] + [VMEM] * 5 + [ANY] * 8,
        out_specs=[ANY] * 4,
        scratch_shapes=[
            pltpu.VMEM((len(pieces), rows // len(pieces), width), jnp.bfloat16),
            pltpu.VMEM((2, rows, depth), jnp.bfloat16),
            pltpu.VMEM((3, 2, depth, TILE), jnp.bfloat16),
            pltpu.VMEM((unit_steps, 2, depth, UNIT_TILE), jnp.bfloat16),
            pltpu.VMEM((3, rows, TILE), jnp.bfloat16),
            pltpu.VMEM((2, rows, UNIT_TILE), jnp.bfloat16),
            pltpu.SemaphoreType.DMA((len(pieces),)),
            pltpu.SemaphoreType.DMA((3, 2)),
            pltpu.SemaphoreType.DMA((unit_steps, 2)),
            pltpu.SemaphoreType.DMA((3,)),
            pltpu.SemaphoreType.DMA((2,)),
        ],
        compiler_params=kernel_params(),
        cost_estimate=pl.CostEstimate(
            flops=2 * rows * width * (3 * TILE + units),
            bytes_accessed=2 * width * (3 * TILE + units) + 2 * rows * (width + 3 * TILE + units),
            transcendentals=rows * units,
        ),
        name="project",
    )(half, shift, scale, cos_rows, sin_rows, gain, *pieces, wq_own, wq_other, wu_own, wu_other)


def combine_kernel(
    half_ref,
    bias,
    q,
    k0,
    k1,
    k2,
    k3,
    v0,
    v1,
    v2,
    v3,
    act,
    wa_own,
    wa_other,
    wm_own,
    wm_other,
    *refs,
):
    outs = refs[:-8]
    attended, units, held_a, held_m, ready, act_sem, w_sem, out_sem = refs[-8:]
    half = half_ref[0]
    keys, values = (k0, k1, k2, k3), (v0, v1, v2, v3)
    rows = q.shape[0]
    size = k0.shape[0]
    head = 128
    steps = wa_own.shape[1] // OUT_TILE

    def weights(tile):
        wa, wm = (wa_own, wm_own) if tile < steps else (wa_other, wm_other)
        columns = pl.ds(tile % steps * OUT_TILE, OUT_TILE)
        return [
            pltpu.make_async_copy(wa.at[:, columns], held_a.at[tile], w_sem.at[tile, 0]),
            pltpu.make_async_copy(wm.at[:, columns], held_m.at[tile], w_sem.at[tile, 1]),
        ]

    def landed(index):
        columns = pl.ds(0, OUT_TILE)
        return [
            pltpu.make_async_copy(wa_own.at[:, columns], held_a.at[index], w_sem.at[index, 0]),
            pltpu.make_async_copy(wm_own.at[:, columns], held_m.at[index], w_sem.at[index, 1]),
        ]

    def results(column, slot):
        copies, first = [], 0
        for i, out in enumerate(outs):
            copies.append(
                pltpu.make_async_copy(
                    ready.at[slot, pl.ds(first, out.shape[0])],
                    out.at[:, pl.ds(column, OUT_TILE)],
                    out_sem.at[slot, i],
                )
            )
            first += out.shape[0]
        return copies

    load = pltpu.make_async_copy(act, units, act_sem)
    load.start()
    for tile in range(steps):
        for copy in weights(tile):
            copy.start()

    @pl.loop(0, q.shape[1] // head)
    def _(index):
        lanes = pl.ds(pl.multiple_of(index * head, head), head)
        total = jnp.zeros((rows, 1), jnp.float32)
        numerator = jnp.zeros((rows, head), jnp.float32)
        for part in range(len(keys)):
            scores = lax.dot_general(
                q[:, lanes],
                keys[part][:, lanes],
                (((1,), (1,)), ((), ())),
                preferred_element_type=jnp.float32,
            )
            soft = jnp.exp(
                scores * (1.0 / math.sqrt(head)) + bias[:, part * size : (part + 1) * size]
            )
            total += jnp.sum(soft, axis=-1, keepdims=True)
            numerator += jnp.dot(
                soft.astype(jnp.bfloat16), values[part][:, lanes], preferred_element_type=jnp.float32
            )
        attended[:, lanes] = (numerator / total).astype(jnp.bfloat16)

    for tile in range(steps, 2 * steps):
        for copy in weights(tile):
            copy.start()
    load.wait()

    @pl.loop(0, 2 * steps)
    def _(index):
        to = lax.rem(index, 2)
        place = lax.rem(index + steps * half, 2 * steps)
        for copy in landed(index):
            copy.wait()
        partial = jnp.dot(attended[...], held_a[index], preferred_element_type=jnp.float32)
        partial += jnp.dot(units[...], held_m[index], preferred_element_type=jnp.float32)

        @pl.when(index >= 2)
        def _():
            for copy in results(0, to):
                copy.wait()

        ready[to] = partial.astype(jnp.bfloat16)
        for copy in results(pl.multiple_of(place * OUT_TILE, OUT_TILE), to):
            copy.start()

    for slot in range(2):
        for copy in results(0, slot):
            copy.wait()


def combine(half, bias, q, keys, values, act, wa_own, wa_other, wm_own, wm_other, out_rows):
    rows, heads = q.shape
    units = act.shape[1]
    slots = bias.shape[1]
    half_cols = wa_own.shape[1]
    tiles = 2 * (half_cols // OUT_TILE)
    pieces = len(keys)
    parts = [jax.ShapeDtypeStruct((n, 2 * half_cols), jnp.bfloat16) for n in out_rows]
    return pl.pallas_call(
        combine_kernel,
        out_shape=tuple(parts),
        in_specs=[SMEM] + [VMEM] * (2 + 2 * pieces) + [ANY] * 5,
        out_specs=[ANY] * len(parts),
        scratch_shapes=[
            pltpu.VMEM((rows, heads), jnp.bfloat16),
            pltpu.VMEM((rows, units), jnp.bfloat16),
            pltpu.VMEM((tiles, heads, OUT_TILE), jnp.bfloat16),
            pltpu.VMEM((tiles, units, OUT_TILE), jnp.bfloat16),
            pltpu.VMEM((2, rows, OUT_TILE), jnp.bfloat16),
            pltpu.SemaphoreType.DMA,
            pltpu.SemaphoreType.DMA((tiles, 2)),
            pltpu.SemaphoreType.DMA((2, len(parts))),
        ],
        compiler_params=kernel_params(),
        cost_estimate=pl.CostEstimate(
            flops=4 * rows * (heads + units) * half_cols + 4 * rows * slots * heads,
            bytes_accessed=4 * (heads + units) * half_cols + 2 * rows * (heads + units + 2 * half_cols),
            transcendentals=rows * slots * heads // 128,
        ),
        name="combine",
    )(half, bias, q, *keys, *values, act, wa_own, wa_other, wm_own, wm_other)


def finish_kernel(*refs, terms):
    parts, refs = refs[:terms], refs[terms:]
    if terms == 1:
        shift, scale, w_final, speed = refs
        stream = parts[0][...]
    else:
        states, gate, shift, scale, w_final, stream_out, speed = refs
        branch = parts[0][...].astype(jnp.float32)
        for part in parts[1:]:
            branch = branch + part[...].astype(jnp.float32)
        stream = (states[...].astype(jnp.float32) + gate[...] * branch).astype(jnp.bfloat16)
        stream_out[...] = stream
    normed = (layer_norm(stream.astype(jnp.float32)) * scale[...] + shift[...]).astype(jnp.bfloat16)
    speed[...] = lax.dot_general(
        normed, w_final[...], (((1,), (1,)), ((), ())), preferred_element_type=jnp.float32
    )


def finish(parts, shift, scale, w_final, states=None, gate=None):
    rows, width = parts[0].shape
    channels = w_final.shape[0]
    steps = 2
    by_rows = lambda cols: pl.BlockSpec((rows // steps, cols), lambda i: (i, 0))
    whole = lambda array: pl.BlockSpec(array.shape, lambda i: (0, 0))
    out_shape = [jax.ShapeDtypeStruct((rows, channels), jnp.float32)]
    blocks, vectors = list(parts), [shift, scale, w_final]
    if states is not None:
        out_shape.insert(0, jax.ShapeDtypeStruct((rows, width), jnp.bfloat16))
        blocks.append(states)
        vectors.insert(0, gate)
    return pl.pallas_call(
        functools.partial(finish_kernel, terms=len(parts)),
        out_shape=tuple(out_shape),
        grid=(steps,),
        in_specs=[by_rows(width)] * len(blocks) + [whole(a) for a in vectors],
        out_specs=[by_rows(out.shape[1]) for out in out_shape],
        compiler_params=kernel_params(),
        cost_estimate=pl.CostEstimate(
            flops=2 * rows * width * channels,
            bytes_accessed=2 * rows * width * (len(blocks) + 1),
            transcendentals=0,
        ),
        name="finish",
    )(*blocks, *vectors)


def add(left, right):
    return (left.astype(jnp.float32) + right.astype(jnp.float32)).astype(jnp.bfloat16)


def after(values, *done):
    return lax.optimization_barrier((values, *done))[0]


def by_prompt(
    hidden,
    latents,
    vec,
    slot_token,
    text_len,
    step_index,
    guidance,
    w_mod,
    w_qkv,
    w_mlp_in,
    qk_gain,
    w_attn_out,
    w_mlp_out,
    w_final,
):
    rows_dev, prompts, model_width = hidden.shape[1:]
    head_size = qk_gain.shape[-1]
    tok_index = lax.axis_index("tok")
    mlp_index = lax.axis_index("mlp")
    half_index = lax.axis_index("cfg")
    half = half_index[None].astype(jnp.int32)

    silu_vec = jax.nn.silu(vec[0]).astype(jnp.bfloat16)
    silu_vec = jnp.dot(xor_rows(prompts, tok_index).astype(jnp.bfloat16), silu_vec).astype(jnp.bfloat16)
    mod_part = jnp.dot(silu_vec, w_mod, preferred_element_type=jnp.float32)
    mod_near = xor_swap(mod_part[1::2], "tok", 1)

    states = jnp.transpose(after(hidden[0], mod_part), (1, 0, 2))
    sends = pick(tok_index[None].astype(jnp.int32), after(states, mod_near))

    cosine, sine_table, bias = tables(
        jnp.stack([tok_index, mlp_index]).astype(jnp.int32),
        text_len[0],
        after(slot_token, sends[0]).reshape(-1, rows_dev),
        head_size,
    )
    tables_done = bias

    wq_own = jnp.transpose(w_qkv[0], (1, 0, 2))
    wu_own, wa_own, wm_own = w_mlp_in[0], w_attn_out[0], w_mlp_out[0]
    wq_other = xor_swap(wq_own, "cfg", 1)
    wu_other = xor_swap(after(wu_own, wq_other, sends[0]), "cfg", 1)
    gain = qk_gain[0]

    states_0, states_1 = sends[0], xor_swap(sends[1], "tok", 1)
    by_x, by_y = xor_swap(states_0, "mlp", 1), xor_swap(states_0, "mlp", 2)
    order = xor_rows(4 * prompts, 4 * tok_index + mlp_index)
    mods = jnp.stack([mod_part[0::2], mod_near], 1)
    mods = jnp.concatenate([mods[0], xor_swap(after(mods[1], sends[0]), "tok", 2)], 0)
    mods = jnp.stack([mods, xor_swap(after(mods, tables_done), "mlp", 1)], 1)
    cut = rows_dev // 2
    far_top, far_low = xor_swap(by_x[:cut], "mlp", 2), xor_swap(by_y[cut:], "mlp", 1)
    mods = jnp.concatenate([mods, xor_swap(after(mods, states_1, by_x, by_y), "mlp", 2)], 1)
    mods = after(mods, far_top, far_low)
    mods = jnp.dot(
        order.astype(jnp.float32), mods.reshape(order.shape[0], -1), precision=lax.Precision.HIGHEST
    )
    shift_mod, scale_mod, gate_mod, final_shift, final_scale = jnp.split(
        mods.reshape(1, 5 * model_width), 5, 1
    )
    scale_mod = 1.0 + scale_mod
    final_scale = 1.0 + final_scale

    wm_other = xor_swap(after(wm_own, shift_mod), "cfg", 1)

    own, queries, keys, values, acts = [], [], [], [], []
    done = (far_top, far_low)
    for j in range(prompts):
        if j == 0:
            states, far = states_0, jnp.concatenate([far_top, far_low], 0)
        else:
            states = states_1 if j == 1 else xor_swap(after(sends[j], own[-1], *queries[: j - 2]), "tok", j)
            send = after(states, *done)
            by_x, by_y, far = [xor_swap(send, "mlp", k) for k in (1, 2, 3)]
        own.append(states)
        q, k, v, act = project(
            half,
            (states, by_x, by_y, far),
            shift_mod,
            scale_mod,
            cosine[j],
            sine_table[j],
            gain,
            wq_own,
            wq_other,
            wu_own,
            wu_other,
        )
        if j == 0:
            bias = after(tables_done, q).reshape(1, -1)
        queries.append(q)
        keys.append(k)
        values.append(v)
        acts.append(act)
        if j == 1:
            wa_other = xor_swap(after(wa_own, q, wm_other), "cfg", 1)
        if j:
            done = (queries[j - 1], by_x, by_y, far) + ((wm_other,) if j == 2 else ())

    streams, speeds, marks, parts = ([None] * prompts for _ in range(4))

    def first_step(j, *done):
        if j == 0:
            p0, p1_top, p1_low, p2_top, p2_low, top, low = parts[0]
            top, low = xor_swap(after(top, *done), "mlp", 1), xor_swap(after(low, *done), "mlp", 2)
            parts[0] = (p0, (p1_top, p1_low), (p2_top, p2_low), top, low)
            return
        p0, p1, p2, p3 = parts[j]
        p3 = after(p3, *done)
        if j % 2:
            top, low = xor_swap(p3, "mlp", 1), None
        else:
            top, low = None, xor_swap(p3, "mlp", 2)
        parts[j] = (p0, p1, p2, top, low)

    def second_step(j, *done):
        p0, p1, p2, top, low = parts[j]
        if j == 0:
            low = after(low, *done)
            p1 = jnp.concatenate([p1[0], add(p1[1], low)], 0)
            p2 = jnp.concatenate([add(p2[0], top), p2[1]], 0)
        elif j % 2:
            p2 = add(p2, after(top, *done))
            p1 = after(p1, p2)
        else:
            p1 = add(p1, after(low, *done))
            p2 = after(p2, p1)
        parts[j] = (p0, [xor_swap(p1, "mlp", 1), xor_swap(p2, "mlp", 2)])
        return p2 if j % 2 else p1

    def sum_up(j, *done):
        p0, terms = parts[j]
        branch = after(p0, *done).astype(jnp.float32)
        for term in terms:
            branch = branch + term.astype(jnp.float32)
        marks[j] = (own[j].astype(jnp.float32) + gate_mod * branch).astype(jnp.bfloat16)
        streams[j] = xor_swap(marks[j], "tok", j)

    def speed_of(j, *done):
        return finish([after(marks[j], *done)], final_shift, final_scale, w_final.T)[0]

    done = ()
    for j in reversed(range(prompts)):
        parts[j] = combine(
            half,
            bias,
            after(queries[j], *done),
            keys,
            values,
            acts[j],
            wa_own,
            wa_other,
            wm_own,
            wm_other,
            (rows_dev,) * 4 if j else (rows_dev,) + (cut,) * 6,
        )
        done = (parts[j][0],)
        if j == 0:
            break
        sent = (second_step(j + 1, *done),) if j + 1 < prompts else ()
        if j + 2 < prompts:
            sum_up(j + 2, *done)
            done += (marks[j + 2],)
        first_step(j, *sent)
        done += sent
    first_step(0, *parts[2][1])
    sum_up(2, *done)
    sent = second_step(1, marks[2])
    speeds[3], speeds[2] = speed_of(3, sent, streams[3]), speed_of(2, sent)
    sent = second_step(0, speeds[3], speeds[2])
    sum_up(1, sent)
    speeds[1] = speed_of(1)
    p0, terms = parts[0]
    streams[0], speeds[0] = finish(
        [after(p0, marks[1], streams[2]), *terms], final_shift, final_scale, w_final.T, own[0], gate_mod
    )
    for j in (3, 2, 1):
        speeds[j] = xor_swap(after(speeds[j], sent), "tok", j)

    stream = from_xor_order(jnp.stack(streams, 1), 1, tok_index, 2)
    half_velocity = from_xor_order(jnp.stack([after(speeds[0], streams[1]), *speeds[1:]], 1), 1, tok_index, 2)
    own_first = (tok_index * 4 + mlp_index) * rows_dev
    own_tokens = lax.dynamic_slice_in_dim(slot_token, own_first, rows_dev, 1).T
    half_velocity = jnp.where((own_tokens >= TXT)[:, :, None], half_velocity, 0.0)
    return guided(half_velocity, half_index, latents, step_index, guidance) + (stream[None],)


def guided(half_velocity, half_index, latents, step_index, guidance):
    channel_half = latents.shape[2]
    own_part = lax.dynamic_slice_in_dim(half_velocity, half_index * channel_half, channel_half, 2)
    sent_part = lax.dynamic_slice_in_dim(
        half_velocity, (1 - half_index) * channel_half, channel_half, 2
    )
    partner = xor_swap(sent_part, "cfg", 1)
    first_half = half_index == 0
    cond_part = jnp.where(first_half, own_part, partner)
    uncond_part = jnp.where(first_half, partner, own_part)
    velocity = uncond_part + guidance[0] * (cond_part - uncond_part)
    current = step_index[0].astype(jnp.float32)
    step_size = sigma_at(current + 1.0, STEPS) - sigma_at(current, STEPS)
    return (velocity, latents + step_size * velocity)


def fits_by_prompt(mesh):
    return mesh.shape["cfg"] == 2 and mesh.shape["tok"] == PROMPTS and mesh.shape["mlp"] == 4


def solution(mesh):
    return jax.shard_map(
        by_prompt if fits_by_prompt(mesh) else on_device,
        mesh=mesh,
        in_specs=(
            P("cfg", ("tok", "mlp"), None, None),
            P(("tok", "mlp"), None, "cfg"),
            P("cfg", None, None),
            P(),
            P("cfg", None),
            P(),
            P(),
            P(None, ("tok", "mlp")),
            P(None, "cfg", None, "mlp"),
            P(None, "cfg", "mlp"),
            P(),
            P(None, "mlp", "cfg"),
            P(None, "mlp", "cfg"),
            P(),
        ),
        out_specs=(
            P(("tok", "mlp"), None, "cfg"),
            P(("tok", "mlp"), None, "cfg"),
            P("cfg", ("tok", "mlp"), None, None),
        ),
        check_vma=False,
    )
```
